32 devices in a mesh: dp: 8 (over y, x, core), tensor: 4 (over z).
Axes of the slice: x: 2, y: 2, z: 4, core: 2. Of those that a mesh axis runs over, the one named last changes fastest.
Arguments:
- inputs: float32 [4096, 768], P(('dp', 'tensor')), may hold values from -6 to 6
- cotangent: float32 [4096, 768], P(('dp', 'tensor')), may hold values from -6 to 6
- lengths: int32 [8, 4], P('dp'), may hold values from 0 to 512, as said below
- ln1_gain: float32 [2, 768], replicated, may hold values from 0.5 to 1.5
- ln1_bias: float32 [2, 768], replicated, may hold values from -1.25 to 1.25
- w_in: bfloat16 [2, 768, 3, 768], P(None, None, None, 'tensor'), may hold values from -0.21875 to 0.21875
- b_in: float32 [2, 3, 768], P(None, None, 'tensor'), may hold values from -1.25 to 1.25
- conv_weight: float32 [2, 3, 3, 768], P(None, None, None, 'tensor'), may hold values from -3.5 to 3.5
- conv_bias: float32 [2, 3, 768], P(None, None, 'tensor'), may hold values from -1.75 to 1.75
- filt_w1: float32 [2, 33, 64], replicated, may hold values from -1 to 1
- filt_b1: float32 [2, 64], replicated, may hold values from -3 to 3
- filt_w2: float32 [2, 64, 64], replicated, may hold values from -0.75 to 0.75
- filt_b2: float32 [2, 64], replicated, may hold values from -3 to 3
- filt_freq: float32 [2, 2, 64], replicated, may hold values from 0.5 to 1.5
- filt_w3: float32 [2, 64, 768], P(None, None, 'tensor'), may hold values from -0.03125 to 0.03125
- decay_rate: float32 [2, 768], P(None, 'tensor'), may hold values from 0.0005859375 to 0.03
- skip_gain: float32 [2, 768], P(None, 'tensor'), may hold values from -6 to 6
- w_out: bfloat16 [2, 768, 768], P(None, 'tensor'), may hold values from -0.21875 to 0.21875
- b_out: float32 [2, 768], replicated, may hold values from -1.25 to 1.25
- ln2_gain: float32 [2, 768], replicated, may hold values from 0.5 to 1.5
- ln2_bias: float32 [2, 768], replicated, may hold values from -1.25 to 1.25
- w_up: bfloat16 [2, 768, 3072], P(None, None, ('dp', 'tensor')), may hold values from -0.21875 to 0.21875
- b_up: bfloat16 [2, 3072], P(None, ('dp', 'tensor')), may hold values from -1.25 to 1.25
- w_down: bfloat16 [2, 3072, 768], P(None, ('dp', 'tensor')), may hold values from -0.109375 to 0.109375
- b_down: float32 [2, 768], replicated, may hold values from -1.25 to 1.25
Outputs:
- out: float32 [4096, 768], P(('dp', 'tensor'))
- grad_inputs: float32 [4096, 768], P(('dp', 'tensor'))
- grad_ln1_gain: float32 [2, 768], replicated
- grad_ln1_bias: float32 [2, 768], replicated
- grad_w_in: float32 [2, 768, 3, 768], P(None, 'dp', None, 'tensor')
- grad_b_in: float32 [2, 3, 768], P(None, None, 'tensor')
- grad_conv_weight: float32 [2, 3, 3, 768], P(None, None, None, 'tensor')
- grad_conv_bias: float32 [2, 3, 768], P(None, None, 'tensor')
- grad_filt_w1: float32 [2, 33, 64], replicated
- grad_filt_b1: float32 [2, 64], replicated
- grad_filt_w2: float32 [2, 64, 64], replicated
- grad_filt_b2: float32 [2, 64], replicated
- grad_filt_freq: float32 [2, 2, 64], replicated
- grad_filt_w3: float32 [2, 64, 768], P(None, None, 'tensor')
- grad_decay_rate: float32 [2, 768], P(None, 'tensor')
- grad_skip_gain: float32 [2, 768], P(None, 'tensor')
- grad_w_out: float32 [2, 768, 768], P(None, 'tensor', 'dp')
- grad_b_out: float32 [2, 768], replicated
- grad_ln2_gain: float32 [2, 768], replicated
- grad_ln2_bias: float32 [2, 768], replicated
- grad_w_up: float32 [2, 768, 3072], P(None, None, ('dp', 'tensor'))
- grad_b_up: float32 [2, 3072], P(None, ('dp', 'tensor'))
- grad_w_down: float32 [2, 3072, 768], P(None, ('dp', 'tensor'))
- grad_b_down: float32 [2, 768], replicated
The draws below stay inside these ranges and needn't reach their ends.
Inputs may be any that keep to these rules, and one draw needn't show every extreme that they name: `lengths`: each row sums to 512; its first entry is 448 or more, exactly that in some row, and 512 (the others zero) in another.
All inputs are finite; a program needn't handle non-finite values.
Results may differ from the reference program's by a relative error of at most 0.025.
Values may be sent and summed in bfloat16 or wider, within the bound.
A program may use at most 256 MiB of HBM per device.

```python
import math
import jax
import jax.numpy as jnp
from jax import lax

D = 768
FF = 3072
FILT = 64
EMB = 33
LAYERS = 2
TOK_DEV = 128
GT = 512
TOKENS = 4096
N_DP = 8


def draw_lengths(key, part):
    key = jax.random.fold_in(key, 11)
    keys = jax.random.split(key, 4)
    half = TOK_DEV // 2
    groups = jnp.arange(N_DP).astype(jnp.int32)
    rest = jax.random.randint(keys[0], (N_DP,), 0, half + 1).astype(jnp.int32)
    whole = jax.random.randint(keys[1], (), 0, N_DP).astype(jnp.int32)
    fullest = (whole + 1 + jax.random.randint(keys[2], (), 0, N_DP - 1).astype(jnp.int32)) % N_DP
    rest = jnp.where(groups == whole, 0, jnp.where(groups == fullest, half, rest)).astype(jnp.int32)
    cuts = jax.random.randint(keys[3], (N_DP, 2), 0, half + 1).astype(jnp.int32) % (rest[:, None] + 1)
    lower = jnp.minimum(cuts[:, 0], cuts[:, 1])
    upper = jnp.maximum(cuts[:, 0], cuts[:, 1])
    return jnp.stack([GT - rest, lower, upper - lower, rest - upper], axis=1).astype(jnp.int32)


def block_levels(stream_key, dims, shards, smallest, largest):
    factor_of, own = 1.0, jax.random.fold_in(stream_key, 6)
    for position, shards_of in shards:
        steps = jnp.exp(jax.random.uniform(jax.random.fold_in(own, position), (shards_of,), jnp.float32, smallest / len(shards), largest / len(shards)))
        factor_of = factor_of * jnp.repeat(steps, dims[position] // shards_of).reshape([-1 if axis == position else 1 for axis in range(len(dims))])
    return factor_of


def bell_draw(stream_key, extent, scale, limit, shards=(), kind=jnp.bfloat16):
    level = block_levels(stream_key, extent, shards, -0.22, 0.18) if shards else 1.0
    drawn = jax.random.normal(stream_key, extent, jnp.float32) * scale * level
    return jnp.minimum(jnp.maximum(drawn, -limit), limit).astype(kind)


def setup_inputs(seed: int = 0) -> dict:
    splits = jax.random.split(jax.random.key(seed), 26)
    inputs = bell_draw(splits[0], (TOKENS, D), 1.0, 6.0, ((0, 32),), jnp.float32)
    cotangent = bell_draw(splits[1], (TOKENS, D), 1.0, 6.0, ((0, 32),), jnp.float32)
    lengths = draw_lengths(jax.random.fold_in(splits[25], 71), 0)
    ln1_gain = jnp.clip(1.0 + 0.1 * jax.random.normal(splits[3], (LAYERS, D), jnp.float32), 0.5, 1.5)
    ln1_bias = bell_draw(splits[4], (LAYERS, D), 0.2, 1.25, (), jnp.float32)
    w_in = bell_draw(splits[5], (LAYERS, D, 3, D), D ** -0.5, 0.21875, ((3, 4),))
    b_in = bell_draw(splits[6], (LAYERS, 3, D), 0.2, 1.25, ((2, 4),), jnp.float32)
    conv_weight = bell_draw(splits[7], (LAYERS, 3, 3, D), 3 ** -0.5, 3.5, ((3, 4),), jnp.float32)
    conv_bias = bell_draw(splits[8], (LAYERS, 3, D), 0.3, 1.75, ((2, 4),), jnp.float32)
    filt_w1 = bell_draw(splits[9], (LAYERS, EMB, FILT), EMB ** -0.5, 1.0, (), jnp.float32)
    filt_b1 = bell_draw(splits[10], (LAYERS, FILT), 0.5, 3.0, (), jnp.float32)
    filt_w2 = bell_draw(splits[11], (LAYERS, FILT, FILT), FILT ** -0.5, 0.75, (), jnp.float32)
    filt_b2 = bell_draw(splits[12], (LAYERS, FILT), 0.5, 3.0, (), jnp.float32)
    filt_freq = jnp.clip(jax.random.uniform(splits[13], (LAYERS, 2, FILT), jnp.float32, 0.5, 1.5), 0.5, 1.5)
    filt_w3 = bell_draw(splits[14], (LAYERS, FILT, D), (FILT * GT) ** -0.5, 0.03125, ((2, 4),), jnp.float32)
    decay_rate = jnp.clip(jnp.exp(math.log(0.03) - 3.9357395 * jax.random.uniform(splits[15], (LAYERS, D), jnp.float32) ** block_levels(splits[15], (LAYERS, D), ((1, 4),), -0.2, 0.2)), 0.0005859375, 0.03)
    skip_gain = bell_draw(splits[16], (LAYERS, D), 1.0, 6.0, ((1, 4),), jnp.float32)
    w_out = bell_draw(splits[17], (LAYERS, D, D), D ** -0.5, 0.21875, ((1, 4),))
    b_out = bell_draw(splits[18], (LAYERS, D), 0.2, 1.25, (), jnp.float32)
    ln2_gain = jnp.clip(1.0 + 0.1 * jax.random.normal(splits[19], (LAYERS, D), jnp.float32), 0.5, 1.5)
    ln2_bias = bell_draw(splits[20], (LAYERS, D), 0.2, 1.25, (), jnp.float32)
    w_up = bell_draw(splits[21], (LAYERS, D, FF), D ** -0.5, 0.21875, ((2, 32),))
    b_up = bell_draw(splits[22], (LAYERS, FF), 0.2, 1.25, ((1, 32),))
    w_down = bell_draw(splits[23], (LAYERS, FF, D), FF ** -0.5, 0.109375, ((1, 32),))
    b_down = bell_draw(splits[24], (LAYERS, D), 0.2, 1.25, (), jnp.float32)
    return dict(inputs=inputs, cotangent=cotangent, lengths=lengths, ln1_gain=ln1_gain, ln1_bias=ln1_bias, w_in=w_in, b_in=b_in, conv_weight=conv_weight, conv_bias=conv_bias, filt_w1=filt_w1, filt_b1=filt_b1, filt_w2=filt_w2, filt_b2=filt_b2, filt_freq=filt_freq, filt_w3=filt_w3, decay_rate=decay_rate, skip_gain=skip_gain, w_out=w_out, b_out=b_out, ln2_gain=ln2_gain, ln2_bias=ln2_bias, w_up=w_up, b_up=b_up, w_down=w_down, b_down=b_down)


NORM_EPS = 1e-05
PRECISE = lax.Precision.HIGHEST

@jax.custom_vjp
def low(v):
    return lax.optimization_barrier(v.astype(jnp.bfloat16)).astype(jnp.float32)

@jax.custom_vjp
def low_back(v):
    return v

def low_keep(v):
    return (low(v), None)

def low_pass(kept, grad):
    return (grad,)

def back_keep(v):
    return (v, None)

def back_low(kept, grad):
    return (low(grad),)
low.defvjp(low_keep, low_pass)
low_back.defvjp(back_keep, back_low)

def layer_norm(values, norm_gain, norm_shift):
    center = values - lax.optimization_barrier(jnp.mean(values, axis=-1, keepdims=True))
    spread = lax.optimization_barrier(jnp.mean(center * center, axis=-1, keepdims=True))
    return center * lax.rsqrt(spread + NORM_EPS) * norm_gain + norm_shift

def filter_taps(w_first, b_first, w_second, b_second, freq_pair, w_third, decay_row, length):
    lag_pos = jnp.arange(length).astype(jnp.float32)
    fraction = lag_pos / length
    band_ids = jnp.arange(1, w_first.shape[0] // 2 + 1).astype(jnp.float32)
    phases = 2.0 * math.pi * fraction[:, None] * band_ids[None, :]
    embedding = jnp.concatenate([fraction[:, None], jnp.cos(phases), jnp.sin(phases)], axis=1)
    layer_one = jnp.sin(freq_pair[0] * (jnp.dot(embedding, w_first, precision=PRECISE) + b_first))
    layer_two = jnp.sin(freq_pair[1] * (jnp.dot(layer_one, w_second, precision=PRECISE) + b_second))
    return jnp.dot(layer_two, w_third, precision=PRECISE) * jnp.exp(-lag_pos[:, None] * decay_row[None, :])

def segment_ids(lens_row, length):
    places = jnp.arange(length).astype(jnp.int32)
    ends = jnp.cumsum(lens_row.astype(jnp.int32)).astype(jnp.int32)
    return lax.optimization_barrier(jnp.sum((places[:, None] >= ends[None, :-1]).astype(jnp.int32), axis=1)).astype(jnp.int32)

def short_conv(projected, weight_short, bias_short, seg_ids):
    summed = bias_short[None] + weight_short[0][None] * projected
    for offset in (1, 2):
        shifted = jnp.concatenate([jnp.zeros((offset,) + projected.shape[1:], jnp.float32), projected[:-offset]], axis=0)
        earlier = jnp.concatenate([jnp.full((offset,), -1, jnp.int32), seg_ids[:-offset]], axis=0)
        within = (earlier == seg_ids).astype(jnp.float32)
        summed = summed + weight_short[offset][None] * shifted * within[:, None, None]
    return summed

def group_mixer(projected, lens_row, weight_short, bias_short, skip_row, spectrum_filter):
    length = projected.shape[0]
    seg_ids = segment_ids(lens_row, length)
    gated = short_conv(projected, weight_short, bias_short, seg_ids)
    mixed_in = gated[:, 2] * gated[:, 1]
    result = skip_row * mixed_in
    for seq_pos in range(lens_row.shape[0]):
        mask_one = (seg_ids == seq_pos).astype(jnp.float32)
        spectrum = jnp.fft.rfft(mixed_in * mask_one[:, None], n=2 * length, axis=0)
        result = result + mask_one[:, None] * jnp.fft.irfft(spectrum * spectrum_filter, n=2 * length, axis=0)[:length]
    return result * gated[:, 0]

def forward(inputs, ln1_gain, ln1_bias, w_in, b_in, conv_weight, conv_bias, filt_w1, filt_b1, filt_w2, filt_b2, filt_freq, filt_w3, decay_rate, skip_gain, w_out, b_out, ln2_gain, ln2_bias, w_up, b_up, w_down, b_down, lengths):
    current = inputs
    for layer_idx in range(LAYERS):
        normed = low(layer_norm(current, ln1_gain[layer_idx], ln1_bias[layer_idx]))
        projected = low_back(jnp.einsum('td,dkc->tkc', normed, w_in[layer_idx], precision=PRECISE) + b_in[layer_idx])
        taps_long = filter_taps(filt_w1[layer_idx], filt_b1[layer_idx], filt_w2[layer_idx], filt_b2[layer_idx], filt_freq[layer_idx], filt_w3[layer_idx], decay_rate[layer_idx], GT)
        spectrum_filter = jnp.fft.rfft(taps_long, n=2 * GT, axis=0)
        grouped = projected.reshape(N_DP, GT, 3, D)
        weight_short = conv_weight[layer_idx]
        bias_short = conv_bias[layer_idx]
        skip_row = skip_gain[layer_idx]
        mixer_val = jax.vmap(lambda proj_group, lens_group: group_mixer(proj_group, lens_group, weight_short, bias_short, skip_row, spectrum_filter))(grouped, lengths)
        mixer_val = low(mixer_val.reshape(TOKENS, D))
        middle = current + low_back(jnp.dot(mixer_val, w_out[layer_idx], precision=PRECISE) + b_out[layer_idx])
        normed_two = low(layer_norm(middle, ln2_gain[layer_idx], ln2_bias[layer_idx]))
        hidden_pre = low_back(jnp.dot(normed_two, w_up[layer_idx], precision=PRECISE) + b_up[layer_idx])
        hidden_low = low(jax.nn.gelu(hidden_pre))
        current = middle + low_back(jnp.dot(hidden_low, w_down[layer_idx], precision=PRECISE) + b_down[layer_idx])
    return current

def reference(inputs, cotangent, lengths, ln1_gain, ln1_bias, w_in, b_in, conv_weight, conv_bias, filt_w1, filt_b1, filt_w2, filt_b2, filt_freq, filt_w3, decay_rate, skip_gain, w_out, b_out, ln2_gain, ln2_bias, w_up, b_up, w_down, b_down):
    lens_int = lengths.astype(jnp.int32)
    floats = [inputs, ln1_gain, ln1_bias, w_in, b_in, conv_weight, conv_bias, filt_w1, filt_b1, filt_w2, filt_b2, filt_freq, filt_w3, decay_rate, skip_gain, w_out, b_out, ln2_gain, ln2_bias, w_up, b_up, w_down, b_down]
    floats = [value.astype(jnp.float32) for value in floats]

    def closed(*values):
        return forward(*values, lens_int)
    result, pull_back = jax.vjp(closed, *floats)
    grads = pull_back(cotangent.astype(jnp.float32))
    return (result, grads[0], grads[1], grads[2], grads[3], grads[4], grads[5], grads[6], grads[7], grads[8], grads[9], grads[10], grads[11], grads[12], grads[13], grads[14], grads[15], grads[16], grads[17], grads[18], grads[19], grads[20], grads[21], grads[22])
```

```python
import functools
import math
import types

import jax
import jax.numpy as jnp
import numpy as np
from jax import lax
from jax.experimental import pallas as pl
from jax.experimental.pallas import tpu as pltpu
from jax.sharding import PartitionSpec as P

NORM_EPS = 1e-05
PRECISE = lax.Precision.HIGHEST


def layer_norm(values, norm_gain, norm_shift):
    center = values - jnp.mean(values, axis=-1, keepdims=True)
    spread = jnp.mean(center * center, axis=-1, keepdims=True)
    return center * lax.rsqrt(spread + NORM_EPS) * norm_gain + norm_shift


def filter_taps(w_first, b_first, w_second, b_second, freq_pair, w_third, decay_row, length):
    lag_pos = jnp.arange(length).astype(jnp.float32)
    fraction = lag_pos / length
    band_ids = jnp.arange(1, w_first.shape[0] // 2 + 1).astype(jnp.float32)
    phases = 2.0 * math.pi * fraction[:, None] * band_ids[None, :]
    embedding = jnp.concatenate([fraction[:, None], jnp.cos(phases), jnp.sin(phases)], axis=1)
    layer_one = jnp.sin(freq_pair[0] * (jnp.dot(embedding, w_first, precision=PRECISE) + b_first))
    layer_two = jnp.sin(freq_pair[1] * (jnp.dot(layer_one, w_second, precision=PRECISE) + b_second))
    return jnp.dot(layer_two, w_third, precision=PRECISE) * jnp.exp(
        -lag_pos[:, None] * decay_row[None, :]
    )


def segment_ids(lens_row, length):
    places = jnp.arange(length)
    ends = jnp.cumsum(lens_row)
    return jnp.sum((places[:, None] >= ends[None, :-1]).astype(jnp.int32), axis=1)


def short_conv(projected, weight_short, bias_short, seg_ids):
    summed = bias_short[None] + weight_short[0][None] * projected
    for offset in (1, 2):
        shifted = jnp.concatenate(
            [jnp.zeros((offset,) + projected.shape[1:], jnp.float32), projected[:-offset]], axis=0
        )
        earlier = jnp.concatenate([jnp.full((offset,), -1, jnp.int32), seg_ids[:-offset]], axis=0)
        within = (earlier == seg_ids).astype(jnp.float32)
        summed = summed + weight_short[offset][None] * shifted * within[:, None, None]
    return summed


def trig_table(count_rows, count_cols, modulus):
    product = jnp.arange(count_rows)[:, None] * jnp.arange(count_cols)[None, :] % modulus
    phases = product.astype(jnp.float32) * (2.0 * math.pi / modulus)
    return (jnp.cos(phases), jnp.sin(phases))


def forward_dft(signal, tables):
    cos_a, sin_a, cos_t, sin_t, cos_b, sin_b = tables
    shaped = signal.reshape(cos_a.shape[0], cos_b.shape[0], signal.shape[1])
    real_one = jnp.einsum("abc,ak->kbc", shaped, cos_a, precision=PRECISE)
    imag_one = -jnp.einsum("abc,ak->kbc", shaped, sin_a, precision=PRECISE)
    turn_re = cos_t[:, :, None]
    turn_im = sin_t[:, :, None]
    real_two = real_one * turn_re + imag_one * turn_im
    imag_two = imag_one * turn_re - real_one * turn_im
    real_out = jnp.einsum("kbc,bj->kjc", real_two, cos_b, precision=PRECISE) + jnp.einsum(
        "kbc,bj->kjc", imag_two, sin_b, precision=PRECISE
    )
    imag_out = jnp.einsum("kbc,bj->kjc", imag_two, cos_b, precision=PRECISE) - jnp.einsum(
        "kbc,bj->kjc", real_two, sin_b, precision=PRECISE
    )
    return (real_out, imag_out)


def inverse_dft(real_in, imag_in, tables):
    cos_a, sin_a, cos_t, sin_t, cos_b, sin_b = tables
    real_one = jnp.einsum("kjc,bj->kbc", real_in, cos_b, precision=PRECISE) - jnp.einsum(
        "kjc,bj->kbc", imag_in, sin_b, precision=PRECISE
    )
    imag_one = jnp.einsum("kjc,bj->kbc", imag_in, cos_b, precision=PRECISE) + jnp.einsum(
        "kjc,bj->kbc", real_in, sin_b, precision=PRECISE
    )
    turn_re = cos_t[:, :, None]
    turn_im = sin_t[:, :, None]
    real_two = real_one * turn_re - imag_one * turn_im
    imag_two = imag_one * turn_re + real_one * turn_im
    shaped = jnp.einsum("kbc,ak->abc", real_two, cos_a, precision=PRECISE) - jnp.einsum(
        "kbc,ak->abc", imag_two, sin_a, precision=PRECISE
    )
    total_len = 2 * shaped.shape[0] * shaped.shape[1]
    return shaped.reshape(shaped.shape[0] * shaped.shape[1], shaped.shape[2]) / total_len


def local(
    inputs,
    cotangent,
    lengths,
    ln1_gain,
    ln1_bias,
    w_in,
    b_in,
    conv_weight,
    conv_bias,
    filt_w1,
    filt_b1,
    filt_w2,
    filt_b2,
    filt_freq,
    filt_w3,
    decay_rate,
    skip_gain,
    w_out,
    b_out,
    ln2_gain,
    ln2_bias,
    w_up,
    b_up,
    w_down,
    b_down,
):
    rows_dev = inputs.shape[0]
    tensor_size = lax.axis_size("tensor")
    group_len = rows_dev * tensor_size
    layer_count = w_in.shape[0]
    seg_ids = segment_ids(lengths[0], group_len)
    masks_seq = tuple(
        ((seg_ids == seq_pos).astype(jnp.float32) for seq_pos in range(lengths.shape[1]))
    )
    full_len = 2 * group_len
    fold_a = math.gcd(full_len, 128)
    fold_b = full_len // fold_a
    cos_a, sin_a = trig_table(fold_a // 2, fold_a, fold_a)
    cos_t, sin_t = trig_table(fold_a, fold_b, full_len)
    cos_b, sin_b = trig_table(fold_b, fold_b, fold_b)
    tables = (cos_a, sin_a, cos_t, sin_t, cos_b, sin_b)

    def mixer_local(
        projected,
        weight_short,
        bias_short,
        fw_one,
        fb_one,
        fw_two,
        fb_two,
        freq_pair,
        fw_three,
        decay_row,
        skip_row,
    ):
        gated = short_conv(projected, weight_short, bias_short, seg_ids)
        taps_long = filter_taps(
            fw_one, fb_one, fw_two, fb_two, freq_pair, fw_three, decay_row, group_len
        )
        filt_re, filt_im = forward_dft(taps_long, tables)
        mixed_in = gated[:, 2] * gated[:, 1]
        result = skip_row * mixed_in
        for mask_one in masks_seq:
            sig_re, sig_im = forward_dft(mixed_in * mask_one[:, None], tables)
            result = result + mask_one[:, None] * inverse_dft(
                sig_re * filt_re - sig_im * filt_im, sig_re * filt_im + sig_im * filt_re, tables
            )
        return result * gated[:, 0]

    kept_list = []
    current = inputs
    for layer_idx in range(layer_count):
        normed, norm_back = jax.vjp(layer_norm, current, ln1_gain[layer_idx], ln1_bias[layer_idx])
        normed_full = lax.all_gather(normed.astype(jnp.bfloat16), "tensor", axis=0, tiled=True)
        projected = (
            jnp.einsum(
                "td,dkc->tkc", normed_full, w_in[layer_idx], preferred_element_type=jnp.float32
            )
            + b_in[layer_idx]
        )
        mixer_val, mixer_back = jax.vjp(
            mixer_local,
            projected,
            conv_weight[layer_idx],
            conv_bias[layer_idx],
            filt_w1[layer_idx],
            filt_b1[layer_idx],
            filt_w2[layer_idx],
            filt_b2[layer_idx],
            filt_freq[layer_idx],
            filt_w3[layer_idx],
            decay_rate[layer_idx],
            skip_gain[layer_idx],
        )
        mixer_low = mixer_val.astype(jnp.bfloat16)
        weight_out = w_out[layer_idx]
        keep_out = lax.all_to_all(mixer_low, "tensor", split_axis=0, concat_axis=1, tiled=True)
        weight_out = lax.all_gather(weight_out, "tensor", axis=0, tiled=True)
        branch_out = jnp.dot(keep_out, weight_out, preferred_element_type=jnp.float32)
        middle = current + branch_out + b_out[layer_idx]
        normed_two, norm_two_back = jax.vjp(
            layer_norm, middle, ln2_gain[layer_idx], ln2_bias[layer_idx]
        )
        normed_two_low = normed_two.astype(jnp.bfloat16)
        up_full, upb_full, down_full = (
            lax.all_gather(w_up[layer_idx], ("dp", "tensor"), axis=1, tiled=True),
            lax.all_gather(b_up[layer_idx], ("dp", "tensor"), axis=0, tiled=True),
            lax.all_gather(w_down[layer_idx], ("dp", "tensor"), axis=0, tiled=True),
        )
        hidden_pre = jnp.dot(
            normed_two_low, up_full, preferred_element_type=jnp.float32
        ) + upb_full.astype(jnp.float32)
        hidden_act, gelu_back = jax.vjp(jax.nn.gelu, hidden_pre)
        hidden_low = hidden_act.astype(jnp.bfloat16)
        current = (
            middle
            + jnp.dot(hidden_low, down_full, preferred_element_type=jnp.float32)
            + b_down[layer_idx]
        )
        kept_list.append(
            (
                norm_back,
                normed_full,
                mixer_back,
                keep_out,
                weight_out,
                norm_two_back,
                normed_two_low,
                None,
                None,
                hidden_low,
                gelu_back,
            )
        )
    grad_rows = cotangent
    per_layer = [None] * layer_count
    for layer_idx in reversed(range(layer_count)):
        (
            norm_back,
            normed_full,
            mixer_back,
            keep_out,
            weight_out,
            norm_two_back,
            normed_two_low,
            up_full,
            down_full,
            hidden_low,
            gelu_back,
        ) = kept_list[layer_idx]
        up_full, down_full = (
            lax.all_gather(w_up[layer_idx], ("dp", "tensor"), axis=1, tiled=True),
            lax.all_gather(w_down[layer_idx], ("dp", "tensor"), axis=0, tiled=True),
        )
        down_low = grad_rows.astype(jnp.bfloat16)
        grad_b_down = jnp.sum(down_low.astype(jnp.float32), axis=0)
        grad_w_down = jnp.einsum(
            "tf,td->fd", hidden_low, down_low, preferred_element_type=jnp.float32
        )
        grad_hidden = jnp.einsum(
            "td,fd->tf", down_low, down_full, preferred_element_type=jnp.float32
        )
        (grad_pre,) = gelu_back(grad_hidden)
        pre_low = grad_pre.astype(jnp.bfloat16)
        grad_w_up = jnp.einsum(
            "td,tf->df", normed_two_low, pre_low, preferred_element_type=jnp.float32
        )
        grad_b_up = jnp.sum(pre_low.astype(jnp.float32), axis=0)
        grad_normed_two = jnp.einsum(
            "tf,df->td", pre_low, up_full, preferred_element_type=jnp.float32
        )
        shard_w_up, shard_b_up, shard_w_down = (
            lax.psum_scatter(grad_w_up, ("dp", "tensor"), scatter_dimension=1, tiled=True),
            lax.psum_scatter(grad_b_up, ("dp", "tensor"), scatter_dimension=0, tiled=True),
            lax.psum_scatter(grad_w_down, ("dp", "tensor"), scatter_dimension=0, tiled=True),
        )
        grad_middle_ln, grad_ln2_gain, grad_ln2_bias = norm_two_back(grad_normed_two)
        grad_middle = grad_rows + grad_middle_ln
        out_low = grad_middle.astype(jnp.bfloat16)
        grad_b_out = jnp.sum(out_low.astype(jnp.float32), axis=0)
        grad_rows_mixed = jnp.einsum(
            "td,cd->tc", out_low, weight_out, preferred_element_type=jnp.float32
        )
        grad_mixed = lax.all_to_all(
            grad_rows_mixed.astype(jnp.bfloat16), "tensor", split_axis=1, concat_axis=0, tiled=True
        ).astype(grad_rows_mixed.dtype)
        grad_w_out = lax.psum_scatter(
            jnp.einsum("tc,td->cd", keep_out, out_low, preferred_element_type=jnp.float32).astype(
                jnp.bfloat16
            ),
            "tensor",
            scatter_dimension=0,
            tiled=True,
        ).astype(jnp.float32)
        grads_mixer = mixer_back(grad_mixed)
        proj_low = grads_mixer[0].astype(jnp.bfloat16)
        grad_w_in = jnp.einsum(
            "td,tkc->dkc", normed_full, proj_low, preferred_element_type=jnp.float32
        )
        grad_b_in = jnp.sum(proj_low.astype(jnp.float32), axis=0)
        weight_in = w_in[layer_idx]
        grad_normed = lax.psum_scatter(
            jnp.einsum(
                "tkc,dkc->td", proj_low, weight_in, preferred_element_type=jnp.float32
            ).astype(jnp.bfloat16),
            "tensor",
            scatter_dimension=0,
            tiled=True,
        ).astype(jnp.float32)
        grad_in_ln, grad_ln1_gain, grad_ln1_bias = norm_back(grad_normed)
        grad_rows = grad_middle + grad_in_ln
        per_layer[layer_idx] = (
            grad_ln1_gain,
            grad_ln1_bias,
            grad_w_in,
            grad_b_in,
            grads_mixer[1],
            grads_mixer[2],
            grads_mixer[3],
            grads_mixer[4],
            grads_mixer[5],
            grads_mixer[6],
            grads_mixer[7],
            grads_mixer[8],
            grads_mixer[9],
            grads_mixer[10],
            grad_w_out,
            grad_b_out,
            grad_ln2_gain,
            grad_ln2_bias,
            shard_w_up,
            shard_b_up,
            shard_w_down,
            grad_b_down,
        )
    stacks = [
        jnp.stack([per_layer[layer_pos][slot_pos] for layer_pos in range(layer_count)])
        for slot_pos in range(22)
    ]
    shared_done = lax.psum(
        (
            stacks[0],
            stacks[1],
            stacks[6],
            stacks[7],
            stacks[8],
            stacks[9],
            stacks[10],
            stacks[15],
            stacks[16],
            stacks[17],
            stacks[21],
        ),
        ("dp", "tensor"),
    )
    weight_done = (
        lax.psum_scatter(
            stacks[2].astype(jnp.bfloat16), "dp", scatter_dimension=1, tiled=True
        ).astype(jnp.float32),
        lax.psum_scatter(
            stacks[14].astype(jnp.bfloat16), "dp", scatter_dimension=2, tiled=True
        ).astype(jnp.float32),
    )
    group_done = (
        lax.psum(stacks[3].astype(jnp.bfloat16), "dp").astype(jnp.float32),
        lax.psum(stacks[4].astype(jnp.bfloat16), "dp").astype(jnp.float32),
        lax.psum(stacks[5].astype(jnp.bfloat16), "dp").astype(jnp.float32),
        lax.psum(stacks[11].astype(jnp.bfloat16), "dp").astype(jnp.float32),
        lax.psum(stacks[12].astype(jnp.bfloat16), "dp").astype(jnp.float32),
        lax.psum(stacks[13].astype(jnp.bfloat16), "dp").astype(jnp.float32),
    )
    return (
        current,
        grad_rows,
        shared_done[0],
        shared_done[1],
        weight_done[0],
        group_done[0],
        group_done[1],
        group_done[2],
        shared_done[2],
        shared_done[3],
        shared_done[4],
        shared_done[5],
        shared_done[6],
        group_done[3],
        group_done[4],
        group_done[5],
        weight_done[1],
        shared_done[7],
        shared_done[8],
        shared_done[9],
        stacks[18],
        stacks[19],
        stacks[20],
        shared_done[10],
    )


BF16 = jnp.bfloat16
F32 = jnp.float32
MESH = pl.DeviceIdType.MESH
SHARE = 4
GELU_C = math.sqrt(2.0 / math.pi)
GELU_A = 0.044715


def dot_nn(a, b, precision=None):
    return lax.dot_general(
        a, b, (((1,), (0,)), ((), ())), precision=precision, preferred_element_type=F32
    )


def dot_nt(a, b, precision=None):
    return lax.dot_general(
        a, b, (((1,), (1,)), ((), ())), precision=precision, preferred_element_type=F32
    )


def dot_tn(a, b, precision=None):
    return lax.dot_general(
        a, b, (((0,), (0,)), ((), ())), precision=precision, preferred_element_type=F32
    )


class Sizes:
    def __init__(self, mesh_dp, mesh_tp, rows, width, chan, shard, slots, layers, emb, filt):
        self.ndp, self.n = mesh_dp, mesh_tp
        self.R, self.D, self.C = rows, width, chan
        self.T = rows * mesh_tp
        self.FFs = shard
        self.FFp = -(-shard // 16) * 16
        self.FR = 2 * self.FFp + 16
        self.Y = mesh_dp // SHARE
        self.FB = mesh_tp * self.FFp
        self.SL, self.L = slots, layers
        self.EMB, self.FILT = emb, filt
        self.EP = -(-emb // 8) * 8
        self.DB = width // mesh_dp
        self.TL = rows // 2
        self.FROWS = self.EP + filt + 8


INPUTS = (
    "x", "cot", "lens", "ln1g", "ln1b", "w_in", "b_in", "cw", "cb", "emb", "fw1", "fb1", "fw2",
    "fb2", "freq", "fw3", "decay", "skip", "w_out", "b_out", "ln2g", "ln2b", "ff", "b_down",
    "dft", "dftt",
)
OUTPUTS = ("out", "gin", "ffo", "wo", "sa", "sf", "sc")


def scratch_shapes(z):
    R, D, C, T, n, L, Y = z.R, z.D, z.C, z.T, z.n, z.L, z.Y
    steps_dp = z.ndp.bit_length() - 1
    steps = steps_dp + n.bit_length() - 1
    per = 6 * (n - 1) + n * (Y - 1) + 3 * 4 + (Y - 1) + (n - 1) + (z.ndp - 1)
    sems = L * (per + 3 * steps)
    shapes = dict(
        xs=((max(L - 1, 1), R, D), F32),
        mids=((L, R, D), F32),
        gx=((R, D), F32),
        nF=((L, n, R, D), BF16),
        p=((L, 3, T + 8, C), F32),
        inn=((L, T, C), F32),
        innb=((T, C), BF16),
        g0s=((T, C), F32),
        z12=((L, 2, T, z.FILT), F32),
        taps=((L, T, C), F32),
        hs=((L, 2, T, C), F32),
        xf=((L, 2, T, C), BF16),
        yb=((2, T, C), BF16),
        qb=((2, T, C), BF16),
        longs=((L, T, C), F32),
        mx=((L, T, C), BF16),
        zp=((n, R, D), BF16),
        zr=((L, n - 1, R, D), BF16),
        n2S=((L, SHARE, R, D), BF16),
        ffw=((L, Y, n, z.FR, D), BF16),
        bup=((L, Y, 8, z.FB), F32),
        hp=((L, Y, SHARE * R, z.FB), BF16),
        sp=((3, R, D), BF16),
        sr=((L, 3, R, D), BF16),
        gdS=((L, SHARE, R, D), BF16),
        hb=((Y, SHARE * R, z.FB), BF16),
        gpb=((Y, SHARE * R, z.FB), BF16),
        ffg=((Y, n, z.FR, D), BF16),
        ffry=((L, Y - 1, n, z.FR, D), BF16),
        ffrz=((L, n - 1, z.FR, D), BF16),
        goF=((L, n, R, D), BF16),
        gg=((3, T + 8, C), F32),
        gpj=((3, T, C), BF16),
        gl=((T, C), F32),
        gtp=((T, C), F32),
        gtt=((z.TL, C), F32),
        wg=((z.ndp, 4, z.DB, C), BF16),
        wr=((L, z.ndp - 1, 4, z.DB, C), BF16),
        rA=((L, steps, 8, D), F32),
        rF=((L, steps, z.FROWS, z.FILT), F32),
        rC=((L, steps_dp, 24 + z.FILT, C), F32),
    )
    return shapes, sems, steps_dp, steps


def vmem_bytes(shapes):
    total = 0
    for dims, kind in shapes.values():
        size = 2 if kind == BF16 else 4
        sub = 32 // size
        lanes = -(-dims[-1] // 128) * 128
        rows = -(-dims[-2] // sub) * sub
        total += math.prod(dims[:-2]) * rows * lanes * size
    return total


def fused_kernel(z, names, *refs):
    R, D, C, T, n, L, Y, ndp = z.R, z.D, z.C, z.T, z.n, z.L, z.Y, z.ndp
    FFp, FB, FILT, EP, DB, TL = z.FFp, z.FB, z.FILT, z.EP, z.DB, z.TL
    s = types.SimpleNamespace(**dict(zip(names, refs)))
    dp = lax.axis_index("dp")
    ti = lax.axis_index("tensor")
    y = dp // SHARE
    q = dp % SHARE
    sib = dp + 1 - 2 * (dp % 2)
    xnb = dp + 2 - 4 * ((dp // 2) % 2)
    used = [0]
    open_sends = []

    def push(src, dst, dev):
        idx = used[0]
        used[0] += 1
        copy = pltpu.make_async_remote_copy(
            src_ref=src, dst_ref=dst, send_sem=s.ssem.at[idx], recv_sem=s.rsem.at[idx],
            device_id=dev, device_id_type=MESH,
        )
        copy.start()
        open_sends.append(copy)
        return copy

    def flush():
        for copy in open_sends:
            copy.wait_send()
        open_sends.clear()

    def done(copy):
        copy.wait_recv()

    barrier = pltpu.get_barrier_semaphore()
    for d in range(1, ndp):
        pl.semaphore_signal(barrier, inc=1, device_id=((dp + d) % ndp, ti), device_id_type=MESH)
    for d in range(1, n):
        pl.semaphore_signal(barrier, inc=1, device_id=(dp, (ti + d) % n), device_id_type=MESH)
    pl.semaphore_wait(barrier, ndp - 1 + n - 1)

    ends = []
    total = s.lens[0, 0]
    ends.append(total)
    for k in range(1, z.SL - 1):
        total = total + s.lens[0, k]
        ends.append(total)

    def ln_parts(v):
        mu = jnp.mean(v, axis=-1, keepdims=True)
        c = v - mu
        r = lax.rsqrt(jnp.mean(c * c, axis=-1, keepdims=True) + NORM_EPS)
        return c * r, r

    def ln_back(v, gy, gain):
        xhat, r = ln_parts(v)
        gz = gy * gain
        gv = r * (
            gz - jnp.mean(gz, axis=-1, keepdims=True)
            - xhat * jnp.mean(gz * xhat, axis=-1, keepdims=True)
        )
        return gv, jnp.sum(gy * xhat, axis=0, keepdims=True), jnp.sum(gy, axis=0, keepdims=True)

    def layer_input(l):
        return s.x[...] if l == 0 else s.xs[l - 1]

    def gather_z(buf, l):
        return [
            push(buf.at[l, ti], buf.at[l, ti], (dp, (ti + d) % n)) for d in range(1, n)
        ]

    def scatter_z(l):
        copies = []
        for d in range(1, n):
            j = (ti + d) % n
            copies.append(push(s.zp.at[j], s.zr.at[l, d - 1], (dp, j)))
        return copies

    def sum_z(l, copies):
        acc = s.zp[ti].astype(F32)
        for d in range(1, n):
            done(copies[d - 1])
            acc = acc + s.zr[l, d - 1].astype(F32)
        return acc

    def gather_s(buf, l):
        to_sib = push(buf.at[l, 0], buf.at[l, 1], (sib, ti))
        to_x = push(buf.at[l, 0], buf.at[l, 2], (xnb, ti))
        done(to_x)
        onward = push(buf.at[l, 2], buf.at[l, 3], (sib, ti))
        done(to_sib)
        done(onward)

    def scatter_s(l, block):
        s.sp[0] = block(3).astype(BF16)
        c3 = push(s.sp.at[0], s.sr.at[l, 1], (sib, ti))
        v2 = block(2)
        done(c3)
        s.sp[1] = (v2 + s.sr[l, 1].astype(F32)).astype(BF16)
        cx = push(s.sp.at[1], s.sr.at[l, 2], (xnb, ti))
        s.sp[2] = block(1).astype(BF16)
        c1 = push(s.sp.at[2], s.sr.at[l, 0], (sib, ti))
        v0 = block(0)
        done(c1)
        done(cx)
        return v0 + s.sr[l, 0].astype(F32) + s.sr[l, 2].astype(F32)

    def ff_start(l):
        s.ffw[l, y, ti] = s.ff[l]
        return [
            push(s.ffw.at[l, y, ti], s.ffw.at[l, y, ti], (dp, (ti + d) % n))
            for d in range(1, n)
        ]

    def ff_own(l):
        return [
            push(s.ffw.at[l, y, ti], s.ffw.at[l, y, ti], (((y + e) % Y) * SHARE + q, ti))
            for e in range(1, Y)
        ]

    def ff_forward(l, copies):
        sent = []
        for d in range(1, n):
            done(copies[d - 1])
            j = (ti + n - d) % n
            for e in range(1, Y):
                sent.append(
                    push(s.ffw.at[l, y, j], s.ffw.at[l, y, j], (((y + e) % Y) * SHARE + q, ti))
                )
        return sent

    def ff_ready(l):
        for b in range(Y):
            row = jnp.zeros((16, D), F32)
            for j in range(n):
                part = s.ffw[l, b, j, 2 * FFp : 2 * FFp + 16, :].astype(F32)
                row = row + (pltpu.roll(part, FFp * j, 1) if j else part)
            s.bup[l, b] = row[:8, :FB]

    def ff_up(l, b):
        return s.ffw[l, b, :, 0:FFp, :].reshape(FB, D)

    def ff_down(l, b):
        return s.ffw[l, b, :, FFp : 2 * FFp, :].reshape(FB, D)

    CH = 64

    def chunk_masks(r0, rows):
        t = lax.broadcasted_iota(jnp.int32, (rows, C), 0) + r0
        one = jnp.ones((rows, C), F32)
        m1 = one
        for e in ends:
            m1 = jnp.where(t == e, 0.0, m1)
        m2 = m1
        for e in ends:
            m2 = jnp.where(t == e + 1, 0.0, m2)
        return m1, m2

    def conv_row(l, step, k):
        return s.cw[l, step * 3 + k : step * 3 + k + 1, :]

    def shifted(l, k, r0, m1, m2):
        blk = s.p[l, k, pl.ds(r0, CH + 8), :]
        return blk[8:], blk[7:-1] * m1, blk[6:-2] * m2

    def gate(l, k, parts):
        return (
            s.cb[l, k : k + 1, :]
            + conv_row(l, 0, k) * parts[0]
            + conv_row(l, 1, k) * parts[1]
            + conv_row(l, 2, k) * parts[2]
        )

    def lag_rows(rows, cols, r0=0):
        return (lax.broadcasted_iota(jnp.int32, (rows, cols), 0) + r0).astype(F32)

    def filter_forward(l):
        freq0 = s.freq[l, 0:1, :]
        freq1 = s.freq[l, 1:2, :]
        z1 = dot_nn(s.emb[...], s.fw1[l], PRECISE) + s.fb1[l]
        s.z12[l, 0] = z1
        a1 = jnp.sin(freq0 * z1)
        z2 = dot_nn(a1, s.fw2[l], PRECISE) + s.fb2[l]
        s.z12[l, 1] = z2
        a2 = jnp.sin(freq1 * z2)
        tp = dot_nn(a2, s.fw3[l], PRECISE) * jnp.exp(-lag_rows(T, C) * s.decay[l])
        s.taps[l] = tp
        s.innb[...] = tp.astype(BF16)

        @pl.loop(0, n)
        def _(i):
            rows = pl.ds(pl.multiple_of(i * R, R), R)
            s.hs[l, 0, rows, :] = dot_nn(s.dft[0, rows, :], s.innb[...])
            s.hs[l, 1, rows, :] = dot_nn(s.dft[1, rows, :], s.innb[...])

    def tail_index():
        return lax.broadcasted_iota(jnp.int32, (TL, C), 0)

    def tail_starts():
        t = tail_index() + (T - TL)
        st = jnp.full((TL, C), T, jnp.int32)
        for k in range(z.SL - 1):
            st = jnp.where(t >= ends[k], ends[k] - (T - TL), st)
        return st

    def tail_ends():
        t = tail_index() + (T - TL)
        en = jnp.full((TL, C), TL, jnp.int32)
        for k in range(z.SL - 2, 0, -1):
            en = jnp.where(t < ends[k], ends[k] - (T - TL), en)
        return jnp.where(t < ends[0], -T, en)

    def mixer_forward(l):
        @pl.loop(0, T // CH)
        def _(i):
            r0 = pl.multiple_of(i * CH, CH)
            m1, m2 = chunk_masks(r0, CH)
            g0 = gate(l, 0, shifted(l, 0, r0, m1, m2))
            g1 = gate(l, 1, shifted(l, 1, r0, m1, m2))
            g2 = gate(l, 2, shifted(l, 2, r0, m1, m2))
            inner = g2 * g1
            s.g0s[pl.ds(r0, CH), :] = g0
            s.inn[l, pl.ds(r0, CH), :] = inner
            s.innb[pl.ds(r0, CH), :] = inner.astype(BF16)

        @pl.loop(0, n)
        def _(i):
            rows = pl.ds(pl.multiple_of(i * R, R), R)
            xr = dot_nn(s.dft[0, rows, :], s.innb[...])
            xi = dot_nn(s.dft[1, rows, :], s.innb[...])
            hr = s.hs[l, 0, rows, :]
            hi = s.hs[l, 1, rows, :]
            s.xf[l, 0, rows, :] = xr.astype(BF16)
            s.xf[l, 1, rows, :] = xi.astype(BF16)
            s.yb[0, rows, :] = (xr * hr - xi * hi).astype(BF16)
            s.yb[1, rows, :] = (xr * hi + xi * hr).astype(BF16)

        idx = tail_index()
        starts = tail_starts()

        def lag_step(d, carry):
            acc, cur = carry
            tap = s.taps[l, pl.ds(d, 1), :]
            acc = acc + jnp.where(idx - d >= starts, cur, 0.0) * tap
            return acc, pltpu.roll(cur, 1, 0)

        tail, _ = lax.fori_loop(
            0, TL, lag_step, (jnp.zeros((TL, C), F32), s.inn[l, T - TL : T, :])
        )
        s.gtt[...] = tail

        @pl.loop(0, n)
        def _(i):
            rows = pl.ds(pl.multiple_of(i * R, R), R)
            s.longs[l, rows, :] = (
                dot_nn(s.dftt[0, rows, :], s.yb[0]) + dot_nn(s.dftt[1, rows, :], s.yb[1])
            ) * (1.0 / T)
        first = (tail_index() + (T - TL)) < ends[0]
        s.longs[l, T - TL : T, :] = jnp.where(first, s.longs[l, T - TL : T, :], s.gtt[...])

        @pl.loop(0, n)
        def _(i):
            rows = pl.ds(pl.multiple_of(i * R, R), R)
            lg = s.longs[l, rows, :] + s.skip[l] * s.inn[l, rows, :]
            s.longs[l, rows, :] = lg
            mixed = (lg * s.g0s[rows, :]).astype(BF16)
            s.mx[l, rows, :] = mixed
            s.zp[i] = dot_nn(mixed, s.w_out[l]).astype(BF16)

    def gelu_parts(v):
        th = jnp.tanh(GELU_C * (v + GELU_A * v * v * v))
        return th

    def forward_layer(l, ff_copies):
        x = layer_input(l)
        xhat, _ = ln_parts(x)
        s.nF[l, ti] = (xhat * s.ln1g[l] + s.ln1b[l]).astype(BF16)
        ag = gather_z(s.nF, l)
        if l == 0:
            ff_copies = ff_start(l)
        own = ff_own(l)
        filter_forward(l)
        for k in range(3):
            s.p[l, k, 0:8, :] = jnp.zeros((8, C), F32)
        for c in ag:
            done(c)

        @pl.loop(0, n)
        def _(j):
            rows = pl.ds(pl.multiple_of(j * R + 8, 8), R)
            for k in range(3):
                s.p[l, k, rows, :] = dot_nn(s.nF[l, j], s.w_in[l, k]) + s.b_in[l, k : k + 1, :]

        mixer_forward(l)
        rs = scatter_z(l)
        passed = ff_forward(l, ff_copies)
        mid = x + s.b_out[l] + sum_z(l, rs)
        s.mids[l] = mid
        xhat2, _ = ln_parts(mid)
        s.n2S[l, 0] = (xhat2 * s.ln2g[l] + s.ln2b[l]).astype(BF16)
        gather_s(s.n2S, l)
        for c in own + passed:
            done(c)
        ff_ready(l)
        nxt = ff_start(l + 1) if l + 1 < L else None

        def block(r):
            v = s.n2S[l, r]
            acc = jnp.zeros((R, D), F32)
            for b in range(Y):
                pre = dot_nt(v, ff_up(l, b)) + s.bup[l, b, 0:1, :]
                s.hp[l, b, r * R : (r + 1) * R, :] = pre.astype(BF16)
                act = 0.5 * pre * (1.0 + gelu_parts(pre))
                acc = acc + dot_nn(act.astype(BF16), ff_down(l, b))
            return acc

        res = scatter_s(l, block)
        cur = s.mids[l] + s.b_down[l] + res
        if l + 1 < L:
            s.xs[l] = cur
        else:
            s.out[...] = cur
        flush_layer()
        return nxt

    def flush_layer():
        flush()

    def ff_backward(l):
        gd = s.gx[...].astype(BF16)
        s.gdS[l, 0] = gd
        s.sa[l, 5:6, :] = jnp.sum(gd.astype(F32), axis=0, keepdims=True)
        gather_s(s.gdS, l)

        def block(r):
            g = s.gdS[l, r]
            acc = jnp.zeros((R, D), F32)
            rows = slice(r * R, (r + 1) * R)
            for b in range(Y):
                gh = dot_nt(g, ff_down(l, b))
                v = s.hp[l, b, rows, :].astype(F32)
                th = gelu_parts(v)
                s.hb[b, rows, :] = (0.5 * v * (1.0 + th)).astype(BF16)
                slope = 0.5 * (1.0 + th) + 0.5 * v * (1.0 - th * th) * (
                    GELU_C * (1.0 + 3.0 * GELU_A * v * v)
                )
                gp = (gh * slope).astype(BF16)
                s.gpb[b, rows, :] = gp
                acc = acc + dot_nn(gp, ff_up(l, b))
            return acc

        return scatter_s(l, block)

    def ff_grads(l):
        act = s.n2S[l].reshape(SHARE * R, D)
        gds = s.gdS[l].reshape(SHARE * R, D)

        def fill(b):
            g = s.gpb[b]
            h = s.hb[b]
            s.ffg[b, :, 0:FFp, :] = dot_tn(g, act).astype(BF16).reshape(n, FFp, D)
            s.ffg[b, :, FFp : 2 * FFp, :] = dot_tn(h, gds).astype(BF16).reshape(n, FFp, D)
            sums = jnp.sum(g.astype(F32), axis=0, keepdims=True)
            row = jnp.concatenate([sums, jnp.zeros((1, D - FB), F32)], axis=1) if D > FB else sums
            row = jnp.broadcast_to(row, (16, D))
            for j in range(n):
                part = pltpu.roll(row, (D - FFp * j) % D, 1) if j else row
                s.ffg[b, j, 2 * FFp : 2 * FFp + 16, :] = part.astype(BF16)

        copies = []
        for e in range(1, Y):
            b = (y + e) % Y
            fill(b)
            copies.append(push(s.ffg.at[b], s.ffry.at[l, e - 1], (b * SHARE + q, ti)))
        fill(y)
        return copies

    def ff_second(l, copies):
        for c in copies:
            done(c)

        @pl.loop(0, n)
        def _(j):
            acc = s.ffg[y, j].astype(F32)
            for e in range(1, Y):
                acc = acc + s.ffry[l, e - 1, j].astype(F32)
            s.ffg[y, j] = acc.astype(BF16)

        sent = []
        for d in range(1, n):
            j = (ti + d) % n
            sent.append(push(s.ffg.at[y, j], s.ffrz.at[l, d - 1], (dp, j)))
        return sent

    def ff_last(l, copies):
        acc = s.ffg[y, ti].astype(F32)
        for d in range(1, n):
            done(copies[d - 1])
            acc = acc + s.ffrz[l, d - 1].astype(F32)
        s.ffo[l] = acc

    def mixer_backward(l):
        @pl.loop(0, T // CH)
        def _(i):
            r0 = pl.multiple_of(i * CH, CH)
            rows = pl.ds(r0, CH)
            m1, m2 = chunk_masks(r0, CH)
            g0 = gate(l, 0, shifted(l, 0, r0, m1, m2))
            gm = s.gtp[rows, :]
            glong = gm * g0
            s.gg[0, rows, :] = gm * s.longs[l, rows, :]
            s.gl[rows, :] = glong
            t = lax.broadcasted_iota(jnp.int32, (CH, C), 0) + r0
            s.innb[rows, :] = jnp.where(t < ends[0], glong, 0.0).astype(BF16)

        @pl.loop(0, n)
        def _(i):
            rows = pl.ds(pl.multiple_of(i * R, R), R)
            gr = dot_nn(s.dft[0, rows, :], s.innb[...])
            gi = dot_nn(s.dft[1, rows, :], s.innb[...])
            hr = s.hs[l, 0, rows, :]
            hi = s.hs[l, 1, rows, :]
            s.yb[0, rows, :] = (gr * hr + gi * hi).astype(BF16)
            s.yb[1, rows, :] = (gi * hr - gr * hi).astype(BF16)
            xr = s.xf[l, 0, rows, :].astype(F32)
            xi = s.xf[l, 1, rows, :].astype(F32)
            s.qb[0, rows, :] = (gr * xr + gi * xi).astype(BF16)
            s.qb[1, rows, :] = (gi * xr - gr * xi).astype(BF16)

        idx = tail_index()
        stops = tail_ends()
        inner_tail = s.inn[l, T - TL : T, :]

        def lag_step(d, carry):
            acc, cur = carry
            live = jnp.where(idx + d < stops, cur, 0.0)
            acc = acc + live * s.taps[l, pl.ds(d, 1), :]
            s.gtt[pl.ds(d, 1), :] = jnp.sum(live * inner_tail, axis=0, keepdims=True)
            return acc, pltpu.roll(cur, TL - 1, 0)

        tail, _ = lax.fori_loop(
            0, TL, lag_step, (jnp.zeros((TL, C), F32), s.gl[T - TL : T, :])
        )

        @pl.loop(0, n)
        def _(i):
            rows = pl.ds(pl.multiple_of(i * R, R), R)
            s.g0s[rows, :] = (
                dot_nn(s.dftt[0, rows, :], s.yb[0]) + dot_nn(s.dftt[1, rows, :], s.yb[1])
            ) * (1.0 / T)
            s.gtp[rows, :] = (
                dot_nn(s.dftt[0, rows, :], s.qb[0]) + dot_nn(s.dftt[1, rows, :], s.qb[1])
            ) * (1.0 / T)

        first = (tail_index() + (T - TL)) < ends[0]
        s.g0s[T - TL : T, :] = jnp.where(first, s.g0s[T - TL : T, :], tail)
        s.gtp[0:TL, :] = s.gtp[0:TL, :] + s.gtt[...]

        def fold(v):
            return jnp.sum(v.reshape(CH // 8, 8, C), axis=0)

        for k in range(3):
            s.gg[k, T : T + 8, :] = jnp.zeros((8, C), F32)

        def gate_step(i, sums):
            r0 = pl.multiple_of(i * CH, CH)
            rows = pl.ds(r0, CH)
            m1, m2 = chunk_masks(r0, CH)
            parts = [shifted(l, k, r0, m1, m2) for k in range(3)]
            gl = s.gl[rows, :]
            ginner = s.g0s[rows, :] + s.skip[l] * gl
            gk = [s.gg[0, rows, :], ginner * gate(l, 2, parts[2]), ginner * gate(l, 1, parts[1])]
            s.gg[1, rows, :] = gk[1]
            s.gg[2, rows, :] = gk[2]
            new = []
            for step in range(3):
                for k in range(3):
                    new.append(sums[step * 3 + k] + fold(gk[k] * parts[k][step]))
            for k in range(3):
                new.append(sums[9 + k] + fold(gk[k]))
            new.append(sums[12] + fold(gl * s.inn[l, rows, :]))
            return tuple(new)

        sums = lax.fori_loop(
            0, T // CH, gate_step, tuple(jnp.zeros((8, C), F32) for _ in range(13))
        )
        for pos in range(12):
            s.sc[l, 3 + pos : 4 + pos, :] = jnp.sum(sums[pos], axis=0, keepdims=True)
        s.sc[l, 16:17, :] = jnp.sum(sums[12], axis=0, keepdims=True)

        def proj_step(i, sums):
            r0 = pl.multiple_of(i * CH, CH)
            m1, m2 = chunk_masks(r0, CH + 8)
            new = []
            for k in range(3):
                blk = s.gg[k, pl.ds(r0, CH + 8), :]
                b1 = blk * m1
                b2 = blk * m2
                gp = (
                    conv_row(l, 0, k) * blk[0:CH]
                    + conv_row(l, 1, k) * b1[1 : CH + 1]
                    + conv_row(l, 2, k) * b2[2 : CH + 2]
                ).astype(BF16)
                s.gpj[k, pl.ds(r0, CH), :] = gp
                new.append(sums[k] + fold(gp.astype(F32)))
            return tuple(new)

        sums = lax.fori_loop(
            0, T // CH, proj_step, tuple(jnp.zeros((8, C), F32) for _ in range(3))
        )
        for k in range(3):
            s.sc[l, k : k + 1, :] = jnp.sum(sums[k], axis=0, keepdims=True)

    def filter_backward(l):
        lag = lag_rows(T, C)
        gt = s.gtp[...]
        s.sc[l, 15:16, :] = -jnp.sum(lag * gt * s.taps[l], axis=0, keepdims=True)
        gtr = gt * jnp.exp(-lag * s.decay[l])
        freq0 = s.freq[l, 0:1, :]
        freq1 = s.freq[l, 1:2, :]
        z1 = s.z12[l, 0]
        z2 = s.z12[l, 1]
        u2 = freq1 * z2
        s.sc[l, 24 : 24 + FILT, :] = dot_tn(jnp.sin(u2), gtr, PRECISE)
        gu2 = dot_nt(gtr, s.fw3[l], PRECISE) * jnp.cos(u2)
        gz2 = gu2 * freq1
        u1 = freq0 * z1
        s.sf[l, EP : EP + FILT, :] = dot_tn(jnp.sin(u1), gz2, PRECISE)
        gu1 = dot_nt(gz2, s.fw2[l], PRECISE) * jnp.cos(u1)
        gz1 = gu1 * freq0
        s.sf[l, 0:EP, :] = dot_tn(s.emb[...], gz1, PRECISE)
        row = EP + FILT
        s.sf[l, row : row + 1, :] = jnp.sum(gz1, axis=0, keepdims=True)
        s.sf[l, row + 1 : row + 2, :] = jnp.sum(gz2, axis=0, keepdims=True)
        s.sf[l, row + 2 : row + 3, :] = jnp.sum(gu1 * z1, axis=0, keepdims=True)
        s.sf[l, row + 3 : row + 4, :] = jnp.sum(gu2 * z2, axis=0, keepdims=True)

    def weight_grads(l):
        rows_all = s.nF[l].reshape(T, D)
        go_all = s.goF[l].reshape(T, D)
        for k in range(4):
            for h in range(0, D, 256):
                if k < 3:
                    g = dot_tn(rows_all[:, h : h + 256], s.gpj[k])
                else:
                    g = dot_tn(go_all[:, h : h + 256], s.mx[l])
                gb = g.astype(BF16)
                lo = h
                while lo < h + 256:
                    b = lo // DB
                    off = lo % DB
                    cnt = min(DB - off, h + 256 - lo)
                    s.wg[b, k, off : off + cnt, :] = gb[lo - h : lo - h + cnt]
                    lo += cnt
        copies = []
        for d in range(1, ndp):
            j = (dp + d) % ndp
            copies.append(push(s.wg.at[j], s.wr.at[l, d - 1], (j, ti)))
        return copies

    def weight_last(l, copies):
        acc = s.wg[dp].astype(F32)
        for d in range(1, ndp):
            done(copies[d - 1])
            acc = acc + s.wr[l, d - 1].astype(F32)
        s.wo[l] = acc

    def small_sums(l):
        step = 0
        bit = 1
        while bit < ndp:
            peer = (dp + bit - 2 * bit * ((dp // bit) % 2), ti)
            trio = [
                push(s.sa.at[l], s.rA.at[l, step], peer),
                push(s.sf.at[l], s.rF.at[l, step], peer),
                push(s.sc.at[l], s.rC.at[l, step], peer),
            ]
            for c in trio:
                c.wait_recv()
            flush()
            s.sa[l] = s.sa[l] + s.rA[l, step]
            s.sf[l] = s.sf[l] + s.rF[l, step]
            s.sc[l] = s.sc[l] + s.rC[l, step]
            step += 1
            bit *= 2
        bit = 1
        while bit < n:
            peer = (dp, ti + bit - 2 * bit * ((ti // bit) % 2))
            duo = [
                push(s.sa.at[l], s.rA.at[l, step], peer),
                push(s.sf.at[l], s.rF.at[l, step], peer),
            ]
            for c in duo:
                c.wait_recv()
            flush()
            s.sa[l] = s.sa[l] + s.rA[l, step]
            s.sf[l] = s.sf[l] + s.rF[l, step]
            step += 1
            bit *= 2

    def backward_layer(l):
        s.sa[l] = jnp.zeros((8, D), F32)
        s.sf[l] = jnp.zeros((z.FROWS, FILT), F32)
        s.sc[l] = jnp.zeros((24 + FILT, C), F32)
        gn2 = ff_backward(l)
        ffc = ff_grads(l)
        gv, gg_row, gb_row = ln_back(s.mids[l], gn2, s.ln2g[l])
        s.sa[l, 2:3, :] = gg_row
        s.sa[l, 3:4, :] = gb_row
        gm = s.gx[...] + gv
        s.gx[...] = gm
        go = gm.astype(BF16)
        s.sa[l, 4:5, :] = jnp.sum(go.astype(F32), axis=0, keepdims=True)
        s.goF[l, ti] = go
        for c in gather_z(s.goF, l):
            done(c)

        @pl.loop(0, n)
        def _(j):
            s.gtp[pl.ds(pl.multiple_of(j * R, R), R), :] = dot_nt(s.goF[l, j], s.w_out[l])

        mixer_backward(l)

        @pl.loop(0, n)
        def _(j):
            rows = pl.ds(pl.multiple_of(j * R, R), R)
            acc = dot_nt(s.gpj[0, rows, :], s.w_in[l, 0])
            acc = acc + dot_nt(s.gpj[1, rows, :], s.w_in[l, 1])
            acc = acc + dot_nt(s.gpj[2, rows, :], s.w_in[l, 2])
            s.zp[j] = acc.astype(BF16)

        rs = scatter_z(l)
        ffz = ff_second(l, ffc)
        wc = weight_grads(l)
        filter_backward(l)
        gn = sum_z(l, rs)
        gv, gg_row, gb_row = ln_back(layer_input(l), gn, s.ln1g[l])
        s.sa[l, 0:1, :] = gg_row
        s.sa[l, 1:2, :] = gb_row
        s.gx[...] = s.gx[...] + gv
        if l == 0:
            s.gin[...] = s.gx[...]
        ff_last(l, ffz)
        weight_last(l, wc)
        small_sums(l)
        flush()

    nxt = None
    for l in range(L):
        nxt = forward_layer(l, nxt)
    s.gx[...] = s.cot[...]
    for l in reversed(range(L)):
        backward_layer(l)


def fused_local(z, *args):
    (inputs, cotangent, lengths, ln1_gain, ln1_bias, w_in, b_in, conv_weight, conv_bias, filt_w1,
     filt_b1, filt_w2, filt_b2, filt_freq, filt_w3, decay_rate, skip_gain, w_out, b_out, ln2_gain,
     ln2_bias, w_up, b_up, w_down, b_down) = args
    L, D, C, T, FFs, FFp, FILT = z.L, z.D, z.C, z.T, z.FFs, z.FFp, z.FILT
    pad = ((0, 0), (0, FFp - FFs), (0, 0))
    ff = jnp.concatenate(
        [
            jnp.pad(jnp.swapaxes(w_up, 1, 2), pad),
            jnp.pad(w_down, pad),
            jnp.pad(b_up[:, None, :], ((0, 0), (0, 15), (0, D - FFs))),
        ],
        axis=1,
    )
    lag = np.arange(T) / T
    bands = np.arange(1, z.EMB // 2 + 1)
    phases = 2.0 * math.pi * lag[:, None] * bands[None, :]
    emb = np.concatenate([lag[:, None], np.cos(phases), np.sin(phases)], axis=1)
    emb = np.pad(emb, ((0, 0), (0, z.EP - z.EMB))).astype(np.float32)
    turn = (np.arange(T) * 2 + 1)[:, None] * np.arange(T)[None, :] % (4 * T)
    turn = turn * (math.pi / (2 * T))
    table = np.stack([np.cos(turn), np.sin(turn)])
    dft = table.astype(jnp.bfloat16)
    dftt = np.ascontiguousarray(np.swapaxes(table, 1, 2)).astype(jnp.bfloat16)
    row = lambda v: v[:, None, :]
    values = (
        inputs, cotangent, lengths, row(ln1_gain), row(ln1_bias), jnp.swapaxes(w_in, 1, 2), b_in,
        conv_weight.reshape(L, 9, C), conv_bias, jnp.asarray(emb),
        jnp.pad(filt_w1, ((0, 0), (0, z.EP - z.EMB), (0, 0))), row(filt_b1), filt_w2,
        row(filt_b2), filt_freq, filt_w3, row(decay_rate), row(skip_gain), w_out, row(b_out),
        row(ln2_gain), row(ln2_bias), ff, row(b_down), jnp.asarray(dft), jnp.asarray(dftt),
    )
    shapes, sems, _, _ = scratch_shapes(z)
    names = INPUTS + OUTPUTS + tuple(shapes) + ("ssem", "rsem")
    outs = (
        jax.ShapeDtypeStruct((z.R, D), F32),
        jax.ShapeDtypeStruct((z.R, D), F32),
        jax.ShapeDtypeStruct((L, z.FR, D), F32),
        jax.ShapeDtypeStruct((L, 4, z.DB, C), F32),
        jax.ShapeDtypeStruct((L, 8, D), F32),
        jax.ShapeDtypeStruct((L, z.FROWS, FILT), F32),
        jax.ShapeDtypeStruct((L, 24 + FILT, C), F32),
    )
    vmem = pl.BlockSpec(memory_space=pltpu.VMEM)
    specs = [
        pl.BlockSpec(memory_space=pltpu.SMEM) if name == "lens" else vmem for name in INPUTS
    ]
    out, gin, ffo, wo, sa, sf, sc = pl.pallas_call(
        functools.partial(fused_kernel, z, names),
        out_shape=outs,
        in_specs=specs,
        out_specs=[vmem] * len(outs),
        scratch_shapes=[pltpu.VMEM(*spec) for spec in shapes.values()]
        + [pltpu.SemaphoreType.DMA((sems,)), pltpu.SemaphoreType.DMA((sems,))],
        compiler_params=pltpu.CompilerParams(
            collective_id=0, has_side_effects=True, vmem_limit_bytes=VMEM_LIMIT
        ),
        name="hyena_layers",
    )(*values)
    at = z.EP + FILT
    return (
        out,
        gin,
        sa[:, 0],
        sa[:, 1],
        jnp.swapaxes(wo[:, :3], 1, 2),
        sc[:, 0:3],
        sc[:, 3:12].reshape(L, 3, 3, C),
        sc[:, 12:15],
        sf[:, : z.EMB],
        sf[:, at],
        sf[:, z.EP : z.EP + FILT],
        sf[:, at + 1],
        sf[:, at + 2 : at + 4],
        sc[:, 24:],
        sc[:, 15],
        sc[:, 16],
        jnp.swapaxes(wo[:, 3], 1, 2),
        sa[:, 4],
        sa[:, 2],
        sa[:, 3],
        jnp.swapaxes(ffo[:, :FFs], 1, 2),
        ffo[:, 2 * FFp, :FFs],
        ffo[:, FFp : FFp + FFs],
        sa[:, 5],
    )


VMEM_LIMIT = 63 * 1024 * 1024


def local_any(mesh, *args):
    z = Sizes(
        mesh.shape["dp"], mesh.shape["tensor"], args[0].shape[0], args[0].shape[1],
        args[5].shape[3], args[21].shape[2], args[2].shape[1], args[5].shape[0],
        args[9].shape[1], args[9].shape[2],
    )
    shapes, _, _, _ = scratch_shapes(z)
    small = vmem_bytes(shapes) < VMEM_LIMIT - 10 * 1024 * 1024
    if z.ndp % SHARE == 0 and z.ndp > SHARE and z.n > 1 and z.FB <= z.D and small:
        return fused_local(z, *args)
    return local(*args)


def solution(mesh):
    in_specs = (
        P(("dp", "tensor"), None),
        P(("dp", "tensor"), None),
        P("dp", None),
        P(),
        P(),
        P(None, None, None, "tensor"),
        P(None, None, "tensor"),
        P(None, None, None, "tensor"),
        P(None, None, "tensor"),
        P(),
        P(),
        P(),
        P(),
        P(),
        P(None, None, "tensor"),
        P(None, "tensor"),
        P(None, "tensor"),
        P(None, "tensor", None),
        P(),
        P(),
        P(),
        P(None, None, ("dp", "tensor")),
        P(None, ("dp", "tensor")),
        P(None, ("dp", "tensor"), None),
        P(),
    )
    out_specs = (
        P(("dp", "tensor"), None),
        P(("dp", "tensor"), None),
        P(),
        P(),
        P(None, "dp", None, "tensor"),
        P(None, None, "tensor"),
        P(None, None, None, "tensor"),
        P(None, None, "tensor"),
        P(),
        P(),
        P(),
        P(),
        P(),
        P(None, None, "tensor"),
        P(None, "tensor"),
        P(None, "tensor"),
        P(None, "tensor", "dp"),
        P(),
        P(),
        P(),
        P(None, None, ("dp", "tensor")),
        P(None, ("dp", "tensor")),
        P(None, ("dp", "tensor"), None),
        P(),
    )
    return jax.shard_map(functools.partial(local_any, mesh), mesh=mesh, in_specs=in_specs, out_specs=out_specs, check_vma=False)
```

```python
import functools
import math
import types

import jax
import jax.numpy as jnp
import numpy as np
from jax import lax
from jax.experimental import pallas as pl
from jax.experimental.pallas import tpu as pltpu
from jax.sharding import PartitionSpec as P

NORM_EPS = 1e-05
PRECISE = lax.Precision.HIGHEST


def layer_norm(values, norm_gain, norm_shift):
    center = values - jnp.mean(values, axis=-1, keepdims=True)
    spread = jnp.mean(center * center, axis=-1, keepdims=True)
    return center * lax.rsqrt(spread + NORM_EPS) * norm_gain + norm_shift


def filter_taps(w_first, b_first, w_second, b_second, freq_pair, w_third, decay_row, length):
    lag_pos = jnp.arange(length).astype(jnp.float32)
    fraction = lag_pos / length
    band_ids = jnp.arange(1, w_first.shape[0] // 2 + 1).astype(jnp.float32)
    phases = 2.0 * math.pi * fraction[:, None] * band_ids[None, :]
    embedding = jnp.concatenate([fraction[:, None], jnp.cos(phases), jnp.sin(phases)], axis=1)
    layer_one = jnp.sin(freq_pair[0] * (jnp.dot(embedding, w_first, precision=PRECISE) + b_first))
    layer_two = jnp.sin(freq_pair[1] * (jnp.dot(layer_one, w_second, precision=PRECISE) + b_second))
    return jnp.dot(layer_two, w_third, precision=PRECISE) * jnp.exp(
        -lag_pos[:, None] * decay_row[None, :]
    )


def segment_ids(lens_row, length):
    places = jnp.arange(length)
    ends = jnp.cumsum(lens_row)
    return jnp.sum((places[:, None] >= ends[None, :-1]).astype(jnp.int32), axis=1)


def short_conv(projected, weight_short, bias_short, seg_ids):
    summed = bias_short[None] + weight_short[0][None] * projected
    for offset in (1, 2):
        shifted = jnp.concatenate(
            [jnp.zeros((offset,) + projected.shape[1:], jnp.float32), projected[:-offset]], axis=0
        )
        earlier = jnp.concatenate([jnp.full((offset,), -1, jnp.int32), seg_ids[:-offset]], axis=0)
        within = (earlier == seg_ids).astype(jnp.float32)
        summed = summed + weight_short[offset][None] * shifted * within[:, None, None]
    return summed


def trig_table(count_rows, count_cols, modulus):
    product = jnp.arange(count_rows)[:, None] * jnp.arange(count_cols)[None, :] % modulus
    phases = product.astype(jnp.float32) * (2.0 * math.pi / modulus)
    return (jnp.cos(phases), jnp.sin(phases))


def forward_dft(signal, tables):
    cos_a, sin_a, cos_t, sin_t, cos_b, sin_b = tables
    shaped = signal.reshape(cos_a.shape[0], cos_b.shape[0], signal.shape[1])
    real_one = jnp.einsum("abc,ak->kbc", shaped, cos_a, precision=PRECISE)
    imag_one = -jnp.einsum("abc,ak->kbc", shaped, sin_a, precision=PRECISE)
    turn_re = cos_t[:, :, None]
    turn_im = sin_t[:, :, None]
    real_two = real_one * turn_re + imag_one * turn_im
    imag_two = imag_one * turn_re - real_one * turn_im
    real_out = jnp.einsum("kbc,bj->kjc", real_two, cos_b, precision=PRECISE) + jnp.einsum(
        "kbc,bj->kjc", imag_two, sin_b, precision=PRECISE
    )
    imag_out = jnp.einsum("kbc,bj->kjc", imag_two, cos_b, precision=PRECISE) - jnp.einsum(
        "kbc,bj->kjc", real_two, sin_b, precision=PRECISE
    )
    return (real_out, imag_out)


def inverse_dft(real_in, imag_in, tables):
    cos_a, sin_a, cos_t, sin_t, cos_b, sin_b = tables
    real_one = jnp.einsum("kjc,bj->kbc", real_in, cos_b, precision=PRECISE) - jnp.einsum(
        "kjc,bj->kbc", imag_in, sin_b, precision=PRECISE
    )
    imag_one = jnp.einsum("kjc,bj->kbc", imag_in, cos_b, precision=PRECISE) + jnp.einsum(
        "kjc,bj->kbc", real_in, sin_b, precision=PRECISE
    )
    turn_re = cos_t[:, :, None]
    turn_im = sin_t[:, :, None]
    real_two = real_one * turn_re - imag_one * turn_im
    imag_two = imag_one * turn_re + real_one * turn_im
    shaped = jnp.einsum("kbc,ak->abc", real_two, cos_a, precision=PRECISE) - jnp.einsum(
        "kbc,ak->abc", imag_two, sin_a, precision=PRECISE
    )
    total_len = 2 * shaped.shape[0] * shaped.shape[1]
    return shaped.reshape(shaped.shape[0] * shaped.shape[1], shaped.shape[2]) / total_len


def local(
    inputs,
    cotangent,
    lengths,
    ln1_gain,
    ln1_bias,
    w_in,
    b_in,
    conv_weight,
    conv_bias,
    filt_w1,
    filt_b1,
    filt_w2,
    filt_b2,
    filt_freq,
    filt_w3,
    decay_rate,
    skip_gain,
    w_out,
    b_out,
    ln2_gain,
    ln2_bias,
    w_up,
    b_up,
    w_down,
    b_down,
):
    rows_dev = inputs.shape[0]
    tensor_size = lax.axis_size("tensor")
    group_len = rows_dev * tensor_size
    layer_count = w_in.shape[0]
    seg_ids = segment_ids(lengths[0], group_len)
    masks_seq = tuple(
        ((seg_ids == seq_pos).astype(jnp.float32) for seq_pos in range(lengths.shape[1]))
    )
    full_len = 2 * group_len
    fold_a = math.gcd(full_len, 128)
    fold_b = full_len // fold_a
    cos_a, sin_a = trig_table(fold_a // 2, fold_a, fold_a)
    cos_t, sin_t = trig_table(fold_a, fold_b, full_len)
    cos_b, sin_b = trig_table(fold_b, fold_b, fold_b)
    tables = (cos_a, sin_a, cos_t, sin_t, cos_b, sin_b)

    def mixer_local(
        projected,
        weight_short,
        bias_short,
        fw_one,
        fb_one,
        fw_two,
        fb_two,
        freq_pair,
        fw_three,
        decay_row,
        skip_row,
    ):
        gated = short_conv(projected, weight_short, bias_short, seg_ids)
        taps_long = filter_taps(
            fw_one, fb_one, fw_two, fb_two, freq_pair, fw_three, decay_row, group_len
        )
        filt_re, filt_im = forward_dft(taps_long, tables)
        mixed_in = gated[:, 2] * gated[:, 1]
        result = skip_row * mixed_in
        for mask_one in masks_seq:
            sig_re, sig_im = forward_dft(mixed_in * mask_one[:, None], tables)
            result = result + mask_one[:, None] * inverse_dft(
                sig_re * filt_re - sig_im * filt_im, sig_re * filt_im + sig_im * filt_re, tables
            )
        return result * gated[:, 0]

    kept_list = []
    current = inputs
    for layer_idx in range(layer_count):
        normed, norm_back = jax.vjp(layer_norm, current, ln1_gain[layer_idx], ln1_bias[layer_idx])
        normed_full = lax.all_gather(normed.astype(jnp.bfloat16), "tensor", axis=0, tiled=True)
        projected = (
            jnp.einsum(
                "td,dkc->tkc", normed_full, w_in[layer_idx], preferred_element_type=jnp.float32
            )
            + b_in[layer_idx]
        )
        mixer_val, mixer_back = jax.vjp(
            mixer_local,
            projected,
            conv_weight[layer_idx],
            conv_bias[layer_idx],
            filt_w1[layer_idx],
            filt_b1[layer_idx],
            filt_w2[layer_idx],
            filt_b2[layer_idx],
            filt_freq[layer_idx],
            filt_w3[layer_idx],
            decay_rate[layer_idx],
            skip_gain[layer_idx],
        )
        mixer_low = mixer_val.astype(jnp.bfloat16)
        weight_out = w_out[layer_idx]
        keep_out = lax.all_to_all(mixer_low, "tensor", split_axis=0, concat_axis=1, tiled=True)
        weight_out = lax.all_gather(weight_out, "tensor", axis=0, tiled=True)
        branch_out = jnp.dot(keep_out, weight_out, preferred_element_type=jnp.float32)
        middle = current + branch_out + b_out[layer_idx]
        normed_two, norm_two_back = jax.vjp(
            layer_norm, middle, ln2_gain[layer_idx], ln2_bias[layer_idx]
        )
        normed_two_low = normed_two.astype(jnp.bfloat16)
        up_full, upb_full, down_full = (
            lax.all_gather(w_up[layer_idx], ("dp", "tensor"), axis=1, tiled=True),
            lax.all_gather(b_up[layer_idx], ("dp", "tensor"), axis=0, tiled=True),
            lax.all_gather(w_down[layer_idx], ("dp", "tensor"), axis=0, tiled=True),
        )
        hidden_pre = jnp.dot(
            normed_two_low, up_full, preferred_element_type=jnp.float32
        ) + upb_full.astype(jnp.float32)
        hidden_act, gelu_back = jax.vjp(jax.nn.gelu, hidden_pre)
        hidden_low = hidden_act.astype(jnp.bfloat16)
        current = (
            middle
            + jnp.dot(hidden_low, down_full, preferred_element_type=jnp.float32)
            + b_down[layer_idx]
        )
        kept_list.append(
            (
                norm_back,
                normed_full,
                mixer_back,
                keep_out,
                weight_out,
                norm_two_back,
                normed_two_low,
                None,
                None,
                hidden_low,
                gelu_back,
            )
        )
    grad_rows = cotangent
    per_layer = [None] * layer_count
    for layer_idx in reversed(range(layer_count)):
        (
            norm_back,
            normed_full,
            mixer_back,
            keep_out,
            weight_out,
            norm_two_back,
            normed_two_low,
            up_full,
            down_full,
            hidden_low,
            gelu_back,
        ) = kept_list[layer_idx]
        up_full, down_full = (
            lax.all_gather(w_up[layer_idx], ("dp", "tensor"), axis=1, tiled=True),
            lax.all_gather(w_down[layer_idx], ("dp", "tensor"), axis=0, tiled=True),
        )
        down_low = grad_rows.astype(jnp.bfloat16)
        grad_b_down = jnp.sum(down_low.astype(jnp.float32), axis=0)
        grad_w_down = jnp.einsum(
            "tf,td->fd", hidden_low, down_low, preferred_element_type=jnp.float32
        )
        grad_hidden = jnp.einsum(
            "td,fd->tf", down_low, down_full, preferred_element_type=jnp.float32
        )
        (grad_pre,) = gelu_back(grad_hidden)
        pre_low = grad_pre.astype(jnp.bfloat16)
        grad_w_up = jnp.einsum(
            "td,tf->df", normed_two_low, pre_low, preferred_element_type=jnp.float32
        )
        grad_b_up = jnp.sum(pre_low.astype(jnp.float32), axis=0)
        grad_normed_two = jnp.einsum(
            "tf,df->td", pre_low, up_full, preferred_element_type=jnp.float32
        )
        shard_w_up, shard_b_up, shard_w_down = (
            lax.psum_scatter(grad_w_up, ("dp", "tensor"), scatter_dimension=1, tiled=True),
            lax.psum_scatter(grad_b_up, ("dp", "tensor"), scatter_dimension=0, tiled=True),
            lax.psum_scatter(grad_w_down, ("dp", "tensor"), scatter_dimension=0, tiled=True),
        )
        grad_middle_ln, grad_ln2_gain, grad_ln2_bias = norm_two_back(grad_normed_two)
        grad_middle = grad_rows + grad_middle_ln
        out_low = grad_middle.astype(jnp.bfloat16)
        grad_b_out = jnp.sum(out_low.astype(jnp.float32), axis=0)
        grad_rows_mixed = jnp.einsum(
            "td,cd->tc", out_low, weight_out, preferred_element_type=jnp.float32
        )
        grad_mixed = lax.all_to_all(
            grad_rows_mixed.astype(jnp.bfloat16), "tensor", split_axis=1, concat_axis=0, tiled=True
        ).astype(grad_rows_mixed.dtype)
        grad_w_out = lax.psum_scatter(
            jnp.einsum("tc,td->cd", keep_out, out_low, preferred_element_type=jnp.float32).astype(
                jnp.bfloat16
            ),
            "tensor",
            scatter_dimension=0,
            tiled=True,
        ).astype(jnp.float32)
        grads_mixer = mixer_back(grad_mixed)
        proj_low = grads_mixer[0].astype(jnp.bfloat16)
        grad_w_in = jnp.einsum(
            "td,tkc->dkc", normed_full, proj_low, preferred_element_type=jnp.float32
        )
        grad_b_in = jnp.sum(proj_low.astype(jnp.float32), axis=0)
        weight_in = w_in[layer_idx]
        grad_normed = lax.psum_scatter(
            jnp.einsum(
                "tkc,dkc->td", proj_low, weight_in, preferred_element_type=jnp.float32
            ).astype(jnp.bfloat16),
            "tensor",
            scatter_dimension=0,
            tiled=True,
        ).astype(jnp.float32)
        grad_in_ln, grad_ln1_gain, grad_ln1_bias = norm_back(grad_normed)
        grad_rows = grad_middle + grad_in_ln
        per_layer[layer_idx] = (
            grad_ln1_gain,
            grad_ln1_bias,
            grad_w_in,
            grad_b_in,
            grads_mixer[1],
            grads_mixer[2],
            grads_mixer[3],
            grads_mixer[4],
            grads_mixer[5],
            grads_mixer[6],
            grads_mixer[7],
            grads_mixer[8],
            grads_mixer[9],
            grads_mixer[10],
            grad_w_out,
            grad_b_out,
            grad_ln2_gain,
            grad_ln2_bias,
            shard_w_up,
            shard_b_up,
            shard_w_down,
            grad_b_down,
        )
    stacks = [
        jnp.stack([per_layer[layer_pos][slot_pos] for layer_pos in range(layer_count)])
        for slot_pos in range(22)
    ]
    shared_done = lax.psum(
        (
            stacks[0],
            stacks[1],
            stacks[6],
            stacks[7],
            stacks[8],
            stacks[9],
            stacks[10],
            stacks[15],
            stacks[16],
            stacks[17],
            stacks[21],
        ),
        ("dp", "tensor"),
    )
    weight_done = (
        lax.psum_scatter(
            stacks[2].astype(jnp.bfloat16), "dp", scatter_dimension=1, tiled=True
        ).astype(jnp.float32),
        lax.psum_scatter(
            stacks[14].astype(jnp.bfloat16), "dp", scatter_dimension=2, tiled=True
        ).astype(jnp.float32),
    )
    group_done = (
        lax.psum(stacks[3].astype(jnp.bfloat16), "dp").astype(jnp.float32),
        lax.psum(stacks[4].astype(jnp.bfloat16), "dp").astype(jnp.float32),
        lax.psum(stacks[5].astype(jnp.bfloat16), "dp").astype(jnp.float32),
        lax.psum(stacks[11].astype(jnp.bfloat16), "dp").astype(jnp.float32),
        lax.psum(stacks[12].astype(jnp.bfloat16), "dp").astype(jnp.float32),
        lax.psum(stacks[13].astype(jnp.bfloat16), "dp").astype(jnp.float32),
    )
    return (
        current,
        grad_rows,
        shared_done[0],
        shared_done[1],
        weight_done[0],
        group_done[0],
        group_done[1],
        group_done[2],
        shared_done[2],
        shared_done[3],
        shared_done[4],
        shared_done[5],
        shared_done[6],
        group_done[3],
        group_done[4],
        group_done[5],
        weight_done[1],
        shared_done[7],
        shared_done[8],
        shared_done[9],
        stacks[18],
        stacks[19],
        stacks[20],
        shared_done[10],
    )


BF16 = jnp.bfloat16
F32 = jnp.float32
MESH = pl.DeviceIdType.MESH
SHARE = 4
GELU_C = math.sqrt(2.0 / math.pi)
GELU_A = 0.044715
VMEM_LIMIT = 63 * 1024 * 1024
ROW_DECAY, ROW_SKIP, ROW_ENDS, ROW_W3 = 15, 16, 17, 24


def dot_nn(a, b, precision=None):
    return lax.dot_general(
        a, b, (((1,), (0,)), ((), ())), precision=precision, preferred_element_type=F32
    )


def dot_nt(a, b, precision=None):
    return lax.dot_general(
        a, b, (((1,), (1,)), ((), ())), precision=precision, preferred_element_type=F32
    )


def dot_tn(a, b, precision=None):
    return lax.dot_general(
        a, b, (((0,), (0,)), ((), ())), precision=precision, preferred_element_type=F32
    )


class Sizes:
    def __init__(self, mesh_dp, mesh_tp, rows, width, chan, shard, slots, layers, emb, filt):
        self.ndp, self.n = mesh_dp, mesh_tp
        self.R, self.D, self.C = rows, width, chan
        self.T = rows * mesh_tp
        self.FFs = shard
        self.FR = 2 * shard + 16
        self.Y = mesh_dp // SHARE
        self.FB = mesh_tp * shard
        self.SL, self.L = slots, layers
        self.EMB, self.FILT = emb, filt
        self.EP = -(-emb // 8) * 8
        self.DB = width // mesh_dp
        self.DP = 4 * chan // mesh_dp
        self.PK = mesh_dp // 4
        self.TL = rows // 2
        self.FROWS = self.EP + filt + 8
        self.CROWS = ROW_W3 + filt

    def fits(self):
        return (
            self.n == SHARE
            and self.ndp == 2 * SHARE
            and self.FFs % 16 == 0
            and self.DP % 16 == 0
            and self.FB <= self.D
            and self.SL <= 8
            and vmem_bytes(scratch_shapes(self)[0]) < VMEM_LIMIT - 6 * 1024 * 1024
        )


INPUTS = (
    "x", "cot", "lens", "ln1g", "ln1b", "w_in", "b_in", "cw", "cb", "emb", "fw1", "fb1", "fw2",
    "fb2", "freq", "fw3", "decay", "skip", "w_out", "b_out", "ln2g", "ln2b", "w_up", "b_up",
    "w_down", "b_down", "dft", "dftt",
)
OUTPUTS = ("out", "gin", "ffo", "wo", "sa", "sf", "sc")


def scratch_shapes(z):
    R, D, C, T, n, L, Y = z.R, z.D, z.C, z.T, z.n, z.L, z.Y
    steps_dp = z.ndp.bit_length() - 1
    steps = steps_dp + n.bit_length() - 1
    per = 2 * (n - 1) + 2 * (z.ndp - 1) + 24 + n * Y + n * (Y - 1) + (n - 1) + 3 * (n - 1)
    sems = L * (per + 3 * steps + 2) + 8
    shapes = dict(
        xb=((R, D), BF16),
        xv=((R, D), BF16),
        cv=((R, D), BF16),
        ov=((R, D), BF16),
        gv=((R, D), BF16),
        xs=((max(L - 1, 1), R, D), F32),
        mids=((L, R, D), F32),
        gx=((R, D), F32),
        nF=((L, n, R, D), BF16),
        p=((L, 3, T + 8, C), F32),
        inn=((L, T, C), F32),
        innb=((T, C), BF16),
        g0s=((T, C), F32),
        z12=((L, 2, T, z.FILT), F32),
        fw1p=((z.EP, z.FILT), F32),
        taps=((L, T, C), F32),
        hs=((L, 2, T, C), F32),
        xf=((L, 2, T, C), BF16),
        yb=((2, T, C), BF16),
        qb=((2, T, C), BF16),
        longs=((L, T, C), F32),
        mx=((L, T, C), BF16),
        pin=((L, z.CROWS, C), F32),
        pv=((L, z.CROWS, C), F32),
        wz=((L, n, z.DP, D), BF16),
        wfull=((L, z.ndp, z.DP, D), BF16),
        n2S=((L, SHARE, R, D), BF16),
        rowb=((16, D), F32),
        ffw=((L, Y, n, z.FR, D), BF16),
        bup=((L, Y, 8, z.FB), F32),
        hp=((L, Y, SHARE * R, z.FB), BF16),
        sp=((3, R, D), BF16),
        sr=((3, R, D), BF16),
        gdS=((L, SHARE, R, D), BF16),
        hb=((Y, SHARE * R, z.FB), BF16),
        gpb=((Y, SHARE * R, z.FB), BF16),
        ffg=((Y, n, z.FR, D), BF16),
        ffry=((L, Y - 1, n, z.FR, D), BF16),
        ffrz=((L, n - 1, z.FR, D), BF16),
        goF=((n, R, D), BF16),
        gg=((3, T + 8, C), F32),
        gpj=((3, T, C), BF16),
        gl=((T, C), F32),
        gtp=((T, C), F32),
        gtt=((z.TL, C), F32),
        wg=((z.ndp, 4, z.DB, C), BF16),
        wr=((L, Y - 1, SHARE, 4, z.DB, C), BF16),
        wr1=((L, SHARE, 4, z.DB, C), BF16),
        wr2=((L, n - 1, 4, z.DB, C), BF16),
        sc0=((L, z.CROWS, C), F32),
        rA=((L, steps, 8, D), F32),
        rF=((L, steps, z.FROWS, z.FILT), F32),
        rC=((L, steps_dp, z.CROWS, C), F32),
    )
    return shapes, sems, steps_dp, steps


def vmem_bytes(shapes):
    total = 0
    for dims, kind in shapes.values():
        size = 2 if kind == BF16 else 4
        sub = 32 // size
        lanes = -(-dims[-1] // 128) * 128
        rows = -(-dims[-2] // sub) * sub
        total += math.prod(dims[:-2]) * rows * lanes * size
    return total


def fused_kernel(z, names, *refs):
    R, D, C, T, n, L, Y, ndp = z.R, z.D, z.C, z.T, z.n, z.L, z.Y, z.ndp
    FFs, FB, FILT, EP, DB, TL = z.FFs, z.FB, z.FILT, z.EP, z.DB, z.TL
    s = types.SimpleNamespace(**dict(zip(names, refs)))
    dp = lax.axis_index("dp")
    ti = lax.axis_index("tensor")
    y = dp // SHARE
    a = dp % SHARE
    sib = (dp + 1 - 2 * (dp % 2), ti)
    xnb = (dp + 2 - 4 * ((dp // 2) % 2), ti)
    partner = (SHARE * y + ti, a)
    moved = a != ti
    member = [a, a + 1 - 2 * (a % 2), a + 2 - 4 * (a // 2)]
    member.append(member[1] + 2 - 4 * (member[1] // 2))
    used = [0]
    open_sends = []

    def make(src, dst, dev):
        idx = used[0]
        used[0] += 1
        return pltpu.make_async_remote_copy(
            src_ref=src, dst_ref=dst, send_sem=s.ssem.at[idx], recv_sem=s.rsem.at[idx],
            device_id=dev, device_id_type=MESH,
        )

    def push(src, dst, dev, valid=True):
        copy = make(src, dst, dev)
        if valid is True:
            copy.start()
        else:
            pl.when(valid)(copy.start)
        open_sends.append((copy, valid))
        return copy

    def sent(*copies):
        for item in [p for p in open_sends if any(p[0] is c for c in copies)]:
            if item[1] is True:
                item[0].wait_send()
            else:
                pl.when(item[1])(item[0].wait_send)
        open_sends[:] = [p for p in open_sends if not any(p[0] is c for c in copies)]

    def swap(src, dst):
        copy = make(src, dst, partner)
        pl.when(moved)(copy.start)

        @pl.when(a == ti)
        def _():
            dst[...] = src[...]

        open_sends.append((copy, moved))
        return copy

    def swapped(copy):
        pl.when(moved)(copy.wait_recv)

    def flush():
        sent(*[p[0] for p in open_sends])

    def done(copy):
        copy.wait_recv()

    def piece_copy(l, act):
        k = dp // z.PK
        rows = pl.ds(pl.multiple_of((dp % z.PK) * z.DP, z.DP), z.DP)
        dst = s.wz.at[l, ti]

        @pl.when(k < 3)
        def _():
            getattr(pltpu.make_async_copy(s.w_in.at[l, k, rows], dst, s.lsem.at[l]), act)()

        @pl.when(k >= 3)
        def _():
            getattr(pltpu.make_async_copy(s.w_out.at[l, rows], dst, s.lsem.at[l]), act)()

    for l in range(L):
        piece_copy(l, "start")

    barrier = pltpu.get_barrier_semaphore()
    for d in range(1, ndp):
        pl.semaphore_signal(barrier, inc=1, device_id=((dp + d) % ndp, ti), device_id_type=MESH)
    for d in range(1, n):
        pl.semaphore_signal(barrier, inc=1, device_id=(dp, (ti + d) % n), device_id_type=MESH)

    @pl.when(moved)
    def _():
        pl.semaphore_signal(barrier, inc=1, device_id=partner, device_id_type=MESH)

    s.xb[...] = s.x[...].astype(BF16)

    @pl.when(moved)
    def _():
        pl.semaphore_wait(barrier, ndp - 1 + n)

    @pl.when(a == ti)
    def _():
        pl.semaphore_wait(barrier, ndp - 1 + n - 1)

    def ln_parts(v):
        mu = jnp.mean(v, axis=-1, keepdims=True)
        c = v - mu
        r = lax.rsqrt(jnp.mean(c * c, axis=-1, keepdims=True) + NORM_EPS)
        return c * r, r

    def ln_back(v, gy, gain):
        xhat, r = ln_parts(v)
        gz = gy * gain
        gv = r * (
            gz - jnp.mean(gz, axis=-1, keepdims=True)
            - xhat * jnp.mean(gz * xhat, axis=-1, keepdims=True)
        )
        return gv, jnp.sum(gy * xhat, axis=0, keepdims=True), jnp.sum(gy, axis=0, keepdims=True)

    def layer_input(l):
        return s.xv[...].astype(F32) if l == 0 else s.xs[l - 1]

    def gather_s(slot, overlap=None):
        mine = slot(member[0])
        to_x = push(mine, mine, xnb)
        to_sib = push(mine, mine, sib)
        if overlap:
            overlap()
        done(to_x)
        other = slot(member[2])
        onward = push(other, other, sib)
        done(to_sib)
        return to_x, to_sib, onward

    def scatter_s(block, overlap=None):
        s.sp[0] = block(member[3]).astype(BF16)
        c3 = push(s.sp.at[0], s.sr.at[1], sib)
        v2 = block(member[2])
        done(c3)
        s.sp[1] = (v2 + s.sr[1].astype(F32)).astype(BF16)
        cx = push(s.sp.at[1], s.sr.at[2], xnb)
        s.sp[2] = block(member[1]).astype(BF16)
        c1 = push(s.sp.at[2], s.sr.at[0], sib)
        v0 = block(member[0])
        if overlap:
            overlap()
        done(c1)
        done(cx)
        sent(c3, cx, c1)
        return v0 + s.sr[0].astype(F32) + s.sr[2].astype(F32)

    def y_peer(e):
        return (((y + e) % Y) * SHARE + a, ti)

    def w_gather(l):
        piece_copy(l, "wait")
        own = s.wz.at[l, ti]
        along_z = [push(own, own, (dp, (ti + d) % n)) for d in range(1, n)]
        yield
        for c in along_z:
            done(c)
        to_member = []
        for d in (2, 1, 3):
            m = (a + d) % SHARE
            to_member.append(push(s.wz.at[l, m], s.wfull.at[l, dp], (y * SHARE + m, ti)))
        s.wfull[l, dp] = s.wz[l, a]
        mine = s.wfull.at[l, dp]
        along_y = [push(mine, mine, y_peer(e)) for e in range(1, Y)]
        yield
        for c, d in zip(to_member, (2, 1, 3)):
            done(c)
            piece = s.wfull.at[l, y * SHARE + (a + SHARE - d) % SHARE]
            along_y += [push(piece, piece, y_peer(e)) for e in range(1, Y)]
        yield
        for c in along_y:
            done(c)
        yield

    def w_mat(l, k):
        return s.wfull[l, z.PK * k : z.PK * (k + 1)].reshape(C, D)

    def ff_gather(l):
        s.ffw[l, y, ti, 0:FFs, :] = s.w_up[l]
        s.ffw[l, y, ti, FFs : 2 * FFs, :] = s.w_down[l]
        s.rowb[...] = jnp.zeros((16, D), F32)
        s.rowb[0:1, 0:FFs] = s.b_up[...].astype(F32)[l : l + 1, :]
        s.ffw[l, y, ti, 2 * FFs : 2 * FFs + 16, :] = s.rowb[...].astype(BF16)
        along_y = []
        hop = None
        for h in range(n):
            low = (ti + n - h) % n
            high = (ti + h) % n
            has_low = ti >= h
            has_high = ti + h < n
            if h:
                pl.when(has_low)(hop[0].wait_recv)
                pl.when(has_high)(hop[1].wait_recv)
            lo, hi = s.ffw.at[l, y, low], s.ffw.at[l, y, high]
            if h < n - 1:
                hop = (
                    push(lo, lo, (dp, (ti + 1) % n), jnp.logical_and(has_low, ti < n - 1)),
                    push(hi, hi, (dp, (ti + n - 1) % n), jnp.logical_and(has_high, ti > 0)),
                )
            for e in range(1, Y):
                if h == 0:
                    along_y.append((push(lo, lo, y_peer(e)), True))
                else:
                    along_y.append((push(lo, lo, y_peer(e), has_low), has_low))
                    along_y.append((push(hi, hi, y_peer(e), has_high), has_high))
            yield
        for c, valid in along_y:
            if valid is True:
                done(c)
            else:
                pl.when(valid)(c.wait_recv)
        ff_ready(l)
        yield

    def ff_ready(l):
        for b in range(Y):
            row = jnp.zeros((16, D), F32)
            for j in range(n):
                part = s.ffw[l, b, j, 2 * FFs : 2 * FFs + 16, :].astype(F32)
                row = row + (pltpu.roll(part, FFs * j, 1) if j else part)
            s.bup[l, b] = row[:8, :FB]

    def ff_up(l, b):
        return s.ffw[l, b, :, 0:FFs, :].reshape(FB, D)

    def ff_down(l, b):
        return s.ffw[l, b, :, FFs : 2 * FFs, :].reshape(FB, D)

    CH = 64
    ENDS = range(z.SL - 1)

    def end_row(k):
        return s.pv[0, ROW_ENDS + k : ROW_ENDS + k + 1, :]

    def chunk_masks(r0, rows):
        t = (lax.broadcasted_iota(jnp.int32, (rows, C), 0) + r0).astype(F32)
        m1 = jnp.ones((rows, C), F32)
        for k in ENDS:
            m1 = jnp.where(t == end_row(k), 0.0, m1)
        m2 = m1
        for k in ENDS:
            m2 = jnp.where(t == end_row(k) + 1.0, 0.0, m2)
        return m1, m2

    def conv_row(l, step, k):
        return s.pv[l, 3 + step * 3 + k : 4 + step * 3 + k, :]

    def shifted(l, k, r0, m1, m2):
        blk = s.p[l, k, pl.ds(r0, CH + 8), :]
        return blk[8:], blk[7:-1] * m1, blk[6:-2] * m2

    def gate(l, k, parts):
        return (
            s.pv[l, 12 + k : 13 + k, :]
            + conv_row(l, 0, k) * parts[0]
            + conv_row(l, 1, k) * parts[1]
            + conv_row(l, 2, k) * parts[2]
        )

    def lag_rows():
        return lax.broadcasted_iota(jnp.int32, (T, C), 0).astype(F32)

    def decay_row(l):
        return s.pv[l, ROW_DECAY : ROW_DECAY + 1, :]

    def skip_row(l):
        return s.pv[l, ROW_SKIP : ROW_SKIP + 1, :]

    def filter_net(l):
        s.fw1p[...] = jnp.zeros((EP, FILT), F32)
        s.fw1p[0 : z.EMB, :] = s.fw1[l]
        z1 = dot_nn(s.emb[...], s.fw1p[...], PRECISE) + s.fb1[l : l + 1, :]
        s.z12[l, 0] = z1
        a1 = jnp.sin(s.freq[l, 0:1, :] * z1)
        s.z12[l, 1] = dot_nn(a1, s.fw2[l], PRECISE) + s.fb2[l : l + 1, :]

    def filter_taps_of(l):
        a2 = jnp.sin(s.freq[l, 1:2, :] * s.z12[l, 1])
        w3 = s.pv[l, ROW_W3 : ROW_W3 + FILT, :]
        tp = dot_nn(a2, w3, PRECISE) * jnp.exp(-lag_rows() * decay_row(l))
        s.taps[l] = tp
        s.innb[...] = tp.astype(BF16)

        @pl.loop(0, n)
        def _(i):
            rows = pl.ds(pl.multiple_of(i * R, R), R)
            s.hs[l, 0, rows, :] = dot_nn(s.dft[0, rows, :], s.innb[...])
            s.hs[l, 1, rows, :] = dot_nn(s.dft[1, rows, :], s.innb[...])

    def tail_index():
        return lax.broadcasted_iota(jnp.int32, (TL, C), 0).astype(F32)

    def tail_starts():
        t = tail_index() + float(T - TL)
        st = jnp.full((TL, C), float(T), F32)
        for k in ENDS:
            st = jnp.where(t >= end_row(k), end_row(k) - float(T - TL), st)
        return st

    def tail_ends():
        t = tail_index() + float(T - TL)
        en = jnp.full((TL, C), float(TL), F32)
        for k in reversed(ENDS[1:]):
            en = jnp.where(t < end_row(k), end_row(k) - float(T - TL), en)
        return jnp.where(t < end_row(0), -float(T), en)

    def project(l):
        for k in range(3):
            s.p[l, k, 0:8, :] = jnp.zeros((8, C), F32)

        @pl.loop(0, n)
        def _(j):
            rows = pl.ds(pl.multiple_of(j * R + 8, 8), R)
            for k in range(3):
                s.p[l, k, rows, :] = dot_nt(s.nF[l, j], w_mat(l, k)) + s.pv[l, k : k + 1, :]

    def mixer_forward(l):
        @pl.loop(0, T // CH)
        def _(i):
            r0 = pl.multiple_of(i * CH, CH)
            m1, m2 = chunk_masks(r0, CH)
            g0 = gate(l, 0, shifted(l, 0, r0, m1, m2))
            g1 = gate(l, 1, shifted(l, 1, r0, m1, m2))
            g2 = gate(l, 2, shifted(l, 2, r0, m1, m2))
            inner = g2 * g1
            s.g0s[pl.ds(r0, CH), :] = g0
            s.inn[l, pl.ds(r0, CH), :] = inner
            s.innb[pl.ds(r0, CH), :] = inner.astype(BF16)

        @pl.loop(0, n)
        def _(i):
            rows = pl.ds(pl.multiple_of(i * R, R), R)
            xr = dot_nn(s.dft[0, rows, :], s.innb[...])
            xi = dot_nn(s.dft[1, rows, :], s.innb[...])
            hr = s.hs[l, 0, rows, :]
            hi = s.hs[l, 1, rows, :]
            s.xf[l, 0, rows, :] = xr.astype(BF16)
            s.xf[l, 1, rows, :] = xi.astype(BF16)
            s.yb[0, rows, :] = (xr * hr - xi * hi).astype(BF16)
            s.yb[1, rows, :] = (xr * hi + xi * hr).astype(BF16)

        idx = tail_index()
        starts = tail_starts()

        def lag_step(d, carry):
            acc, cur = carry
            tap = s.taps[l, pl.ds(d, 1), :]
            acc = acc + jnp.where(idx - d.astype(F32) >= starts, cur, 0.0) * tap
            return acc, pltpu.roll(cur, 1, 0)

        tail, _ = lax.fori_loop(
            0, TL, lag_step, (jnp.zeros((TL, C), F32), s.inn[l, T - TL : T, :])
        )
        s.gtt[...] = tail

        @pl.loop(0, n)
        def _(i):
            rows = pl.ds(pl.multiple_of(i * R, R), R)
            s.longs[l, rows, :] = (
                dot_nn(s.dftt[0, rows, :], s.yb[0]) + dot_nn(s.dftt[1, rows, :], s.yb[1])
            ) * (1.0 / T)
        first = (tail_index() + float(T - TL)) < end_row(0)
        s.longs[l, T - TL : T, :] = jnp.where(first, s.longs[l, T - TL : T, :], s.gtt[...])

        @pl.loop(0, n)
        def _(i):
            rows = pl.ds(pl.multiple_of(i * R, R), R)
            lg = s.longs[l, rows, :] + skip_row(l) * s.inn[l, rows, :]
            s.longs[l, rows, :] = lg
            s.mx[l, rows, :] = (lg * s.g0s[rows, :]).astype(BF16)

    def block_rows(i):
        return pl.ds(pl.multiple_of(i * R, R), R)

    def gelu_tanh(v):
        return jnp.tanh(GELU_C * (v + GELU_A * v * v * v))

    def ff_backward(l, early, overlap):
        gd = s.gx[...].astype(BF16)
        s.gdS[l, a] = gd
        s.sa[l, 5:6, :] = jnp.sum(gd.astype(F32), axis=0, keepdims=True)
        last = gather_s(lambda i: s.gdS.at[l, i], early)
        done(last[2])

        def block(i):
            g = s.gdS[l, i]
            acc = jnp.zeros((R, D), F32)
            rows = block_rows(i)
            for b in range(Y):
                gh = dot_nt(g, ff_down(l, b))
                v = s.hp[l, b, rows, :].astype(F32)
                th = gelu_tanh(v)
                s.hb[b, rows, :] = (0.5 * v * (1.0 + th)).astype(BF16)
                slope = 0.5 * (1.0 + th) + 0.5 * v * (1.0 - th * th) * (
                    GELU_C * (1.0 + 3.0 * GELU_A * v * v)
                )
                gp = (gh * slope).astype(BF16)
                s.gpb[b, rows, :] = gp
                acc = acc + dot_nn(gp, ff_up(l, b))
            return acc

        return scatter_s(block, overlap)

    def ff_scatter(l):
        act = s.n2S[l].reshape(SHARE * R, D)
        gds = s.gdS[l].reshape(SHARE * R, D)

        def fill(b):
            g = s.gpb[b]
            h = s.hb[b]
            s.ffg[b, :, 0:FFs, :] = dot_tn(g, act).astype(BF16).reshape(n, FFs, D)
            s.ffg[b, :, FFs : 2 * FFs, :] = dot_tn(h, gds).astype(BF16).reshape(n, FFs, D)
            sums = jnp.sum(g.astype(F32), axis=0, keepdims=True)
            row = jnp.concatenate([sums, jnp.zeros((1, D - FB), F32)], axis=1) if D > FB else sums
            row = jnp.broadcast_to(row, (16, D))
            for j in range(n):
                part = pltpu.roll(row, (D - FFs * j) % D, 1) if j else row
                s.ffg[b, j, 2 * FFs : 2 * FFs + 16, :] = part.astype(BF16)

        along_y = []
        for e in range(1, Y):
            b = (y + e) % Y
            fill(b)
            for d in range(n):
                j = (ti + 1 + d) % n
                along_y.append(push(s.ffg.at[b, j], s.ffry.at[l, e - 1, j], y_peer(e)))
        fill(y)
        yield
        along_z = []
        for d in range(n):
            j = (ti + 1 + d) % n
            acc = s.ffg[y, j].astype(F32)
            for e in range(1, Y):
                done(along_y[(e - 1) * n + d])
                acc = acc + s.ffry[l, e - 1, j].astype(F32)
            if d < n - 1:
                s.ffg[y, j] = acc.astype(BF16)
                along_z.append(push(s.ffg.at[y, j], s.ffrz.at[l, d], (dp, j)))
            else:
                s.ffo[l] = acc
            yield
        for d in range(n - 1):
            done(along_z[d])
            s.ffo[l] = s.ffo[l] + s.ffrz[l, d].astype(F32)
        sent(*along_y, *along_z)
        yield

    def mixer_backward(l, ffs, ticks):
        @pl.loop(0, T // CH)
        def _(i):
            r0 = pl.multiple_of(i * CH, CH)
            rows = pl.ds(r0, CH)
            m1, m2 = chunk_masks(r0, CH)
            g0 = gate(l, 0, shifted(l, 0, r0, m1, m2))
            gm = s.gtp[rows, :]
            glong = gm * g0
            s.gg[0, rows, :] = gm * s.longs[l, rows, :]
            s.gl[rows, :] = glong
            t = (lax.broadcasted_iota(jnp.int32, (CH, C), 0) + r0).astype(F32)
            s.innb[rows, :] = jnp.where(t < end_row(0), glong, 0.0).astype(BF16)

        @pl.loop(0, n)
        def _(i):
            rows = pl.ds(pl.multiple_of(i * R, R), R)
            gr = dot_nn(s.dft[0, rows, :], s.innb[...])
            gi = dot_nn(s.dft[1, rows, :], s.innb[...])
            hr = s.hs[l, 0, rows, :]
            hi = s.hs[l, 1, rows, :]
            s.yb[0, rows, :] = (gr * hr + gi * hi).astype(BF16)
            s.yb[1, rows, :] = (gi * hr - gr * hi).astype(BF16)
            xr = s.xf[l, 0, rows, :].astype(F32)
            xi = s.xf[l, 1, rows, :].astype(F32)
            s.qb[0, rows, :] = (gr * xr + gi * xi).astype(BF16)
            s.qb[1, rows, :] = (gi * xr - gr * xi).astype(BF16)

        next(ffs)
        ticks[0]()
        idx = tail_index()
        stops = tail_ends()
        inner_tail = s.inn[l, T - TL : T, :]

        def lag_step(d, carry):
            acc, cur = carry
            live = jnp.where(idx + d.astype(F32) < stops, cur, 0.0)
            acc = acc + live * s.taps[l, pl.ds(d, 1), :]
            s.gtt[pl.ds(d, 1), :] = jnp.sum(live * inner_tail, axis=0, keepdims=True)
            return acc, pltpu.roll(cur, TL - 1, 0)

        tail, _ = lax.fori_loop(
            0, TL, lag_step, (jnp.zeros((TL, C), F32), s.gl[T - TL : T, :])
        )

        @pl.loop(0, n)
        def _(i):
            rows = pl.ds(pl.multiple_of(i * R, R), R)
            s.g0s[rows, :] = (
                dot_nn(s.dftt[0, rows, :], s.yb[0]) + dot_nn(s.dftt[1, rows, :], s.yb[1])
            ) * (1.0 / T)
            s.gtp[rows, :] = (
                dot_nn(s.dftt[0, rows, :], s.qb[0]) + dot_nn(s.dftt[1, rows, :], s.qb[1])
            ) * (1.0 / T)

        first = (tail_index() + float(T - TL)) < end_row(0)
        s.g0s[T - TL : T, :] = jnp.where(first, s.g0s[T - TL : T, :], tail)
        s.gtp[0:TL, :] = s.gtp[0:TL, :] + s.gtt[...]

        next(ffs)
        ticks[1]()

        def fold(v):
            return jnp.sum(v.reshape(CH // 8, 8, C), axis=0)

        for k in range(3):
            s.gg[k, T : T + 8, :] = jnp.zeros((8, C), F32)

        def gate_step(i, sums):
            r0 = pl.multiple_of(i * CH, CH)
            rows = pl.ds(r0, CH)
            m1, m2 = chunk_masks(r0, CH)
            parts = [shifted(l, k, r0, m1, m2) for k in range(3)]
            gl = s.gl[rows, :]
            ginner = s.g0s[rows, :] + skip_row(l) * gl
            gk = [s.gg[0, rows, :], ginner * gate(l, 2, parts[2]), ginner * gate(l, 1, parts[1])]
            s.gg[1, rows, :] = gk[1]
            s.gg[2, rows, :] = gk[2]
            new = []
            for step in range(3):
                for k in range(3):
                    new.append(sums[step * 3 + k] + fold(gk[k] * parts[k][step]))
            for k in range(3):
                new.append(sums[9 + k] + fold(gk[k]))
            new.append(sums[12] + fold(gl * s.inn[l, rows, :]))
            return tuple(new)

        sums = lax.fori_loop(
            0, T // CH, gate_step, tuple(jnp.zeros((8, C), F32) for _ in range(13))
        )
        for pos in range(12):
            s.sc0[l, 3 + pos : 4 + pos, :] = jnp.sum(sums[pos], axis=0, keepdims=True)
        s.sc0[l, ROW_SKIP : ROW_SKIP + 1, :] = jnp.sum(sums[12], axis=0, keepdims=True)

        next(ffs)
        ticks[2]()

        def proj_step(i, sums):
            r0 = pl.multiple_of(i * CH, CH)
            m1, m2 = chunk_masks(r0, CH + 8)
            new = []
            for k in range(3):
                blk = s.gg[k, pl.ds(r0, CH + 8), :]
                b1 = blk * m1
                b2 = blk * m2
                gp = (
                    conv_row(l, 0, k) * blk[0:CH]
                    + conv_row(l, 1, k) * b1[1 : CH + 1]
                    + conv_row(l, 2, k) * b2[2 : CH + 2]
                ).astype(BF16)
                s.gpj[k, pl.ds(r0, CH), :] = gp
                new.append(sums[k] + fold(gp.astype(F32)))
            return tuple(new)

        sums = lax.fori_loop(
            0, T // CH, proj_step, tuple(jnp.zeros((8, C), F32) for _ in range(3))
        )
        for k in range(3):
            s.sc0[l, k : k + 1, :] = jnp.sum(sums[k], axis=0, keepdims=True)

    def filter_backward(l):
        lag = lag_rows()
        gt = s.gtp[...]
        s.sc0[l, ROW_DECAY : ROW_DECAY + 1, :] = -jnp.sum(
            lag * gt * s.taps[l], axis=0, keepdims=True
        )
        gtr = gt * jnp.exp(-lag * decay_row(l))
        freq0 = s.freq[l, 0:1, :]
        freq1 = s.freq[l, 1:2, :]
        z1 = s.z12[l, 0]
        z2 = s.z12[l, 1]
        u2 = freq1 * z2
        s.sc0[l, ROW_W3 : ROW_W3 + FILT, :] = dot_tn(jnp.sin(u2), gtr, PRECISE)
        gu2 = dot_nt(gtr, s.pv[l, ROW_W3 : ROW_W3 + FILT, :], PRECISE) * jnp.cos(u2)
        gz2 = gu2 * freq1
        u1 = freq0 * z1
        s.sf[l, EP : EP + FILT, :] = dot_tn(jnp.sin(u1), gz2, PRECISE)
        gu1 = dot_nt(gz2, s.fw2[l], PRECISE) * jnp.cos(u1)
        gz1 = gu1 * freq0
        s.sf[l, 0:EP, :] = dot_tn(s.emb[...], gz1, PRECISE)
        row = EP + FILT
        s.sf[l, row : row + 1, :] = jnp.sum(gz1, axis=0, keepdims=True)
        s.sf[l, row + 1 : row + 2, :] = jnp.sum(gz2, axis=0, keepdims=True)
        s.sf[l, row + 2 : row + 3, :] = jnp.sum(gu1 * z1, axis=0, keepdims=True)
        s.sf[l, row + 3 : row + 4, :] = jnp.sum(gu2 * z2, axis=0, keepdims=True)

    def w_scatter(l):
        rows_all = s.nF[l].reshape(T, D)
        go_all = s.goF[...].reshape(T, D)
        for k in range(4):
            for h in range(0, D, 256):
                if k < 3:
                    g = dot_tn(rows_all[:, h : h + 256], s.gpj[k])
                else:
                    g = dot_tn(go_all[:, h : h + 256], s.mx[l])
                gb = g.astype(BF16)
                lo = h
                while lo < h + 256:
                    b = lo // DB
                    off = lo % DB
                    cnt = min(DB - off, h + 256 - lo)
                    s.wg[b, k, off : off + cnt, :] = gb[lo - h : lo - h + cnt]
                    lo += cnt
        along_y = []
        for e in range(1, Y):
            for d in (2, 3, 1, 0):
                j = ((y + e) % Y) * SHARE + (a + d) % SHARE
                along_y.append(push(s.wg.at[j], s.wr.at[l, e - 1, (a + d) % SHARE], y_peer(e)))
        yield
        to_member = []
        for pos, d in enumerate((2, 3, 1, 0)):
            m = (a + d) % SHARE
            acc = s.wg[y * SHARE + m].astype(F32)
            for e in range(1, Y):
                done(along_y[(e - 1) * SHARE + pos])
                acc = acc + s.wr[l, e - 1, m].astype(F32)
            if d:
                s.wg[y * SHARE + m] = acc.astype(BF16)
                to_member.append(
                    push(s.wg.at[y * SHARE + m], s.wr1.at[l, a], (y * SHARE + m, ti))
                )
            else:
                s.wr1[l, a] = acc.astype(BF16)
        yield
        for c in to_member:
            done(c)
        along_z = []
        for d in range(1, n):
            j = (ti + d) % n
            along_z.append(push(s.wr1.at[l, j], s.wr2.at[l, d - 1], (dp, j)))
        yield
        acc = s.wr1[l, ti].astype(F32)
        for d in range(1, n):
            done(along_z[d - 1])
            acc = acc + s.wr2[l, d - 1].astype(F32)
        s.wo[l] = acc
        sent(*along_y, *to_member, *along_z)
        yield

    def small_sums(l):
        first = swap(s.sc0.at[l], s.sc.at[l])
        yield
        swapped(first)
        sent(first)
        step = 0
        for size, count in ((ndp, 3), (n, 2)):
            bit = 1
            while bit < size:
                if count == 3:
                    peer = (dp + bit - 2 * bit * ((dp // bit) % 2), ti)
                else:
                    peer = (dp, ti + bit - 2 * bit * ((ti // bit) % 2))
                pairs = ((s.sa, s.rA), (s.sf, s.rF), (s.sc, s.rC))[:count]
                copies = [push(v.at[l], r.at[l, step], peer) for v, r in pairs]
                yield
                for c in copies:
                    done(c)
                sent(*copies)
                for v, r in pairs:
                    v[l] = v[l] + r[l, step]
                step += 1
                bit *= 2
        yield

    xc = swap(s.xb, s.xv)
    wgen = {0: w_gather(0)}
    next(wgen[0])
    for l in range(L):
        s.pin[l] = jnp.zeros((z.CROWS, C), F32)
        for k in range(3):
            s.pin[l, k : k + 1, :] = s.b_in[k, l : l + 1, :]
            s.pin[l, 12 + k : 13 + k, :] = s.cb[k, l : l + 1, :]
        for k in range(9):
            s.pin[l, 3 + k : 4 + k, :] = s.cw[k, l : l + 1, :]
        s.pin[l, ROW_DECAY : ROW_DECAY + 1, :] = s.decay[l : l + 1, :]
        s.pin[l, ROW_SKIP : ROW_SKIP + 1, :] = s.skip[l : l + 1, :]
        s.pin[l, ROW_W3 : ROW_W3 + FILT, :] = s.fw3[l]
    total = s.lens[0, 0]
    for k in ENDS:
        if k:
            total = total + s.lens[0, k]
        s.pin[0, ROW_ENDS + k : ROW_ENDS + k + 1, :] = jnp.full((1, C), total, jnp.int32).astype(F32)
    pc = swap(s.pin, s.pv)
    filter_net(0)
    swapped(xc)
    fgen = {l: ff_gather(l) for l in range(L)}
    wgen[1] = w_gather(1)
    cots = None

    def forward(l):
        x = layer_input(l)
        xhat, _ = ln_parts(x)
        s.nF[l, a] = (xhat * s.ln1g[l : l + 1, :] + s.ln1b[l : l + 1, :]).astype(BF16)

        def while_gather():
            if l == 0:
                next(wgen[0])
                next(fgen[0])

        last = gather_s(lambda i: s.nF.at[l, i], while_gather)
        if l == 0:
            next(wgen[0])
            swapped(pc)
            filter_taps_of(0)
            next(fgen[0])
        done(last[2])
        next(wgen[l])
        project(l)
        if l == 0:
            next(fgen[0])
        if l == 1:
            next(fgen[1])
        mixer_forward(l)
        if l == 0:
            next(fgen[0])
            next(wgen[1])
        if l == 1:
            next(fgen[1])

        def while_scatter():
            if l == 0:
                filter_net(1)

        res = scatter_s(lambda i: dot_nn(s.mx[l, block_rows(i), :], w_mat(l, 3)), while_scatter)
        mid = x + s.b_out[l : l + 1, :] + res
        s.mids[l] = mid
        xhat2, _ = ln_parts(mid)
        s.n2S[l, a] = (xhat2 * s.ln2g[l : l + 1, :] + s.ln2b[l : l + 1, :]).astype(BF16)

        def while_gather2():
            if l == 0:
                filter_taps_of(1)

        last = gather_s(lambda i: s.n2S.at[l, i], while_gather2)
        if l == 0:
            next(wgen[1])
            next(fgen[1])
        done(last[2])
        next(fgen[l])

        def block(i):
            v = s.n2S[l, i]
            acc = jnp.zeros((R, D), F32)
            for b in range(Y):
                pre = dot_nt(v, ff_up(l, b)) + s.bup[l, b, 0:1, :]
                s.hp[l, b, block_rows(i), :] = pre.astype(BF16)
                act = 0.5 * pre * (1.0 + gelu_tanh(pre))
                acc = acc + dot_nn(act.astype(BF16), ff_down(l, b))
            return acc

        def while_scatter2():
            if l == 0:
                next(wgen[1])
                next(fgen[1])

        res = scatter_s(block, while_scatter2)
        return s.mids[l] + s.b_down[l : l + 1, :] + res

    s.xs[0] = forward(0)
    sent(xc)
    s.xb[...] = s.cot[...].astype(BF16)
    cots = swap(s.xb, s.cv)
    s.ov[...] = forward(1).astype(BF16)
    swapped(cots)
    outs = swap(s.ov, s.gv)
    s.gx[...] = s.cv[...].astype(F32)

    def backward(l, ticks):
        s.sa[l] = jnp.zeros((8, D), F32)
        s.sf[l] = jnp.zeros((z.FROWS, FILT), F32)
        s.sc0[l] = jnp.zeros((z.CROWS, C), F32)
        ffs = ff_scatter(l)

        def while_back():
            ticks[1]()
            next(ffs)

        gn2 = ff_backward(l, ticks[0], while_back)
        gv, gain_row, bias_row = ln_back(s.mids[l], gn2, s.ln2g[l : l + 1, :])
        s.sa[l, 2:3, :] = gain_row
        s.sa[l, 3:4, :] = bias_row
        gm = s.gx[...] + gv
        s.gx[...] = gm
        go = gm.astype(BF16)
        s.sa[l, 4:5, :] = jnp.sum(go.astype(F32), axis=0, keepdims=True)
        s.goF[a] = go
        last = gather_s(lambda i: s.goF.at[i], ticks[2])
        done(last[2])
        sent(*last)

        @pl.loop(0, n)
        def _(j):
            s.gtp[block_rows(j), :] = dot_nt(s.goF[j], w_mat(l, 3))

        mixer_backward(l, ffs, ticks[3:7])

        def back_block(i):
            rows = block_rows(i)
            acc = dot_nn(s.gpj[0, rows, :], w_mat(l, 0))
            acc = acc + dot_nn(s.gpj[1, rows, :], w_mat(l, 1))
            return acc + dot_nn(s.gpj[2, rows, :], w_mat(l, 2))

        wsc = w_scatter(l)

        def while_back2():
            next(wsc)
            next(ffs)
            filter_backward(l)
            ticks[7]()

        gn = scatter_s(back_block, while_back2)
        gv, gain_row, bias_row = ln_back(layer_input(l), gn, s.ln1g[l : l + 1, :])
        s.sa[l, 0:1, :] = gain_row
        s.sa[l, 1:2, :] = bias_row
        s.gx[...] = s.gx[...] + gv
        return ffs, wsc

    nothing = [lambda: None] * 8
    ffs1, wsc1 = backward(1, nothing)
    small1 = small_sums(1)

    def run(*gens):
        def go():
            for g in gens:
                next(g)

        return go

    ffs0, wsc0 = backward(
        0,
        [
            run(small1),
            run(wsc1, small1, ffs1),
            run(wsc1, small1),
            run(small1),
            run(small1),
            run(small1, wsc1),
            lambda: None,
            run(small1),
        ],
    )
    small0 = small_sums(0)
    next(small0)
    sent(outs)
    s.ov[...] = s.gx[...].astype(BF16)
    gins = swap(s.ov, s.cv)
    swapped(outs)
    s.out[...] = s.gv[...].astype(F32)
    next(wsc0)
    next(small0)
    next(ffs0)
    next(small0)
    next(wsc0)
    for _ in range(3):
        next(small0)
    swapped(gins)
    s.gin[...] = s.cv[...].astype(F32)
    next(wsc0)
    next(small0)
    flush()


def finish_kernel(z, *refs):
    ffo, wo, sa, sf, sc = refs[:5]
    o = types.SimpleNamespace(**dict(zip(FINAL, refs[5:])))
    at = z.EP + z.FILT
    for l in range(z.L):
        row = slice(l, l + 1)
        for pos, ref in enumerate((o.ln1g, o.ln1b, o.ln2g, o.ln2b, o.b_out, o.b_down)):
            ref[row, :] = sa[l, pos : pos + 1, :]
        for k in range(3):
            o.w_in[l, k] = wo[l, k]
            o.b_in[k, row, :] = sc[l, k : k + 1, :]
            o.cb[k, row, :] = sc[l, 12 + k : 13 + k, :]
        for k in range(9):
            o.cw[k, row, :] = sc[l, 3 + k : 4 + k, :]
        o.w_out[l] = wo[l, 3].T
        for r in range(z.EMB):
            o.fw1[r, row, :] = sf[l, r : r + 1, :]
        o.fw2[l] = sf[l, z.EP : at, :]
        o.fb1[row, :] = sf[l, at : at + 1, :]
        o.fb2[row, :] = sf[l, at + 1 : at + 2, :]
        o.freq[l] = sf[l, at + 2 : at + 4, :]
        o.fw3[l] = sc[l, ROW_W3:, :]
        o.decay[row, :] = sc[l, ROW_DECAY : ROW_DECAY + 1, :]
        o.skip[row, :] = sc[l, ROW_SKIP : ROW_SKIP + 1, :]
        o.w_up[l] = ffo[l, 0 : z.FFs, :]
        o.w_down[l] = ffo[l, z.FFs : 2 * z.FFs, :]
        o.b_up[row, :] = ffo[l, 2 * z.FFs : 2 * z.FFs + 1, 0 : z.FFs]


FINAL = (
    "ln1g", "ln1b", "w_in", "b_in", "cw", "cb", "fw1", "fb1", "fw2", "fb2", "freq", "fw3",
    "decay", "skip", "w_out", "b_out", "ln2g", "ln2b", "w_up", "b_up", "w_down", "b_down",
)


def fused_local(z, *args):
    (inputs, cotangent, lengths, ln1_gain, ln1_bias, w_in, b_in, conv_weight, conv_bias, filt_w1,
     filt_b1, filt_w2, filt_b2, filt_freq, filt_w3, decay_rate, skip_gain, w_out, b_out, ln2_gain,
     ln2_bias, w_up, b_up, w_down, b_down) = args
    L, D, C, T, FFs, FILT = z.L, z.D, z.C, z.T, z.FFs, z.FILT
    lag = np.arange(T) / T
    bands = np.arange(1, z.EMB // 2 + 1)
    phases = 2.0 * math.pi * lag[:, None] * bands[None, :]
    emb = np.concatenate([lag[:, None], np.cos(phases), np.sin(phases)], axis=1)
    emb = np.pad(emb, ((0, 0), (0, z.EP - z.EMB))).astype(np.float32)
    turn = (np.arange(T) * 2 + 1)[:, None] * np.arange(T)[None, :] % (4 * T)
    turn = turn * (math.pi / (2 * T))
    table = np.stack([np.cos(turn), np.sin(turn)])
    dft = table.astype(jnp.bfloat16)
    dftt = np.ascontiguousarray(np.swapaxes(table, 1, 2)).astype(jnp.bfloat16)
    values = (
        inputs, cotangent, lengths, ln1_gain, ln1_bias, jnp.transpose(w_in, (0, 2, 3, 1)),
        jnp.swapaxes(b_in, 0, 1), jnp.transpose(conv_weight, (1, 2, 0, 3)).reshape(9, L, C),
        jnp.swapaxes(conv_bias, 0, 1), jnp.asarray(emb), filt_w1, filt_b1, filt_w2, filt_b2,
        filt_freq, filt_w3, decay_rate, skip_gain, w_out, b_out, ln2_gain, ln2_bias,
        jnp.swapaxes(w_up, 1, 2), b_up, w_down, b_down, jnp.asarray(dft), jnp.asarray(dftt),
    )
    shapes, sems, _, _ = scratch_shapes(z)
    names = INPUTS + OUTPUTS + tuple(shapes) + ("ssem", "rsem", "lsem")
    f32 = lambda *dims: jax.ShapeDtypeStruct(dims, F32)
    outs = (
        f32(z.R, D), f32(z.R, D), f32(L, z.FR, D), f32(L, 4, z.DB, C), f32(L, 8, D),
        f32(L, z.FROWS, FILT), f32(L, z.CROWS, C),
    )
    vmem = pl.BlockSpec(memory_space=pltpu.VMEM)
    place = {"lens": pltpu.SMEM, "w_in": pl.ANY, "w_out": pl.ANY}
    specs = [pl.BlockSpec(memory_space=place.get(name, pltpu.VMEM)) for name in INPUTS]
    out, gin, *packed = pl.pallas_call(
        functools.partial(fused_kernel, z, names),
        out_shape=outs,
        in_specs=specs,
        out_specs=[vmem] * len(outs),
        scratch_shapes=[pltpu.VMEM(*spec) for spec in shapes.values()]
        + [
            pltpu.SemaphoreType.DMA((sems,)),
            pltpu.SemaphoreType.DMA((sems,)),
            pltpu.SemaphoreType.DMA((L,)),
        ],
        compiler_params=pltpu.CompilerParams(
            collective_id=0, has_side_effects=True, vmem_limit_bytes=VMEM_LIMIT
        ),
        name="hyena_layers",
    )(*values)
    final = dict(
        ln1g=f32(L, D), ln1b=f32(L, D), w_in=f32(L, 3, z.DB, C), b_in=f32(3, L, C),
        cw=f32(9, L, C), cb=f32(3, L, C), fw1=f32(z.EMB, L, FILT), fb1=f32(L, FILT),
        fw2=f32(L, FILT, FILT), fb2=f32(L, FILT), freq=f32(L, 2, FILT), fw3=f32(L, FILT, C),
        decay=f32(L, C), skip=f32(L, C), w_out=f32(L, C, z.DB), b_out=f32(L, D),
        ln2g=f32(L, D), ln2b=f32(L, D), w_up=f32(L, FFs, D), b_up=f32(L, FFs),
        w_down=f32(L, FFs, D), b_down=f32(L, D),
    )
    res = pl.pallas_call(
        functools.partial(finish_kernel, z),
        out_shape=tuple(final[name] for name in FINAL),
        in_specs=[vmem] * len(packed),
        out_specs=[vmem] * len(FINAL),
        compiler_params=pltpu.CompilerParams(vmem_limit_bytes=40 * 1024 * 1024),
        name="hyena_unpack",
    )(*packed)
    g = types.SimpleNamespace(**dict(zip(FINAL, res)))
    return (
        out, gin, g.ln1g, g.ln1b, jnp.swapaxes(g.w_in, 1, 2), jnp.swapaxes(g.b_in, 0, 1),
        jnp.transpose(g.cw.reshape(3, 3, L, C), (2, 0, 1, 3)), jnp.swapaxes(g.cb, 0, 1),
        jnp.swapaxes(g.fw1, 0, 1), g.fb1, g.fw2, g.fb2, g.freq, g.fw3, g.decay, g.skip, g.w_out,
        g.b_out, g.ln2g, g.ln2b, jnp.swapaxes(g.w_up, 1, 2), g.b_up, g.w_down, g.b_down,
    )


def local_any(mesh, *args):
    z = Sizes(
        mesh.shape["dp"], mesh.shape["tensor"], args[0].shape[0], args[0].shape[1],
        args[5].shape[3], args[21].shape[2], args[2].shape[1], args[5].shape[0],
        args[9].shape[1], args[9].shape[2],
    )
    return fused_local(z, *args) if z.fits() else local(*args)


def solution(mesh):
    in_specs = (
        P(("dp", "tensor"), None),
        P(("dp", "tensor"), None),
        P("dp", None),
        P(),
        P(),
        P(None, None, None, "tensor"),
        P(None, None, "tensor"),
        P(None, None, None, "tensor"),
        P(None, None, "tensor"),
        P(),
        P(),
        P(),
        P(),
        P(),
        P(None, None, "tensor"),
        P(None, "tensor"),
        P(None, "tensor"),
        P(None, "tensor", None),
        P(),
        P(),
        P(),
        P(None, None, ("dp", "tensor")),
        P(None, ("dp", "tensor")),
        P(None, ("dp", "tensor"), None),
        P(),
    )
    out_specs = (
        P(("dp", "tensor"), None),
        P(("dp", "tensor"), None),
        P(),
        P(),
        P(None, "dp", None, "tensor"),
        P(None, None, "tensor"),
        P(None, None, None, "tensor"),
        P(None, None, "tensor"),
        P(),
        P(),
        P(),
        P(),
        P(),
        P(None, None, "tensor"),
        P(None, "tensor"),
        P(None, "tensor"),
        P(None, "tensor", "dp"),
        P(),
        P(),
        P(),
        P(None, None, ("dp", "tensor")),
        P(None, ("dp", "tensor")),
        P(None, ("dp", "tensor"), None),
        P(),
    )
    return jax.shard_map(functools.partial(local_any, mesh), mesh=mesh, in_specs=in_specs, out_specs=out_specs, check_vma=False)
```

```python
import functools
import math
import types

import jax
import jax.numpy as jnp
import numpy as np
from jax import lax
from jax.experimental import pallas as pl
from jax.experimental.pallas import tpu as pltpu
from jax.sharding import PartitionSpec as P

NORM_EPS = 1e-05
PRECISE = lax.Precision.HIGHEST


def layer_norm(values, norm_gain, norm_shift):
    center = values - jnp.mean(values, axis=-1, keepdims=True)
    spread = jnp.mean(center * center, axis=-1, keepdims=True)
    return center * lax.rsqrt(spread + NORM_EPS) * norm_gain + norm_shift


def filter_taps(w_first, b_first, w_second, b_second, freq_pair, w_third, decay_row, length):
    lag_pos = jnp.arange(length).astype(jnp.float32)
    fraction = lag_pos / length
    band_ids = jnp.arange(1, w_first.shape[0] // 2 + 1).astype(jnp.float32)
    phases = 2.0 * math.pi * fraction[:, None] * band_ids[None, :]
    embedding = jnp.concatenate([fraction[:, None], jnp.cos(phases), jnp.sin(phases)], axis=1)
    layer_one = jnp.sin(freq_pair[0] * (jnp.dot(embedding, w_first, precision=PRECISE) + b_first))
    layer_two = jnp.sin(freq_pair[1] * (jnp.dot(layer_one, w_second, precision=PRECISE) + b_second))
    return jnp.dot(layer_two, w_third, precision=PRECISE) * jnp.exp(
        -lag_pos[:, None] * decay_row[None, :]
    )


def segment_ids(lens_row, length):
    places = jnp.arange(length)
    ends = jnp.cumsum(lens_row)
    return jnp.sum((places[:, None] >= ends[None, :-1]).astype(jnp.int32), axis=1)


def short_conv(projected, weight_short, bias_short, seg_ids):
    summed = bias_short[None] + weight_short[0][None] * projected
    for offset in (1, 2):
        shifted = jnp.concatenate(
            [jnp.zeros((offset,) + projected.shape[1:], jnp.float32), projected[:-offset]], axis=0
        )
        earlier = jnp.concatenate([jnp.full((offset,), -1, jnp.int32), seg_ids[:-offset]], axis=0)
        within = (earlier == seg_ids).astype(jnp.float32)
        summed = summed + weight_short[offset][None] * shifted * within[:, None, None]
    return summed


def trig_table(count_rows, count_cols, modulus):
    product = jnp.arange(count_rows)[:, None] * jnp.arange(count_cols)[None, :] % modulus
    phases = product.astype(jnp.float32) * (2.0 * math.pi / modulus)
    return (jnp.cos(phases), jnp.sin(phases))


def forward_dft(signal, tables):
    cos_a, sin_a, cos_t, sin_t, cos_b, sin_b = tables
    shaped = signal.reshape(cos_a.shape[0], cos_b.shape[0], signal.shape[1])
    real_one = jnp.einsum("abc,ak->kbc", shaped, cos_a, precision=PRECISE)
    imag_one = -jnp.einsum("abc,ak->kbc", shaped, sin_a, precision=PRECISE)
    turn_re = cos_t[:, :, None]
    turn_im = sin_t[:, :, None]
    real_two = real_one * turn_re + imag_one * turn_im
    imag_two = imag_one * turn_re - real_one * turn_im
    real_out = jnp.einsum("kbc,bj->kjc", real_two, cos_b, precision=PRECISE) + jnp.einsum(
        "kbc,bj->kjc", imag_two, sin_b, precision=PRECISE
    )
    imag_out = jnp.einsum("kbc,bj->kjc", imag_two, cos_b, precision=PRECISE) - jnp.einsum(
        "kbc,bj->kjc", real_two, sin_b, precision=PRECISE
    )
    return (real_out, imag_out)


def inverse_dft(real_in, imag_in, tables):
    cos_a, sin_a, cos_t, sin_t, cos_b, sin_b = tables
    real_one = jnp.einsum("kjc,bj->kbc", real_in, cos_b, precision=PRECISE) - jnp.einsum(
        "kjc,bj->kbc", imag_in, sin_b, precision=PRECISE
    )
    imag_one = jnp.einsum("kjc,bj->kbc", imag_in, cos_b, precision=PRECISE) + jnp.einsum(
        "kjc,bj->kbc", real_in, sin_b, precision=PRECISE
    )
    turn_re = cos_t[:, :, None]
    turn_im = sin_t[:, :, None]
    real_two = real_one * turn_re - imag_one * turn_im
    imag_two = imag_one * turn_re + real_one * turn_im
    shaped = jnp.einsum("kbc,ak->abc", real_two, cos_a, precision=PRECISE) - jnp.einsum(
        "kbc,ak->abc", imag_two, sin_a, precision=PRECISE
    )
    total_len = 2 * shaped.shape[0] * shaped.shape[1]
    return shaped.reshape(shaped.shape[0] * shaped.shape[1], shaped.shape[2]) / total_len


def local(
    inputs,
    cotangent,
    lengths,
    ln1_gain,
    ln1_bias,
    w_in,
    b_in,
    conv_weight,
    conv_bias,
    filt_w1,
    filt_b1,
    filt_w2,
    filt_b2,
    filt_freq,
    filt_w3,
    decay_rate,
    skip_gain,
    w_out,
    b_out,
    ln2_gain,
    ln2_bias,
    w_up,
    b_up,
    w_down,
    b_down,
):
    rows_dev = inputs.shape[0]
    tensor_size = lax.axis_size("tensor")
    group_len = rows_dev * tensor_size
    layer_count = w_in.shape[0]
    seg_ids = segment_ids(lengths[0], group_len)
    masks_seq = tuple(
        ((seg_ids == seq_pos).astype(jnp.float32) for seq_pos in range(lengths.shape[1]))
    )
    full_len = 2 * group_len
    fold_a = math.gcd(full_len, 128)
    fold_b = full_len // fold_a
    cos_a, sin_a = trig_table(fold_a // 2, fold_a, fold_a)
    cos_t, sin_t = trig_table(fold_a, fold_b, full_len)
    cos_b, sin_b = trig_table(fold_b, fold_b, fold_b)
    tables = (cos_a, sin_a, cos_t, sin_t, cos_b, sin_b)

    def mixer_local(
        projected,
        weight_short,
        bias_short,
        fw_one,
        fb_one,
        fw_two,
        fb_two,
        freq_pair,
        fw_three,
        decay_row,
        skip_row,
    ):
        gated = short_conv(projected, weight_short, bias_short, seg_ids)
        taps_long = filter_taps(
            fw_one, fb_one, fw_two, fb_two, freq_pair, fw_three, decay_row, group_len
        )
        filt_re, filt_im = forward_dft(taps_long, tables)
        mixed_in = gated[:, 2] * gated[:, 1]
        result = skip_row * mixed_in
        for mask_one in masks_seq:
            sig_re, sig_im = forward_dft(mixed_in * mask_one[:, None], tables)
            result = result + mask_one[:, None] * inverse_dft(
                sig_re * filt_re - sig_im * filt_im, sig_re * filt_im + sig_im * filt_re, tables
            )
        return result * gated[:, 0]

    kept_list = []
    current = inputs
    for layer_idx in range(layer_count):
        normed, norm_back = jax.vjp(layer_norm, current, ln1_gain[layer_idx], ln1_bias[layer_idx])
        normed_full = lax.all_gather(normed.astype(jnp.bfloat16), "tensor", axis=0, tiled=True)
        projected = (
            jnp.einsum(
                "td,dkc->tkc", normed_full, w_in[layer_idx], preferred_element_type=jnp.float32
            )
            + b_in[layer_idx]
        )
        mixer_val, mixer_back = jax.vjp(
            mixer_local,
            projected,
            conv_weight[layer_idx],
            conv_bias[layer_idx],
            filt_w1[layer_idx],
            filt_b1[layer_idx],
            filt_w2[layer_idx],
            filt_b2[layer_idx],
            filt_freq[layer_idx],
            filt_w3[layer_idx],
            decay_rate[layer_idx],
            skip_gain[layer_idx],
        )
        mixer_low = mixer_val.astype(jnp.bfloat16)
        weight_out = w_out[layer_idx]
        keep_out = lax.all_to_all(mixer_low, "tensor", split_axis=0, concat_axis=1, tiled=True)
        weight_out = lax.all_gather(weight_out, "tensor", axis=0, tiled=True)
        branch_out = jnp.dot(keep_out, weight_out, preferred_element_type=jnp.float32)
        middle = current + branch_out + b_out[layer_idx]
        normed_two, norm_two_back = jax.vjp(
            layer_norm, middle, ln2_gain[layer_idx], ln2_bias[layer_idx]
        )
        normed_two_low = normed_two.astype(jnp.bfloat16)
        up_full, upb_full, down_full = (
            lax.all_gather(w_up[layer_idx], ("dp", "tensor"), axis=1, tiled=True),
            lax.all_gather(b_up[layer_idx], ("dp", "tensor"), axis=0, tiled=True),
            lax.all_gather(w_down[layer_idx], ("dp", "tensor"), axis=0, tiled=True),
        )
        hidden_pre = jnp.dot(
            normed_two_low, up_full, preferred_element_type=jnp.float32
        ) + upb_full.astype(jnp.float32)
        hidden_act, gelu_back = jax.vjp(jax.nn.gelu, hidden_pre)
        hidden_low = hidden_act.astype(jnp.bfloat16)
        current = (
            middle
            + jnp.dot(hidden_low, down_full, preferred_element_type=jnp.float32)
            + b_down[layer_idx]
        )
        kept_list.append(
            (
                norm_back,
                normed_full,
                mixer_back,
                keep_out,
                weight_out,
                norm_two_back,
                normed_two_low,
                None,
                None,
                hidden_low,
                gelu_back,
            )
        )
    grad_rows = cotangent
    per_layer = [None] * layer_count
    for layer_idx in reversed(range(layer_count)):
        (
            norm_back,
            normed_full,
            mixer_back,
            keep_out,
            weight_out,
            norm_two_back,
            normed_two_low,
            up_full,
            down_full,
            hidden_low,
            gelu_back,
        ) = kept_list[layer_idx]
        up_full, down_full = (
            lax.all_gather(w_up[layer_idx], ("dp", "tensor"), axis=1, tiled=True),
            lax.all_gather(w_down[layer_idx], ("dp", "tensor"), axis=0, tiled=True),
        )
        down_low = grad_rows.astype(jnp.bfloat16)
        grad_b_down = jnp.sum(down_low.astype(jnp.float32), axis=0)
        grad_w_down = jnp.einsum(
            "tf,td->fd", hidden_low, down_low, preferred_element_type=jnp.float32
        )
        grad_hidden = jnp.einsum(
            "td,fd->tf", down_low, down_full, preferred_element_type=jnp.float32
        )
        (grad_pre,) = gelu_back(grad_hidden)
        pre_low = grad_pre.astype(jnp.bfloat16)
        grad_w_up = jnp.einsum(
            "td,tf->df", normed_two_low, pre_low, preferred_element_type=jnp.float32
        )
        grad_b_up = jnp.sum(pre_low.astype(jnp.float32), axis=0)
        grad_normed_two = jnp.einsum(
            "tf,df->td", pre_low, up_full, preferred_element_type=jnp.float32
        )
        shard_w_up, shard_b_up, shard_w_down = (
            lax.psum_scatter(grad_w_up, ("dp", "tensor"), scatter_dimension=1, tiled=True),
            lax.psum_scatter(grad_b_up, ("dp", "tensor"), scatter_dimension=0, tiled=True),
            lax.psum_scatter(grad_w_down, ("dp", "tensor"), scatter_dimension=0, tiled=True),
        )
        grad_middle_ln, grad_ln2_gain, grad_ln2_bias = norm_two_back(grad_normed_two)
        grad_middle = grad_rows + grad_middle_ln
        out_low = grad_middle.astype(jnp.bfloat16)
        grad_b_out = jnp.sum(out_low.astype(jnp.float32), axis=0)
        grad_rows_mixed = jnp.einsum(
            "td,cd->tc", out_low, weight_out, preferred_element_type=jnp.float32
        )
        grad_mixed = lax.all_to_all(
            grad_rows_mixed.astype(jnp.bfloat16), "tensor", split_axis=1, concat_axis=0, tiled=True
        ).astype(grad_rows_mixed.dtype)
        grad_w_out = lax.psum_scatter(
            jnp.einsum("tc,td->cd", keep_out, out_low, preferred_element_type=jnp.float32).astype(
                jnp.bfloat16
            ),
            "tensor",
            scatter_dimension=0,
            tiled=True,
        ).astype(jnp.float32)
        grads_mixer = mixer_back(grad_mixed)
        proj_low = grads_mixer[0].astype(jnp.bfloat16)
        grad_w_in = jnp.einsum(
            "td,tkc->dkc", normed_full, proj_low, preferred_element_type=jnp.float32
        )
        grad_b_in = jnp.sum(proj_low.astype(jnp.float32), axis=0)
        weight_in = w_in[layer_idx]
        grad_normed = lax.psum_scatter(
            jnp.einsum(
                "tkc,dkc->td", proj_low, weight_in, preferred_element_type=jnp.float32
            ).astype(jnp.bfloat16),
            "tensor",
            scatter_dimension=0,
            tiled=True,
        ).astype(jnp.float32)
        grad_in_ln, grad_ln1_gain, grad_ln1_bias = norm_back(grad_normed)
        grad_rows = grad_middle + grad_in_ln
        per_layer[layer_idx] = (
            grad_ln1_gain,
            grad_ln1_bias,
            grad_w_in,
            grad_b_in,
            grads_mixer[1],
            grads_mixer[2],
            grads_mixer[3],
            grads_mixer[4],
            grads_mixer[5],
            grads_mixer[6],
            grads_mixer[7],
            grads_mixer[8],
            grads_mixer[9],
            grads_mixer[10],
            grad_w_out,
            grad_b_out,
            grad_ln2_gain,
            grad_ln2_bias,
            shard_w_up,
            shard_b_up,
            shard_w_down,
            grad_b_down,
        )
    stacks = [
        jnp.stack([per_layer[layer_pos][slot_pos] for layer_pos in range(layer_count)])
        for slot_pos in range(22)
    ]
    shared_done = lax.psum(
        (
            stacks[0],
            stacks[1],
            stacks[6],
            stacks[7],
            stacks[8],
            stacks[9],
            stacks[10],
            stacks[15],
            stacks[16],
            stacks[17],
            stacks[21],
        ),
        ("dp", "tensor"),
    )
    weight_done = (
        lax.psum_scatter(
            stacks[2].astype(jnp.bfloat16), "dp", scatter_dimension=1, tiled=True
        ).astype(jnp.float32),
        lax.psum_scatter(
            stacks[14].astype(jnp.bfloat16), "dp", scatter_dimension=2, tiled=True
        ).astype(jnp.float32),
    )
    group_done = (
        lax.psum(stacks[3].astype(jnp.bfloat16), "dp").astype(jnp.float32),
        lax.psum(stacks[4].astype(jnp.bfloat16), "dp").astype(jnp.float32),
        lax.psum(stacks[5].astype(jnp.bfloat16), "dp").astype(jnp.float32),
        lax.psum(stacks[11].astype(jnp.bfloat16), "dp").astype(jnp.float32),
        lax.psum(stacks[12].astype(jnp.bfloat16), "dp").astype(jnp.float32),
        lax.psum(stacks[13].astype(jnp.bfloat16), "dp").astype(jnp.float32),
    )
    return (
        current,
        grad_rows,
        shared_done[0],
        shared_done[1],
        weight_done[0],
        group_done[0],
        group_done[1],
        group_done[2],
        shared_done[2],
        shared_done[3],
        shared_done[4],
        shared_done[5],
        shared_done[6],
        group_done[3],
        group_done[4],
        group_done[5],
        weight_done[1],
        shared_done[7],
        shared_done[8],
        shared_done[9],
        stacks[18],
        stacks[19],
        stacks[20],
        shared_done[10],
    )


BF16 = jnp.bfloat16
F32 = jnp.float32
MESH = pl.DeviceIdType.MESH
SHARE = 4
GELU_C = math.sqrt(2.0 / math.pi)
GELU_A = 0.044715
VMEM_LIMIT = 63 * 1024 * 1024
ROW_DECAY, ROW_SKIP, ROW_ENDS, ROW_W3 = 15, 16, 17, 24


def dot_nn(a, b, precision=None):
    return lax.dot_general(
        a, b, (((1,), (0,)), ((), ())), precision=precision, preferred_element_type=F32
    )


def dot_nt(a, b, precision=None):
    return lax.dot_general(
        a, b, (((1,), (1,)), ((), ())), precision=precision, preferred_element_type=F32
    )


def dot_tn(a, b, precision=None):
    return lax.dot_general(
        a, b, (((0,), (0,)), ((), ())), precision=precision, preferred_element_type=F32
    )


class Sizes:
    def __init__(self, mesh_dp, mesh_tp, rows, width, chan, shard, slots, layers, emb, filt):
        self.ndp, self.n = mesh_dp, mesh_tp
        self.R, self.D, self.C = rows, width, chan
        self.T = rows * mesh_tp
        self.FFs = shard
        self.FR = 2 * shard + 16
        self.Y = mesh_dp // SHARE
        self.FB = mesh_tp * shard
        self.SL, self.L = slots, layers
        self.EMB, self.FILT = emb, filt
        self.EP = -(-emb // 8) * 8
        self.DB = width // mesh_dp
        self.DP = 4 * chan // mesh_dp
        self.PK = mesh_dp // 4
        self.TL = rows // 2
        self.FROWS = self.EP + filt + 8
        self.LF = layers * filt
        self.CROWS = ROW_W3 + filt

    def places(self):
        at_wo = self.L * self.FR
        at_rows = at_wo + self.L * self.DB
        at_side = at_rows + 8 * self.L
        at_out = at_side + -(-max(self.FROWS, self.CROWS) // 8) * 8
        return at_wo, at_rows, at_side, at_out

    def fits(self):
        return (
            self.n == SHARE
            and self.ndp == 2 * SHARE
            and self.FFs % 16 == 0
            and self.DP % 16 == 0
            and self.FB <= self.D
            and self.SL <= 8
            and self.TL == 64
            and self.LF + (2 * self.L - 1) * self.C <= self.D
            and 4 * self.C <= self.D
            and self.n == 4
            and vmem_bytes(scratch_shapes(self)[0]) < VMEM_LIMIT - 6 * 1024 * 1024
        )


INPUTS = (
    "x", "cot", "lens", "ln1g", "ln1b", "w_in", "b_in", "cw", "cb", "emb", "fw1", "fb1", "fw2",
    "fb2", "freq", "fw3", "decay", "skip", "w_out", "b_out", "ln2g", "ln2b", "w_up", "b_up",
    "w_down", "b_down", "dft", "dftt", "tdft", "tdftt",
)
OUTPUTS = ("pack",)


def scratch_shapes(z):
    R, D, C, T, n, L, Y = z.R, z.D, z.C, z.T, z.n, z.L, z.Y
    steps_dp = z.ndp.bit_length() - 1
    steps = steps_dp + n.bit_length() - 1
    per = 8 * (n - 1) + 8 * (z.ndp - 1) + 56 + n * Y + n * (Y - 1) + (n - 1) + 3 * (n - 1)
    sems = L * (per + 3 * steps + 2) + 8
    shapes = dict(
        xb=((R, D), BF16),
        xv=((R, D), BF16),
        cv=((R, D), BF16),
        ov=((R, D), BF16),
        gv=((R, D), BF16),
        xs=((max(L - 1, 1), R, D), F32),
        mids=((L, R, D), F32),
        gx=((R, D), F32),
        nF=((L, n, R, D), BF16),
        p=((L, 3, T + 8, C), F32),
        inn=((L, T, C), F32),
        innb=((T, C), BF16),
        g0s=((T, C), F32),
        fz=((2, T, z.LF), F32),
        fc=((2, T, z.LF), F32),
        fa=((2, T, z.LF), BF16),
        fw1p=((z.EP, z.LF), F32),
        fw2p=((z.LF, z.LF), F32),
        fw3p=((L, z.LF, C), BF16),
        frow=((8, z.LF), F32),
        taps=((L, T, C), BF16),
        hs=((L, 2, T, C), BF16),
        xf=((L, 2, T, C), BF16),
        yb=((2, T, C), BF16),
        qb=((2, T, C), BF16),
        longs=((L, T, C), F32),
        mx=((L, T, C), BF16),
        pin=((L, z.CROWS, C), F32),
        pv=((L, z.CROWS, C), F32),
        wz=((L, n, z.DP, D), BF16),
        wfull=((L, z.ndp, z.DP, D), BF16),
        n2S=((L, SHARE, R, D), BF16),
        rowb=((16, D), F32),
        ffw=((L, Y, n, z.FR, D), BF16),
        bup=((L, Y, 8, z.FB), F32),
        hp=((L, Y, SHARE, R, z.FB), BF16),
        spf=((2, SHARE, R // 2, D), F32),
        sp=((2, 3, R // 2, D), BF16),
        sr=((2, 3, R // 2, D), BF16),
        gdS=((L, SHARE, R, D), BF16),
        hb=((Y, SHARE, R, z.FB), BF16),
        gpb=((Y, SHARE, R, z.FB), BF16),
        ffry=((L, Y - 1, n, z.FR, D), BF16),
        ffrz=((L, n - 1, 2, z.FR, D), BF16),
        goF=((n, R, D), BF16),
        gg=((3, T + 8, C), F32),
        gpj=((3, T, C), BF16),
        gl=((T, C), F32),
        gtp=((T, C), F32),
        gtt=((z.TL, C), F32),
        hs64=((L, 2, z.TL, C), F32),
        xt=((L, 2, (z.SL - 1) * z.TL, C), BF16),
        tst=(((z.SL - 1) * z.TL, C), BF16),
        wg=((2, z.ndp, z.DB, 2 * C), BF16),
        wr=((L, 2, Y - 1, SHARE, z.DB, 2 * C), BF16),
        wr1=((L, 2, SHARE, z.DB, 2 * C), BF16),
        wr2=((L, 2, n - 1, z.DB, 2 * C), BF16),
        sa=((L, 8, D), F32),
        sf=((L, z.FROWS, z.LF), F32),
        sc=((L, z.CROWS, C), F32),
        sc0=((L, z.CROWS, C), F32),
        rA=((L, steps_dp, 8, D), F32),
        rF=((L, steps_dp, z.FROWS, z.LF), F32),
        rP=((z.ndp - 1, 8, D), F32),
        rZ=((n - 1, 8, D), F32),
        rAz=((steps - steps_dp, L, 8, D), F32),
        rFz=((steps - steps_dp, z.FROWS, z.LF), F32),
        rC=((L, steps_dp, z.CROWS, C), F32),
    )
    return shapes, sems, steps_dp, steps


def vmem_bytes(shapes):
    total = 0
    for dims, kind in shapes.values():
        size = 2 if kind == BF16 else 4
        sub = 32 // size
        lanes = -(-dims[-1] // 128) * 128
        rows = -(-dims[-2] // sub) * sub
        total += math.prod(dims[:-2]) * rows * lanes * size
    return total


def fused_kernel(z, names, *refs):
    R, D, C, T, n, L, Y, ndp = z.R, z.D, z.C, z.T, z.n, z.L, z.Y, z.ndp
    FFs, FB, FILT, EP, DB, TL, LF = z.FFs, z.FB, z.FILT, z.EP, z.DB, z.TL, z.LF
    s = types.SimpleNamespace(**dict(zip(names, refs)))
    dp = lax.axis_index("dp")
    ti = lax.axis_index("tensor")
    y = dp // SHARE
    a = dp % SHARE
    sib = (dp + 1 - 2 * (dp % 2), ti)
    xnb = (dp + 2 - 4 * ((dp // 2) % 2), ti)
    partner = (SHARE * y + ti, a)
    moved = a != ti
    member = [a, a + 1 - 2 * (a % 2), a + 2 - 4 * (a // 2)]
    member.append(member[1] + 2 - 4 * (member[1] // 2))
    HR = R // 2
    FR = z.FR
    used = [0]
    open_sends = []

    def make(src, dst, dev):
        idx = used[0]
        used[0] += 1
        return pltpu.make_async_remote_copy(
            src_ref=src, dst_ref=dst, send_sem=s.ssem.at[idx], recv_sem=s.rsem.at[idx],
            device_id=dev, device_id_type=MESH,
        )

    def push(src, dst, dev, valid=True):
        copy = make(src, dst, dev)
        if valid is True:
            copy.start()
        else:
            pl.when(valid)(copy.start)
        open_sends.append((copy, valid))
        return copy

    def sent(*copies):
        for item in [p for p in open_sends if any(p[0] is c for c in copies)]:
            if item[1] is True:
                item[0].wait_send()
            else:
                pl.when(item[1])(item[0].wait_send)
        open_sends[:] = [p for p in open_sends if not any(p[0] is c for c in copies)]

    def swap(src, dst):
        copy = make(src, dst, partner)
        pl.when(moved)(copy.start)

        @pl.when(a == ti)
        def _():
            dst[...] = src[...]

        open_sends.append((copy, moved))
        return copy

    def swapped(copy):
        pl.when(moved)(copy.wait_recv)

    def flush():
        sent(*[p[0] for p in open_sends])

    def done(copy):
        copy.wait_recv()

    def piece_copy(l, act):
        k = dp // z.PK
        rows = pl.ds(pl.multiple_of((dp % z.PK) * z.DP, z.DP), z.DP)
        dst = s.wz.at[l, ti]

        @pl.when(k < 3)
        def _():
            getattr(pltpu.make_async_copy(s.w_in.at[l, k, rows], dst, s.lsem.at[l]), act)()

        @pl.when(k >= 3)
        def _():
            getattr(pltpu.make_async_copy(s.w_out.at[l, rows], dst, s.lsem.at[l]), act)()

    for l in range(L):
        piece_copy(l, "start")

    barrier = pltpu.get_barrier_semaphore()
    for d in range(1, ndp):
        pl.semaphore_signal(barrier, inc=1, device_id=((dp + d) % ndp, ti), device_id_type=MESH)
    for d in range(1, n):
        pl.semaphore_signal(barrier, inc=1, device_id=(dp, (ti + d) % n), device_id_type=MESH)

    @pl.when(moved)
    def _():
        pl.semaphore_signal(barrier, inc=1, device_id=partner, device_id_type=MESH)

    s.xb[...] = s.x[...].astype(BF16)

    @pl.when(moved)
    def _():
        pl.semaphore_wait(barrier, ndp - 1 + n)

    @pl.when(a == ti)
    def _():
        pl.semaphore_wait(barrier, ndp - 1 + n - 1)

    def ln_parts(v):
        mu = jnp.mean(v, axis=-1, keepdims=True)
        c = v - mu
        r = lax.rsqrt(jnp.mean(c * c, axis=-1, keepdims=True) + NORM_EPS)
        return c * r, r

    def ln_back(v, gy, gain):
        xhat, r = ln_parts(v)
        gz = gy * gain
        gv = r * (
            gz - jnp.mean(gz, axis=-1, keepdims=True)
            - xhat * jnp.mean(gz * xhat, axis=-1, keepdims=True)
        )
        return gv, jnp.sum(gy * xhat, axis=0, keepdims=True), jnp.sum(gy, axis=0, keepdims=True)

    def chip_rows(i):
        return pl.ds(pl.multiple_of(i * 2 * R, 2 * R), 2 * R)

    def chip_block(ref, i):
        return ref[pl.ds(2 * i, 2)].reshape(2 * R, D)

    def layer_input(l, h):
        return s.xv[half(h), :].astype(F32) if l == 0 else s.xs[l - 1, half(h), :]

    def half(h):
        return pl.ds(h * HR, HR)

    def gather_s(buf, h):
        mine = buf.at[member[0], half(h)]
        to_x = push(mine, mine, xnb)
        to_sib = push(mine, mine, sib)
        yield
        done(to_x)
        other = buf.at[member[2], half(h)]
        onward = push(other, other, sib)
        done(to_sib)
        yield
        done(onward)
        sent(to_x, to_sib, onward)

    def scatter_s(h, block, hook=None):
        s.spf[h] = block().reshape(SHARE, HR, D)
        for chip in range(2):
            s.sp[h, chip] = s.spf[h, 2 * chip + 1 - a % 2].astype(BF16)
        c1 = push(s.sp.at[h, 0:2], s.sr.at[h, 0:2], sib)
        yield
        done(c1)
        far = s.spf[h, member[2]] + s.sr[h, 1 - a // 2].astype(F32)
        s.sp[h, 2] = far.astype(BF16)
        cx = push(s.sp.at[h, 2], s.sr.at[h, 2], xnb)
        if hook:
            hook()
        yield
        near = s.spf[h, a] + s.sr[h, a // 2].astype(F32)
        done(cx)
        sent(c1, cx)
        return near + s.sr[h, 2].astype(F32)

    def weave(*gens):
        gens = list(gens)
        while gens:
            for g in list(gens):
                try:
                    next(g)
                except StopIteration:
                    gens.remove(g)

    def y_peer(e):
        return (((y + e) % Y) * SHARE + a, ti)

    def w_gather(l):
        piece_copy(l, "wait")
        HP = z.DP // 2
        cuts = [pl.ds(h * HP, HP) for h in range(2)]
        order = (2, 1, 3)
        along_z, to_member, along_y = [], [], []
        for cut in cuts:
            own = s.wz.at[l, ti, cut]
            along_z.append([push(own, own, (dp, (ti + d) % n)) for d in range(1, n)])
        yield
        for h, cut in enumerate(cuts):
            for c in along_z[h]:
                done(c)
            to_member.append([])
            for d in order:
                m = (a + d) % SHARE
                to_member[h].append(
                    push(s.wz.at[l, m, cut], s.wfull.at[l, dp, cut], (y * SHARE + m, ti))
                )
            s.wfull[l, dp, cut] = s.wz[l, a, cut]
            mine = s.wfull.at[l, dp, cut]
            along_y += [push(mine, mine, y_peer(e)) for e in range(1, Y)]
            yield
        for h, cut in enumerate(cuts):
            for c, d in zip(to_member[h], order):
                done(c)
                piece = s.wfull.at[l, y * SHARE + (a + SHARE - d) % SHARE, cut]
                along_y += [push(piece, piece, y_peer(e)) for e in range(1, Y)]
            yield
        for c in along_y:
            done(c)
        yield

    def w_mat(l, k):
        return s.wfull[l, z.PK * k : z.PK * (k + 1)].reshape(C, D)

    def ff_gather(l):
        s.ffw[l, y, ti, 0:FFs, :] = s.w_up[l]
        s.ffw[l, y, ti, FFs : 2 * FFs, :] = s.w_down[l]
        s.rowb[...] = jnp.zeros((16, D), F32)
        s.rowb[0:1, 0:FFs] = s.b_up[...].astype(F32)[l : l + 1, :]
        s.ffw[l, y, ti, 2 * FFs : 2 * FFs + 16, :] = s.rowb[...].astype(BF16)
        along_y = []
        hops = []
        hop = None
        for h in range(n):
            low = (ti + n - h) % n
            high = (ti + h) % n
            has_low = ti >= h
            has_high = ti + h < n
            if h:
                pl.when(has_low)(hop[0].wait_recv)
                pl.when(has_high)(hop[1].wait_recv)
            lo, hi = s.ffw.at[l, y, low], s.ffw.at[l, y, high]
            if h < n - 1:
                hop = (
                    push(lo, lo, (dp, (ti + 1) % n), jnp.logical_and(has_low, ti < n - 1)),
                    push(hi, hi, (dp, (ti + n - 1) % n), jnp.logical_and(has_high, ti > 0)),
                )
                hops += hop
            for e in range(1, Y):
                if h == 1:
                    own = s.ffw.at[l, y, ti]
                    along_y.append((push(own, own, y_peer(e)), True))
                if h:
                    along_y.append((push(lo, lo, y_peer(e), has_low), has_low))
                    along_y.append((push(hi, hi, y_peer(e), has_high), has_high))
            yield
        for c, valid in along_y:
            if valid is True:
                done(c)
            else:
                pl.when(valid)(c.wait_recv)
        sent(*hops, *[c for c, _ in along_y])
        ff_ready(l)
        yield

    def ff_ready(l):
        for b in range(Y):
            row = jnp.zeros((16, D), F32)
            for j in range(n):
                part = s.ffw[l, b, j, 2 * FFs : 2 * FFs + 16, :].astype(F32)
                row = row + (pltpu.roll(part, FFs * j, 1) if j else part)
            s.bup[l, b] = row[:8, :FB]

    def ff_up(l, b):
        return s.ffw[l, b, :, 0:FFs, :].reshape(FB, D)

    def ff_down(l, b):
        return s.ffw[l, b, :, FFs : 2 * FFs, :].reshape(FB, D)

    CH = 64
    ENDS = range(z.SL - 1)

    def end_row(k):
        return s.pv[0, ROW_ENDS + k : ROW_ENDS + k + 1, :]

    def chunk_masks(r0, rows):
        t = (lax.broadcasted_iota(jnp.int32, (rows, C), 0) + r0).astype(F32)
        m1 = jnp.ones((rows, C), F32)
        for k in ENDS:
            m1 = jnp.where(t == end_row(k), 0.0, m1)
        m2 = m1
        for k in ENDS:
            m2 = jnp.where(t == end_row(k) + 1.0, 0.0, m2)
        return m1, m2

    def conv_row(l, step, k):
        return s.pv[l, 3 + step * 3 + k : 4 + step * 3 + k, :]

    def shifted(l, k, r0, masks):
        blk = s.p[l, k, pl.ds(r0, CH + 8), :]
        if masks is None:
            return blk[8:], blk[7:-1], blk[6:-2]
        return blk[8:], blk[7:-1] * masks[0], blk[6:-2] * masks[1]

    LAST = T // CH - 1

    def each_chunk(step):
        @pl.loop(0, LAST)
        def _(i):
            step(pl.multiple_of(i * CH, CH), None)

        step(LAST * CH, chunk_masks(LAST * CH, CH))

    def gate(l, k, parts):
        return (
            s.pv[l, 12 + k : 13 + k, :]
            + conv_row(l, 0, k) * parts[0]
            + conv_row(l, 1, k) * parts[1]
            + conv_row(l, 2, k) * parts[2]
        )

    def lag_rows():
        return lax.broadcasted_iota(jnp.int32, (T, C), 0).astype(F32)

    def decay_row(l):
        return s.pv[l, ROW_DECAY : ROW_DECAY + 1, :]

    def skip_row(l):
        return s.pv[l, ROW_SKIP : ROW_SKIP + 1, :]

    def filter_net():
        s.fw1p[...] = jnp.zeros((EP, LF), F32)
        s.fw2p[...] = jnp.zeros((LF, LF), F32)
        for l in range(L):
            at = slice(l * FILT, (l + 1) * FILT)
            row = slice(l, l + 1)
            for r in range(z.EMB):
                s.fw1p[r : r + 1, at] = s.fw1[r, row, :]
            s.fw2p[at, at] = s.fw2[l]
            s.frow[0:1, at] = s.fb1[row, :]
            s.frow[1:2, at] = s.fb2[row, :]
            s.frow[2:4, at] = s.freq[l]
        z1 = dot_nn(s.emb[...], s.fw1p[...], PRECISE) + s.frow[0:1, :]
        u1 = s.frow[2:3, :] * z1
        a1 = jnp.sin(u1)
        s.fz[0] = z1
        s.fa[0] = a1.astype(BF16)
        s.fc[0] = jnp.cos(u1)
        z2 = dot_nn(a1, s.fw2p[...], PRECISE) + s.frow[1:2, :]
        u2 = s.frow[3:4, :] * z2
        s.fz[1] = z2
        s.fa[1] = jnp.sin(u2).astype(BF16)
        s.fc[1] = jnp.cos(u2)

    def filter_taps_of(l):
        s.fw3p[l] = jnp.zeros((LF, C), BF16)
        s.fw3p[l, l * FILT : (l + 1) * FILT, :] = s.pv[l, ROW_W3 : ROW_W3 + FILT, :].astype(BF16)
        tp = dot_nn(s.fa[1], s.fw3p[l]) * jnp.exp(-lag_rows() * decay_row(l))
        s.innb[...] = tp.astype(BF16)
        s.taps[l] = s.innb[...]
        s.hs64[l, 0] = dot_nn(s.tdft[0, 0:TL, 0:TL], s.innb[0:TL, :])
        s.hs64[l, 1] = dot_nn(s.tdft[1, 0:TL, 0:TL], s.innb[0:TL, :])

        @pl.loop(0, n // 2)
        def _(i):
            rows = chip_rows(i)
            s.hs[l, 0, rows, :] = dot_nn(s.dft[0, rows, :], s.innb[...]).astype(BF16)
            s.hs[l, 1, rows, :] = dot_nn(s.dft[1, rows, :], s.innb[...]).astype(BF16)

    def tail_masks():
        t = lax.broadcasted_iota(jnp.int32, (TL, C), 0).astype(F32) + float(T - TL)
        masks = []
        for k in ENDS:
            live = t >= end_row(k)
            if k + 1 < z.SL - 1:
                live = jnp.logical_and(live, t < end_row(k + 1))
            masks.append(live.astype(F32))
        return masks, t < end_row(0)

    def tail_spectrum(rows, masks):
        for k, mask in enumerate(masks):
            s.tst[k * TL : (k + 1) * TL, :] = (rows * mask).astype(BF16)
        return dot_nn(s.tdft[0], s.tst[...]), dot_nn(s.tdft[1], s.tst[...])

    def tail_back(re, im):
        res = dot_nn(s.tdftt[0], re.astype(BF16)) + dot_nn(s.tdftt[1], im.astype(BF16))
        res = res * (1.0 / TL)
        return [res[k * TL : (k + 1) * TL] for k in ENDS]

    def tail_filter(l, part):
        one = s.hs64[l, part]
        return jnp.concatenate([one] * len(ENDS), axis=0)

    def project(l, h):
        rows = s.nF[l, :, half(h), :].reshape(SHARE * HR, D)
        for k in range(3):
            if h == 0:
                s.p[l, k, 0:8, :] = jnp.zeros((8, C), F32)
            res = dot_nt(rows, w_mat(l, k)) + s.pv[l, k : k + 1, :]
            for m in range(SHARE):
                lo = 8 + m * R + h * HR
                s.p[l, k, lo : lo + HR, :] = res[m * HR : (m + 1) * HR]

    def mixer_forward(l, tick):
        def step(r0, masks):
            g0 = gate(l, 0, shifted(l, 0, r0, masks))
            g1 = gate(l, 1, shifted(l, 1, r0, masks))
            g2 = gate(l, 2, shifted(l, 2, r0, masks))
            inner = g2 * g1
            s.g0s[pl.ds(r0, CH), :] = g0
            s.inn[l, pl.ds(r0, CH), :] = inner
            s.innb[pl.ds(r0, CH), :] = inner.astype(BF16)

        each_chunk(step)

        @pl.loop(0, n // 2)
        def _(i):
            rows = chip_rows(i)
            xr = dot_nn(s.dft[0, rows, :], s.innb[...])
            xi = dot_nn(s.dft[1, rows, :], s.innb[...])
            hr = s.hs[l, 0, rows, :].astype(F32)
            hi = s.hs[l, 1, rows, :].astype(F32)
            s.xf[l, 0, rows, :] = xr.astype(BF16)
            s.xf[l, 1, rows, :] = xi.astype(BF16)
            s.yb[0, rows, :] = (xr * hr - xi * hi).astype(BF16)
            s.yb[1, rows, :] = (xr * hi + xi * hr).astype(BF16)

        tick()

        masks, first = tail_masks()
        xr, xi = tail_spectrum(s.inn[l, T - TL : T, :], masks)
        s.xt[l, 0] = xr.astype(BF16)
        s.xt[l, 1] = xi.astype(BF16)
        hr, hi = tail_filter(l, 0), tail_filter(l, 1)
        parts = tail_back(xr * hr - xi * hi, xr * hi + xi * hr)
        tail = parts[0] * masks[0]
        for part, mask in zip(parts[1:], masks[1:]):
            tail = tail + part * mask
        s.gtt[...] = tail

        @pl.loop(0, n // 2)
        def _(i):
            rows = chip_rows(i)
            s.longs[l, rows, :] = (
                dot_nn(s.dftt[0, rows, :], s.yb[0]) + dot_nn(s.dftt[1, rows, :], s.yb[1])
            ) * (1.0 / T)
        s.longs[l, T - TL : T, :] = jnp.where(first, s.longs[l, T - TL : T, :], s.gtt[...])

        @pl.loop(0, n // 2)
        def _(i):
            rows = chip_rows(i)
            lg = s.longs[l, rows, :] + skip_row(l) * s.inn[l, rows, :]
            s.longs[l, rows, :] = lg
            s.mx[l, rows, :] = (lg * s.g0s[rows, :]).astype(BF16)

    def gelu_tanh(v):
        return jnp.tanh(GELU_C * (v + GELU_A * v * v * v))

    def ff_block(l, h):
        v = s.n2S[l, :, half(h), :].reshape(SHARE * HR, D)
        acc = jnp.zeros((SHARE * HR, D), F32)
        for b in range(Y):
            pre = dot_nt(v, ff_up(l, b)) + s.bup[l, b, 0:1, :]
            s.hp[l, b, :, half(h), :] = pre.astype(BF16).reshape(SHARE, HR, FB)
            act = 0.5 * pre * (1.0 + gelu_tanh(pre))
            acc = acc + dot_nn(act.astype(BF16), ff_down(l, b))
        return acc

    def ff_back_block(l, h):
        g = s.gdS[l, :, half(h), :].reshape(SHARE * HR, D)
        acc = jnp.zeros((SHARE * HR, D), F32)
        for b in range(Y):
            gh = dot_nt(g, ff_down(l, b))
            v = s.hp[l, b, :, half(h), :].reshape(SHARE * HR, FB).astype(F32)
            th = gelu_tanh(v)
            act = (0.5 * v * (1.0 + th)).astype(BF16)
            s.hb[b, :, half(h), :] = act.reshape(SHARE, HR, FB)
            slope = 0.5 * (1.0 + th) + 0.5 * v * (1.0 - th * th) * (
                GELU_C * (1.0 + 3.0 * GELU_A * v * v)
            )
            gp = (gh * slope).astype(BF16)
            s.gpb[b, :, half(h), :] = gp.reshape(SHARE, HR, FB)
            acc = acc + dot_nn(gp, ff_up(l, b))
        return acc

    def ff_scatter(l):
        act = s.n2S[l].reshape(SHARE * R, D)
        gds = s.gdS[l].reshape(SHARE * R, D)

        def fill(b):
            g = s.gpb[b].reshape(SHARE * R, FB)
            h = s.hb[b].reshape(SHARE * R, FB)
            s.ffw[l, b, :, 0:FFs, :] = dot_tn(g, act).astype(BF16).reshape(n, FFs, D)
            s.ffw[l, b, :, FFs : 2 * FFs, :] = dot_tn(h, gds).astype(BF16).reshape(n, FFs, D)
            sums = jnp.sum(g.astype(F32), axis=0, keepdims=True)
            row = jnp.concatenate([sums, jnp.zeros((1, D - FB), F32)], axis=1) if D > FB else sums
            row = jnp.broadcast_to(row, (16, D))
            for j in range(n):
                part = pltpu.roll(row, (D - FFs * j) % D, 1) if j else row
                s.ffw[l, b, j, 2 * FFs : 2 * FFs + 16, :] = part.astype(BF16)

        order = [3 * (1 - ti // 2), (2 + 3 * ti) % 5, 1 + ti % 2, ti]
        along_y = []
        for e in range(1, Y):
            b = (y + e) % Y
            fill(b)
            for j in order:
                along_y.append(push(s.ffw.at[l, b, j], s.ffry.at[l, e - 1, j], y_peer(e)))
        fill(y)
        yield
        hop = None
        hops = []
        for pos, j in enumerate(order):
            acc = s.ffw[l, y, j].astype(F32)
            for e in range(1, Y):
                done(along_y[(e - 1) * n + pos])
                acc = acc + s.ffry[l, e - 1, j].astype(F32)
            if pos < n - 1:
                s.ffry[l, 0, j] = acc.astype(BF16)
            else:
                s.pack[l * FR : (l + 1) * FR, :] = acc
                sent(*along_y)
            if pos < n - 1:
                d = n - 1 - pos
                new = []
                for side, (valid, inner, to) in enumerate(
                    ((ti + d < n, ti >= 1, ti + 1), (ti >= d, ti < n - 1, ti + n - 1))
                ):
                    j = (ti + d) % n if side == 0 else (ti + n - d) % n
                    if pos:
                        more = jnp.logical_and(valid, inner)
                        pl.when(more)(hop[side].wait_recv)

                        @pl.when(more)
                        def _():
                            s.ffry[l, 0, j] = (
                                s.ffry[l, 0, j].astype(F32) + s.ffrz[l, pos - 1, side].astype(F32)
                            ).astype(BF16)

                    new.append(
                        push(
                            s.ffry.at[l, 0, j], s.ffrz.at[l, pos, side], (dp, to % n), valid
                        )
                    )
                hop = new
                hops += new
            yield
        for side, inner in ((0, ti >= 1), (1, ti < n - 1)):
            pl.when(inner)(hop[side].wait_recv)

            @pl.when(inner)
            def _():
                s.pack[l * FR : (l + 1) * FR, :] = (
                    s.pack[l * FR : (l + 1) * FR, :] + s.ffrz[l, n - 2, side].astype(F32)
                )

        sent(*hops)
        yield

    def mixer_backward(l, ticks):
        def first_step(r0, masks):
            rows = pl.ds(r0, CH)
            g0 = gate(l, 0, shifted(l, 0, r0, masks))
            gm = s.gtp[rows, :]
            glong = gm * g0
            s.gg[0, rows, :] = gm * s.longs[l, rows, :]
            s.gl[rows, :] = glong
            if masks is not None:
                t = (lax.broadcasted_iota(jnp.int32, (CH, C), 0) + r0).astype(F32)
                glong = jnp.where(t < end_row(0), glong, 0.0)
            s.innb[rows, :] = glong.astype(BF16)

        each_chunk(first_step)

        @pl.loop(0, n // 2)
        def _(i):
            rows = chip_rows(i)
            gr = dot_nn(s.dft[0, rows, :], s.innb[...])
            gi = dot_nn(s.dft[1, rows, :], s.innb[...])
            hr = s.hs[l, 0, rows, :].astype(F32)
            hi = s.hs[l, 1, rows, :].astype(F32)
            s.yb[0, rows, :] = (gr * hr + gi * hi).astype(BF16)
            s.yb[1, rows, :] = (gi * hr - gr * hi).astype(BF16)
            xr = s.xf[l, 0, rows, :].astype(F32)
            xi = s.xf[l, 1, rows, :].astype(F32)
            s.qb[0, rows, :] = (gr * xr + gi * xi).astype(BF16)
            s.qb[1, rows, :] = (gi * xr - gr * xi).astype(BF16)

        ticks[0]()
        masks, first = tail_masks()
        gr, gi = tail_spectrum(s.gl[T - TL : T, :], masks)
        hr, hi = tail_filter(l, 0), tail_filter(l, 1)
        parts = tail_back(gr * hr + gi * hi, gi * hr - gr * hi)
        tail = parts[0] * masks[0]
        for part, mask in zip(parts[1:], masks[1:]):
            tail = tail + part * mask
        xr, xi = s.xt[l, 0].astype(F32), s.xt[l, 1].astype(F32)
        parts = tail_back(gr * xr + gi * xi, gi * xr - gr * xi)
        s.gtt[...] = sum(parts[1:], parts[0])

        @pl.loop(0, n // 2)
        def _(i):
            rows = chip_rows(i)
            s.g0s[rows, :] = (
                dot_nn(s.dftt[0, rows, :], s.yb[0]) + dot_nn(s.dftt[1, rows, :], s.yb[1])
            ) * (1.0 / T)
            s.gtp[rows, :] = (
                dot_nn(s.dftt[0, rows, :], s.qb[0]) + dot_nn(s.dftt[1, rows, :], s.qb[1])
            ) * (1.0 / T)

        s.g0s[T - TL : T, :] = jnp.where(first, s.g0s[T - TL : T, :], tail)
        s.gtp[0:TL, :] = s.gtp[0:TL, :] + s.gtt[...]

        ticks[1]()

        def fold(v):
            return jnp.sum(v.reshape(CH // 8, 8, C), axis=0)

        for k in range(3):
            s.gg[k, T : T + 8, :] = jnp.zeros((8, C), F32)

        def gate_step(r0, masks, sums):
            rows = pl.ds(r0, CH)
            parts = [shifted(l, k, r0, masks) for k in range(3)]
            gl = s.gl[rows, :]
            ginner = s.g0s[rows, :] + skip_row(l) * gl
            gk = [s.gg[0, rows, :], ginner * gate(l, 2, parts[2]), ginner * gate(l, 1, parts[1])]
            s.gg[1, rows, :] = gk[1]
            s.gg[2, rows, :] = gk[2]
            new = []
            for step in range(3):
                for k in range(3):
                    new.append(sums[step * 3 + k] + fold(gk[k] * parts[k][step]))
            for k in range(3):
                new.append(sums[9 + k] + fold(gk[k]))
            new.append(sums[12] + fold(gl * s.inn[l, rows, :]))
            return tuple(new)

        sums = lax.fori_loop(
            0,
            LAST,
            lambda i, sums: gate_step(pl.multiple_of(i * CH, CH), None, sums),
            tuple(jnp.zeros((8, C), F32) for _ in range(13)),
        )
        sums = gate_step(LAST * CH, chunk_masks(LAST * CH, CH), sums)
        for pos in range(12):
            s.sc0[l, 3 + pos : 4 + pos, :] = jnp.sum(sums[pos], axis=0, keepdims=True)
        s.sc0[l, ROW_SKIP : ROW_SKIP + 1, :] = jnp.sum(sums[12], axis=0, keepdims=True)

        ticks[2]()

        def proj_step(r0, masks, sums):
            new = []
            for k in range(3):
                blk = s.gg[k, pl.ds(r0, CH + 8), :]
                b1 = blk if masks is None else blk * masks[0]
                b2 = blk if masks is None else blk * masks[1]
                gp = (
                    conv_row(l, 0, k) * blk[0:CH]
                    + conv_row(l, 1, k) * b1[1 : CH + 1]
                    + conv_row(l, 2, k) * b2[2 : CH + 2]
                ).astype(BF16)
                s.gpj[k, pl.ds(r0, CH), :] = gp
                new.append(sums[k] + fold(gp.astype(F32)))
            return tuple(new)

        sums = lax.fori_loop(
            0,
            LAST - 1,
            lambda i, sums: proj_step(pl.multiple_of(i * CH, CH), None, sums),
            tuple(jnp.zeros((8, C), F32) for _ in range(3)),
        )
        for i in (LAST - 1, LAST):
            sums = proj_step(i * CH, chunk_masks(i * CH, CH + 8), sums)
        for k in range(3):
            s.sc0[l, k : k + 1, :] = jnp.sum(sums[k], axis=0, keepdims=True)

    def filter_backward(l):
        lag = lag_rows()
        gt = s.gtp[...]
        s.sc0[l, ROW_DECAY : ROW_DECAY + 1, :] = -jnp.sum(
            lag * gt * s.taps[l].astype(F32), axis=0, keepdims=True
        )
        gtr = (gt * jnp.exp(-lag * decay_row(l))).astype(BF16)
        gw3 = dot_tn(s.fa[1], gtr)
        s.sc0[l, ROW_W3 : ROW_W3 + FILT, :] = gw3[l * FILT : (l + 1) * FILT]
        gu2 = dot_nt(gtr, s.fw3p[l]) * s.fc[1]
        gz2 = gu2 * s.frow[3:4, :]
        gz2b = gz2.astype(BF16)
        s.sf[l, EP : EP + FILT, :] = dot_tn(s.fa[0], gz2b)[l * FILT : (l + 1) * FILT]
        gu1 = dot_nt(gz2b, s.fw2p[...].astype(BF16)) * s.fc[0]
        gz1 = gu1 * s.frow[2:3, :]
        s.sf[l, 0:EP, :] = dot_tn(s.emb[...].astype(BF16), gz1.astype(BF16))
        row = EP + FILT
        s.sf[l, row : row + 1, :] = jnp.sum(gz1, axis=0, keepdims=True)
        s.sf[l, row + 1 : row + 2, :] = jnp.sum(gz2, axis=0, keepdims=True)
        s.sf[l, row + 2 : row + 3, :] = jnp.sum(gu1 * s.fz[0], axis=0, keepdims=True)
        s.sf[l, row + 3 : row + 4, :] = jnp.sum(gu2 * s.fz[1], axis=0, keepdims=True)

    def w_scatter(l):
        rows_all = s.nF[l].reshape(T, D)
        go_all = s.goF[...].reshape(T, D)
        order = (2, 3, 1, 0)
        along_y, to_member, along_z = [], [], []

        def fill(k):
            at = slice((k % 2) * C, (k % 2 + 1) * C)
            for h in range(0, D, 256):
                if k < 3:
                    g = dot_tn(rows_all[:, h : h + 256], s.gpj[k])
                else:
                    g = dot_tn(go_all[:, h : h + 256], s.mx[l])
                gb = g.astype(BF16)
                lo = h
                while lo < h + 256:
                    b = lo // DB
                    off = lo % DB
                    cnt = min(DB - off, h + 256 - lo)
                    s.wg[k // 2, b, off : off + cnt, at] = gb[lo - h : lo - h + cnt]
                    lo += cnt

        for half in range(2):
            fill(2 * half)
            fill(2 * half + 1)
            along_y.append([])
            for e in range(1, Y):
                for d in order:
                    m = (a + d) % SHARE
                    j = ((y + e) % Y) * SHARE + m
                    along_y[half].append(
                        push(s.wg.at[half, j], s.wr.at[l, half, e - 1, m], y_peer(e))
                    )
        yield

        def members(half):
            to_member.append([])
            for pos, d in enumerate(order):
                m = (a + d) % SHARE
                acc = s.wg[half, y * SHARE + m].astype(F32)
                for e in range(1, Y):
                    done(along_y[half][(e - 1) * SHARE + pos])
                    acc = acc + s.wr[l, half, e - 1, m].astype(F32)
                if d:
                    s.wr[l, half, 0, m] = acc.astype(BF16)
                    to_member[half].append(
                        push(s.wr.at[l, half, 0, m], s.wr1.at[l, half, a], (y * SHARE + m, ti))
                    )
                else:
                    s.wr1[l, half, a] = acc.astype(BF16)

        def levels(half):
            for c in to_member[half]:
                done(c)
            along_z.append([])
            for d in range(1, n):
                j = (ti + d) % n
                along_z[half].append(
                    push(s.wr1.at[l, half, j], s.wr2.at[l, half, d - 1], (dp, j))
                )

        members(0)
        yield
        members(1)
        sent(*along_y[0], *along_y[1])
        levels(0)
        yield
        levels(1)
        yield
        for half in range(2):
            acc = s.wr1[l, half, ti].astype(F32)
            for d in range(1, n):
                done(along_z[half][d - 1])
                acc = acc + s.wr2[l, half, d - 1].astype(F32)
            lo = at_wo + l * DB
            s.pack[lo : lo + DB, half * 2 * C : (half + 1) * 2 * C] = acc
            sent(*to_member[half], *along_z[half])
        yield

    def small_plane(l, names):
        pick = dict(a=(s.sa, s.rA), f=(s.sf, s.rF), c=(s.sc, s.rC))
        pairs = [pick[x] for x in names]
        for step in range(ndp.bit_length() - 1):
            bit = 1 << step
            peer = (dp + bit - 2 * bit * ((dp // bit) % 2), ti)
            copies = [push(v.at[l], r.at[l, step], peer) for v, r in pairs]
            yield
            for c in copies:
                done(c)
            sent(*copies)
            for v, r in pairs:
                v[l] = v[l] + r[l, step]
        yield

    def rows_last():
        copies = [
            push(s.sa.at[0], s.rP.at[d - 1], ((dp + d) % ndp, ti)) for d in range(1, ndp)
        ]
        yield
        acc = s.sa[0]
        for d in range(1, ndp):
            done(copies[d - 1])
            acc = acc + s.rP[d - 1]
        sent(*copies)
        s.sa[0] = acc
        copies = [push(s.sa.at[0], s.rZ.at[d - 1], (dp, (ti + d) % n)) for d in range(1, n)]
        yield
        for d in range(1, n):
            done(copies[d - 1])
            acc = acc + s.rZ[d - 1]
        sent(*copies)
        s.sa[0] = acc
        yield

    def small_levels():
        total = s.sf[0]
        for l in range(1, L):
            total = total + s.sf[l]
        s.sf[0] = total
        for step in range(n.bit_length() - 1):
            bit = 1 << step
            peer = (dp, ti + bit - 2 * bit * ((ti // bit) % 2))
            copies = [push(s.sf.at[0], s.rFz.at[step], peer)]
            for l in range(1, L):
                copies.append(push(s.sa.at[l], s.rAz.at[step, l], peer))
            yield
            for c in copies:
                done(c)
            sent(*copies)
            for l in range(1, L):
                s.sa[l] = s.sa[l] + s.rAz[step, l]
            s.sf[0] = s.sf[0] + s.rFz[step]
        yield

    at_wo, at_rows, at_side, at_out = z.places()
    wgen = {0: w_gather(0)}
    next(wgen[0])
    xc = [swap(s.xb.at[half(h)], s.xv.at[half(h)]) for h in range(2)]
    for l in range(L):
        s.pin[l] = jnp.zeros((z.CROWS, C), F32)
        for k in range(3):
            s.pin[l, k : k + 1, :] = s.b_in[k, l : l + 1, :]
            s.pin[l, 12 + k : 13 + k, :] = s.cb[k, l : l + 1, :]
        for k in range(9):
            s.pin[l, 3 + k : 4 + k, :] = s.cw[k, l : l + 1, :]
        s.pin[l, ROW_DECAY : ROW_DECAY + 1, :] = s.decay[l : l + 1, :]
        s.pin[l, ROW_SKIP : ROW_SKIP + 1, :] = s.skip[l : l + 1, :]
        s.pin[l, ROW_W3 : ROW_W3 + FILT, :] = s.fw3[l]
    total = s.lens[0, 0]
    for k in ENDS:
        if k:
            total = total + s.lens[0, k]
        s.pin[0, ROW_ENDS + k : ROW_ENDS + k + 1, :] = jnp.full((1, C), total, jnp.int32).astype(F32)
    filter_net()
    fgen = {l: ff_gather(l) for l in range(L)}
    wgen[1] = w_gather(1)

    def run(*gens):
        def go():
            for g in gens:
                next(g)

        return go

    def seq(*acts):
        def go():
            for act in acts:
                act()

        return go

    def norm_one(l, h, x):
        xhat, _ = ln_parts(x)
        s.nF[l, a, half(h), :] = (xhat * s.ln1g[l : l + 1, :] + s.ln1b[l : l + 1, :]).astype(BF16)

    def first_rows(h):
        swapped(xc[h])
        norm_one(0, h, layer_input(0, h))
        yield from gather_s(s.nF.at[0], h)

    rows = [first_rows(0), first_rows(1)]
    run(wgen[0], wgen[0])()
    pc = swap(s.pin, s.pv)
    run(rows[0], rows[1], wgen[0], rows[0], rows[1], wgen[0], fgen[0])()
    weave(*rows)
    swapped(pc)
    filter_taps_of(0)
    filter_taps_of(1)
    run(wgen[0])()
    project(0, 0)
    project(0, 1)
    run(fgen[0])()

    def forward_rows(l, h, hooks):
        def call(pos):
            if (h, pos) in hooks:
                hooks[(h, pos)]()

        mixed = lambda: s.mx[l].reshape(SHARE, R, C)[:, h * HR : (h + 1) * HR].reshape(
            SHARE * HR, C
        )
        res = yield from scatter_s(h, lambda: dot_nn(mixed(), w_mat(l, 3)), lambda: call(0))
        mid = layer_input(l, h) + s.b_out[l : l + 1, :] + res
        s.mids[l, half(h), :] = mid
        xhat, _ = ln_parts(mid)
        s.n2S[l, a, half(h), :] = (xhat * s.ln2g[l : l + 1, :] + s.ln2b[l : l + 1, :]).astype(BF16)
        yield from gather_s(s.n2S.at[l], h)
        call(1)
        res = yield from scatter_s(h, lambda: ff_block(l, h), lambda: call(2))
        cur = s.mids[l, half(h), :] + s.b_down[l : l + 1, :] + res
        if l + 1 < L:
            s.xs[l, half(h), :] = cur
            norm_one(l + 1, h, cur)
            yield from gather_s(s.nF.at[l + 1], h)
            call(3)
            project(l + 1, h)
        else:
            s.ov[half(h), :] = cur.astype(BF16)

    mixer_forward(0, run(fgen[0]))
    hooks = {
        (1, 0): run(fgen[0], wgen[1]),
        (0, 1): run(fgen[0]),
        (1, 1): run(fgen[1], wgen[1], wgen[1]),
        (1, 2): run(wgen[1], wgen[1], fgen[1]),
        (0, 3): run(wgen[1]),
    }
    weave(forward_rows(0, 0, hooks), forward_rows(0, 1, hooks))
    sent(*xc)
    s.xb[...] = s.cot[...].astype(BF16)
    mixer_forward(1, run(fgen[1]))
    cots = []
    hooks = {
        (1, 0): seq(run(fgen[1]), lambda: cots.append(swap(s.xb, s.cv))),
        (0, 1): run(fgen[1]),
    }
    weave(forward_rows(1, 0, hooks), forward_rows(1, 1, hooks))
    swapped(cots[0])
    outs = swap(s.ov, s.gv)
    s.gx[...] = s.cv[...].astype(F32)

    def add_row(l, pos, row):
        s.sa[l, pos : pos + 1, :] = s.sa[l, pos : pos + 1, :] + row

    def back_block(l, h):
        def rows(k):
            return s.gpj[k].reshape(SHARE, R, C)[:, h * HR : (h + 1) * HR].reshape(SHARE * HR, C)

        acc = dot_nn(rows(0), w_mat(l, 0))
        acc = acc + dot_nn(rows(1), w_mat(l, 1))
        return acc + dot_nn(rows(2), w_mat(l, 2))

    def backward_rows(l, h, hooks):
        def call(pos):
            if (h, pos) in hooks:
                hooks[(h, pos)]()

        if l + 1 < L:
            yield from last_rows(l + 1, h, hooks)
        if l < 0:
            return
        gd = s.gx[half(h), :].astype(BF16)
        s.gdS[l, a, half(h), :] = gd
        add_row(l, 5, jnp.sum(gd.astype(F32), axis=0, keepdims=True))
        yield from gather_s(s.gdS.at[l], h)
        call(1)
        gn = yield from scatter_s(h, lambda: ff_back_block(l, h), lambda: call(2))
        gv, gain_row, bias_row = ln_back(s.mids[l, half(h), :], gn, s.ln2g[l : l + 1, :])
        add_row(l, 2, gain_row)
        add_row(l, 3, bias_row)
        gm = s.gx[half(h), :] + gv
        s.gx[half(h), :] = gm
        go = gm.astype(BF16)
        add_row(l, 4, jnp.sum(go.astype(F32), axis=0, keepdims=True))
        s.goF[a, half(h), :] = go
        yield from gather_s(s.goF, h)
        call(3)
        rows = s.goF[:, half(h), :].reshape(SHARE * HR, D)
        res = dot_nt(rows, w_mat(l, 3))
        for m in range(SHARE):
            lo = m * R + h * HR
            s.gtp[lo : lo + HR, :] = res[m * HR : (m + 1) * HR]

    def last_rows(l, h, hooks):
        def hook():
            if (h, 0) in hooks:
                hooks[(h, 0)]()

        gn = yield from scatter_s(h, lambda: back_block(l, h), hook)
        gv, gain_row, bias_row = ln_back(layer_input(l, h), gn, s.ln1g[l : l + 1, :])
        add_row(l, 0, gain_row)
        add_row(l, 1, bias_row)
        s.gx[half(h), :] = s.gx[half(h), :] + gv

    for l in range(L):
        s.sa[l] = jnp.zeros((8, D), F32)
        s.sf[l] = jnp.zeros((z.FROWS, LF), F32)
        s.sc0[l] = jnp.zeros((z.CROWS, C), F32)

    ffs = [ff_scatter(l) for l in range(L)]
    wsc = [w_scatter(l) for l in range(L)]
    small1 = small_plane(1, "afc")
    small0 = small_plane(0, "fc")
    rows0 = rows_last()
    levels = small_levels()
    none = lambda: None

    def filters(l):
        def go():
            filter_backward(l)

        return go

    hooks = {(1, 2): run(ffs[1])}
    weave(backward_rows(1, 0, hooks), backward_rows(1, 1, hooks))
    mixer_backward(1, [run(ffs[1]), run(ffs[1]), none])
    corner = {}

    def corner_swap(l):
        def go():
            corner[l] = swap(s.sc0.at[l], s.sc.at[l])

        return go

    hooks = {
        (1, 0): seq(run(wsc[1], ffs[1]), filters(1), corner_swap(1)),
        (1, 1): run(ffs[1]),
        (1, 2): run(ffs[0], wsc[1]),
        (0, 3): run(wsc[1]),
        (1, 3): seq(lambda: swapped(corner[1]), run(small1, ffs[0])),
    }
    weave(backward_rows(0, 0, hooks), backward_rows(0, 1, hooks))
    mixer_backward(
        0, [run(small1, wsc[1], ffs[0]), run(small1, ffs[1], ffs[0]), none]
    )
    run(wsc[0])()
    hooks = {
        (0, 0): run(ffs[0]),
        (1, 0): seq(filters(0), corner_swap(0), run(small1)),
    }
    weave(last_rows(0, 0, hooks), last_rows(0, 1, hooks))
    sent(outs)
    s.ov[...] = s.gx[...].astype(BF16)
    gins = swap(s.ov, s.cv)
    run(wsc[0], rows0, wsc[0], wsc[1])()
    swapped(corner[0])
    run(small0, rows0, wsc[0], small0)()
    swapped(outs)
    s.pack[at_out : at_out + R, :] = s.gv[...].astype(F32)
    run(small0, rows0, small0, levels, levels, ffs[0])()
    swapped(gins)
    s.pack[at_out + R : at_out + 2 * R, :] = s.cv[...].astype(F32)
    run(wsc[0], levels)()
    for l in range(L):
        s.pack[at_rows + 8 * l : at_rows + 8 * (l + 1), :] = s.sa[l]
        lo = LF + 2 * C * l
        s.pack[at_side : at_side + z.CROWS, lo : lo + C] = s.sc[l]
    s.pack[at_side : at_side + z.FROWS, 0:LF] = s.sf[0]
    flush()


class View:
    def __init__(self, ref, row, rows, lane, lanes):
        self.ref, self.row, self.rows, self.lane, self.lanes = ref, row, rows, lane, lanes

    def __getitem__(self, at):
        rows, lanes = at
        top, bottom, _ = rows.indices(self.rows)
        left, right, _ = lanes.indices(self.lanes)
        return self.ref[
            self.row + top : self.row + bottom, self.lane + left : self.lane + right
        ]


def finish_kernel(z, *refs):
    o = types.SimpleNamespace(**dict(zip(FINAL, refs[1 : 1 + len(FINAL)])))
    held, sem = refs[-2:]
    copy = pltpu.make_async_copy(refs[0], held, sem)
    copy.start()
    copy.wait()
    at_wo, at_rows, at_side, at_out = z.places()
    C, R = z.C, z.R
    o.out[...] = held[at_out : at_out + R, :]
    o.gin[...] = held[at_out + R : at_out + 2 * R, :]
    for l in range(z.L):
        at = z.EP + z.FILT
        lo = z.LF + 2 * C * l
        sa = View(held, at_rows + 8 * l, 8, 0, z.D)
        sc = View(held, at_side, z.CROWS, lo, C)
        sf = View(held, at_side, z.FROWS, l * z.FILT, z.FILT)
        wo = View(held, at_wo + l * z.DB, z.DB, 0, 4 * C)
        ffo = View(held, l * z.FR, z.FR, 0, z.D)
        row = slice(l, l + 1)
        for pos, ref in enumerate((o.ln1g, o.ln1b, o.ln2g, o.ln2b, o.b_out, o.b_down)):
            ref[row, :] = sa[pos : pos + 1, :]
        for k in range(3):
            o.w_in[l, k] = wo[:, k * C : (k + 1) * C]
            o.b_in[k, row, :] = sc[k : k + 1, :]
            o.cb[k, row, :] = sc[12 + k : 13 + k, :]
        for k in range(9):
            o.cw[k, row, :] = sc[3 + k : 4 + k, :]
        o.w_out[l] = wo[:, 3 * C : 4 * C].T
        for r in range(z.EMB):
            o.fw1[r, row, :] = sf[r : r + 1, :]
        o.fw2[l] = sf[z.EP : at, :]
        o.fb1[row, :] = sf[at : at + 1, :]
        o.fb2[row, :] = sf[at + 1 : at + 2, :]
        o.freq[l] = sf[at + 2 : at + 4, :]
        o.fw3[l] = sc[ROW_W3 : z.CROWS, :]
        o.decay[row, :] = sc[ROW_DECAY : ROW_DECAY + 1, :]
        o.skip[row, :] = sc[ROW_SKIP : ROW_SKIP + 1, :]
        o.w_up[l] = ffo[0 : z.FFs, :]
        o.w_down[l] = ffo[z.FFs : 2 * z.FFs, :]
        o.b_up[row, :] = ffo[2 * z.FFs : 2 * z.FFs + 1, 0 : z.FFs]


FINAL = (
    "out", "gin", "ln1g", "ln1b", "w_in", "b_in", "cw", "cb", "fw1", "fb1", "fw2", "fb2", "freq", "fw3",
    "decay", "skip", "w_out", "b_out", "ln2g", "ln2b", "w_up", "b_up", "w_down", "b_down",
)


def fused_local(z, *args):
    (inputs, cotangent, lengths, ln1_gain, ln1_bias, w_in, b_in, conv_weight, conv_bias, filt_w1,
     filt_b1, filt_w2, filt_b2, filt_freq, filt_w3, decay_rate, skip_gain, w_out, b_out, ln2_gain,
     ln2_bias, w_up, b_up, w_down, b_down) = args
    L, D, C, T, FFs, FILT = z.L, z.D, z.C, z.T, z.FFs, z.FILT
    lag = np.arange(T) / T
    bands = np.arange(1, z.EMB // 2 + 1)
    phases = 2.0 * math.pi * lag[:, None] * bands[None, :]
    emb = np.concatenate([lag[:, None], np.cos(phases), np.sin(phases)], axis=1)
    emb = np.pad(emb, ((0, 0), (0, z.EP - z.EMB))).astype(np.float32)
    def tables(length, copies):
        turn = (np.arange(length) * 2 + 1)[:, None] * np.arange(length)[None, :] % (4 * length)
        turn = turn * (math.pi / (2 * length))
        pair = [np.kron(np.eye(copies), f(turn)) for f in (np.cos, np.sin)]
        there = np.stack(pair).astype(jnp.bfloat16)
        back = np.stack([m.T for m in pair]).astype(jnp.bfloat16)
        return jnp.asarray(there), jnp.asarray(back)

    values = (
        inputs, cotangent, lengths, ln1_gain, ln1_bias, jnp.transpose(w_in, (0, 2, 3, 1)),
        jnp.swapaxes(b_in, 0, 1), jnp.transpose(conv_weight, (1, 2, 0, 3)).reshape(9, L, C),
        jnp.swapaxes(conv_bias, 0, 1), jnp.asarray(emb), jnp.swapaxes(filt_w1, 0, 1), filt_b1, filt_w2, filt_b2,
        filt_freq, filt_w3, decay_rate, skip_gain, w_out, b_out, ln2_gain, ln2_bias,
        jnp.swapaxes(w_up, 1, 2), b_up, w_down, b_down, *tables(T, 1), *tables(z.TL, z.SL - 1),
    )
    shapes, sems, _, _ = scratch_shapes(z)
    names = INPUTS + OUTPUTS + tuple(shapes) + ("ssem", "rsem", "lsem")
    f32 = lambda *dims: jax.ShapeDtypeStruct(dims, F32)
    outs = (f32(z.places()[3] + 2 * z.R, D),)
    vmem = pl.BlockSpec(memory_space=pltpu.VMEM)
    place = {"lens": pltpu.SMEM, "w_in": pl.ANY, "w_out": pl.ANY}
    specs = [pl.BlockSpec(memory_space=place.get(name, pltpu.VMEM)) for name in INPUTS]
    (packed,) = pl.pallas_call(
        functools.partial(fused_kernel, z, names),
        out_shape=outs,
        in_specs=specs,
        out_specs=[vmem] * len(outs),
        scratch_shapes=[pltpu.VMEM(*spec) for spec in shapes.values()]
        + [
            pltpu.SemaphoreType.DMA((sems,)),
            pltpu.SemaphoreType.DMA((sems,)),
            pltpu.SemaphoreType.DMA((L,)),
        ],
        compiler_params=pltpu.CompilerParams(
            collective_id=0, has_side_effects=True, vmem_limit_bytes=VMEM_LIMIT
        ),
        name="hyena_layers",
    )(*values)
    final = dict(
        out=f32(z.R, D), gin=f32(z.R, D),
        ln1g=f32(L, D), ln1b=f32(L, D), w_in=f32(L, 3, z.DB, C), b_in=f32(3, L, C),
        cw=f32(9, L, C), cb=f32(3, L, C), fw1=f32(z.EMB, L, FILT), fb1=f32(L, FILT),
        fw2=f32(L, FILT, FILT), fb2=f32(L, FILT), freq=f32(L, 2, FILT), fw3=f32(L, FILT, C),
        decay=f32(L, C), skip=f32(L, C), w_out=f32(L, C, z.DB), b_out=f32(L, D),
        ln2g=f32(L, D), ln2b=f32(L, D), w_up=f32(L, FFs, D), b_up=f32(L, FFs),
        w_down=f32(L, FFs, D), b_down=f32(L, D),
    )
    res = pl.pallas_call(
        functools.partial(finish_kernel, z),
        out_shape=tuple(final[name] for name in FINAL),
        in_specs=[pl.BlockSpec(memory_space=pl.ANY)],
        out_specs=[vmem] * len(FINAL),
        scratch_shapes=[pltpu.VMEM(packed.shape, F32), pltpu.SemaphoreType.DMA],
        compiler_params=pltpu.CompilerParams(vmem_limit_bytes=40 * 1024 * 1024),
        name="hyena_unpack",
    )(packed)
    g = types.SimpleNamespace(**dict(zip(FINAL, res)))
    return (
        g.out, g.gin, g.ln1g, g.ln1b, jnp.swapaxes(g.w_in, 1, 2), jnp.swapaxes(g.b_in, 0, 1),
        jnp.transpose(g.cw.reshape(3, 3, L, C), (2, 0, 1, 3)), jnp.swapaxes(g.cb, 0, 1),
        jnp.swapaxes(g.fw1, 0, 1), g.fb1, g.fw2, g.fb2, g.freq, g.fw3, g.decay, g.skip, g.w_out,
        g.b_out, g.ln2g, g.ln2b, jnp.swapaxes(g.w_up, 1, 2), g.b_up, g.w_down, g.b_down,
    )


def local_any(mesh, *args):
    z = Sizes(
        mesh.shape["dp"], mesh.shape["tensor"], args[0].shape[0], args[0].shape[1],
        args[5].shape[3], args[21].shape[2], args[2].shape[1], args[5].shape[0],
        args[9].shape[1], args[9].shape[2],
    )
    return fused_local(z, *args) if z.fits() else local(*args)


def solution(mesh):
    in_specs = (
        P(("dp", "tensor"), None),
        P(("dp", "tensor"), None),
        P("dp", None),
        P(),
        P(),
        P(None, None, None, "tensor"),
        P(None, None, "tensor"),
        P(None, None, None, "tensor"),
        P(None, None, "tensor"),
        P(),
        P(),
        P(),
        P(),
        P(),
        P(None, None, "tensor"),
        P(None, "tensor"),
        P(None, "tensor"),
        P(None, "tensor", None),
        P(),
        P(),
        P(),
        P(None, None, ("dp", "tensor")),
        P(None, ("dp", "tensor")),
        P(None, ("dp", "tensor"), None),
        P(),
    )
    out_specs = (
        P(("dp", "tensor"), None),
        P(("dp", "tensor"), None),
        P(),
        P(),
        P(None, "dp", None, "tensor"),
        P(None, None, "tensor"),
        P(None, None, None, "tensor"),
        P(None, None, "tensor"),
        P(),
        P(),
        P(),
        P(),
        P(),
        P(None, None, "tensor"),
        P(None, "tensor"),
        P(None, "tensor"),
        P(None, "tensor", "dp"),
        P(),
        P(),
        P(),
        P(None, None, ("dp", "tensor")),
        P(None, ("dp", "tensor")),
        P(None, ("dp", "tensor"), None),
        P(),
    )
    return jax.shard_map(functools.partial(local_any, mesh), mesh=mesh, in_specs=in_specs, out_specs=out_specs, check_vma=False)
```

```python
import functools
import math
import types

import jax
import jax.numpy as jnp
import numpy as np
from jax import lax
from jax.experimental import pallas as pl
from jax.experimental.pallas import tpu as pltpu
from jax.sharding import PartitionSpec as P

NORM_EPS = 1e-05
PRECISE = lax.Precision.HIGHEST


def layer_norm(values, norm_gain, norm_shift):
    center = values - jnp.mean(values, axis=-1, keepdims=True)
    spread = jnp.mean(center * center, axis=-1, keepdims=True)
    return center * lax.rsqrt(spread + NORM_EPS) * norm_gain + norm_shift


def filter_taps(w_first, b_first, w_second, b_second, freq_pair, w_third, decay_row, length):
    lag_pos = jnp.arange(length).astype(jnp.float32)
    fraction = lag_pos / length
    band_ids = jnp.arange(1, w_first.shape[0] // 2 + 1).astype(jnp.float32)
    phases = 2.0 * math.pi * fraction[:, None] * band_ids[None, :]
    embedding = jnp.concatenate([fraction[:, None], jnp.cos(phases), jnp.sin(phases)], axis=1)
    layer_one = jnp.sin(freq_pair[0] * (jnp.dot(embedding, w_first, precision=PRECISE) + b_first))
    layer_two = jnp.sin(freq_pair[1] * (jnp.dot(layer_one, w_second, precision=PRECISE) + b_second))
    return jnp.dot(layer_two, w_third, precision=PRECISE) * jnp.exp(
        -lag_pos[:, None] * decay_row[None, :]
    )


def segment_ids(lens_row, length):
    places = jnp.arange(length)
    ends = jnp.cumsum(lens_row)
    return jnp.sum((places[:, None] >= ends[None, :-1]).astype(jnp.int32), axis=1)


def short_conv(projected, weight_short, bias_short, seg_ids):
    summed = bias_short[None] + weight_short[0][None] * projected
    for offset in (1, 2):
        shifted = jnp.concatenate(
            [jnp.zeros((offset,) + projected.shape[1:], jnp.float32), projected[:-offset]], axis=0
        )
        earlier = jnp.concatenate([jnp.full((offset,), -1, jnp.int32), seg_ids[:-offset]], axis=0)
        within = (earlier == seg_ids).astype(jnp.float32)
        summed = summed + weight_short[offset][None] * shifted * within[:, None, None]
    return summed


def trig_table(count_rows, count_cols, modulus):
    product = jnp.arange(count_rows)[:, None] * jnp.arange(count_cols)[None, :] % modulus
    phases = product.astype(jnp.float32) * (2.0 * math.pi / modulus)
    return (jnp.cos(phases), jnp.sin(phases))


def forward_dft(signal, tables):
    cos_a, sin_a, cos_t, sin_t, cos_b, sin_b = tables
    shaped = signal.reshape(cos_a.shape[0], cos_b.shape[0], signal.shape[1])
    real_one = jnp.einsum("abc,ak->kbc", shaped, cos_a, precision=PRECISE)
    imag_one = -jnp.einsum("abc,ak->kbc", shaped, sin_a, precision=PRECISE)
    turn_re = cos_t[:, :, None]
    turn_im = sin_t[:, :, None]
    real_two = real_one * turn_re + imag_one * turn_im
    imag_two = imag_one * turn_re - real_one * turn_im
    real_out = jnp.einsum("kbc,bj->kjc", real_two, cos_b, precision=PRECISE) + jnp.einsum(
        "kbc,bj->kjc", imag_two, sin_b, precision=PRECISE
    )
    imag_out = jnp.einsum("kbc,bj->kjc", imag_two, cos_b, precision=PRECISE) - jnp.einsum(
        "kbc,bj->kjc", real_two, sin_b, precision=PRECISE
    )
    return (real_out, imag_out)


def inverse_dft(real_in, imag_in, tables):
    cos_a, sin_a, cos_t, sin_t, cos_b, sin_b = tables
    real_one = jnp.einsum("kjc,bj->kbc", real_in, cos_b, precision=PRECISE) - jnp.einsum(
        "kjc,bj->kbc", imag_in, sin_b, precision=PRECISE
    )
    imag_one = jnp.einsum("kjc,bj->kbc", imag_in, cos_b, precision=PRECISE) + jnp.einsum(
        "kjc,bj->kbc", real_in, sin_b, precision=PRECISE
    )
    turn_re = cos_t[:, :, None]
    turn_im = sin_t[:, :, None]
    real_two = real_one * turn_re - imag_one * turn_im
    imag_two = imag_one * turn_re + real_one * turn_im
    shaped = jnp.einsum("kbc,ak->abc", real_two, cos_a, precision=PRECISE) - jnp.einsum(
        "kbc,ak->abc", imag_two, sin_a, precision=PRECISE
    )
    total_len = 2 * shaped.shape[0] * shaped.shape[1]
    return shaped.reshape(shaped.shape[0] * shaped.shape[1], shaped.shape[2]) / total_len


def local(
    inputs,
    cotangent,
    lengths,
    ln1_gain,
    ln1_bias,
    w_in,
    b_in,
    conv_weight,
    conv_bias,
    filt_w1,
    filt_b1,
    filt_w2,
    filt_b2,
    filt_freq,
    filt_w3,
    decay_rate,
    skip_gain,
    w_out,
    b_out,
    ln2_gain,
    ln2_bias,
    w_up,
    b_up,
    w_down,
    b_down,
):
    rows_dev = inputs.shape[0]
    tensor_size = lax.axis_size("tensor")
    group_len = rows_dev * tensor_size
    layer_count = w_in.shape[0]
    seg_ids = segment_ids(lengths[0], group_len)
    masks_seq = tuple(
        ((seg_ids == seq_pos).astype(jnp.float32) for seq_pos in range(lengths.shape[1]))
    )
    full_len = 2 * group_len
    fold_a = math.gcd(full_len, 128)
    fold_b = full_len // fold_a
    cos_a, sin_a = trig_table(fold_a // 2, fold_a, fold_a)
    cos_t, sin_t = trig_table(fold_a, fold_b, full_len)
    cos_b, sin_b = trig_table(fold_b, fold_b, fold_b)
    tables = (cos_a, sin_a, cos_t, sin_t, cos_b, sin_b)

    def mixer_local(
        projected,
        weight_short,
        bias_short,
        fw_one,
        fb_one,
        fw_two,
        fb_two,
        freq_pair,
        fw_three,
        decay_row,
        skip_row,
    ):
        gated = short_conv(projected, weight_short, bias_short, seg_ids)
        taps_long = filter_taps(
            fw_one, fb_one, fw_two, fb_two, freq_pair, fw_three, decay_row, group_len
        )
        filt_re, filt_im = forward_dft(taps_long, tables)
        mixed_in = gated[:, 2] * gated[:, 1]
        result = skip_row * mixed_in
        for mask_one in masks_seq:
            sig_re, sig_im = forward_dft(mixed_in * mask_one[:, None], tables)
            result = result + mask_one[:, None] * inverse_dft(
                sig_re * filt_re - sig_im * filt_im, sig_re * filt_im + sig_im * filt_re, tables
            )
        return result * gated[:, 0]

    kept_list = []
    current = inputs
    for layer_idx in range(layer_count):
        normed, norm_back = jax.vjp(layer_norm, current, ln1_gain[layer_idx], ln1_bias[layer_idx])
        normed_full = lax.all_gather(normed.astype(jnp.bfloat16), "tensor", axis=0, tiled=True)
        projected = (
            jnp.einsum(
                "td,dkc->tkc", normed_full, w_in[layer_idx], preferred_element_type=jnp.float32
            )
            + b_in[layer_idx]
        )
        mixer_val, mixer_back = jax.vjp(
            mixer_local,
            projected,
            conv_weight[layer_idx],
            conv_bias[layer_idx],
            filt_w1[layer_idx],
            filt_b1[layer_idx],
            filt_w2[layer_idx],
            filt_b2[layer_idx],
            filt_freq[layer_idx],
            filt_w3[layer_idx],
            decay_rate[layer_idx],
            skip_gain[layer_idx],
        )
        mixer_low = mixer_val.astype(jnp.bfloat16)
        weight_out = w_out[layer_idx]
        keep_out = lax.all_to_all(mixer_low, "tensor", split_axis=0, concat_axis=1, tiled=True)
        weight_out = lax.all_gather(weight_out, "tensor", axis=0, tiled=True)
        branch_out = jnp.dot(keep_out, weight_out, preferred_element_type=jnp.float32)
        middle = current + branch_out + b_out[layer_idx]
        normed_two, norm_two_back = jax.vjp(
            layer_norm, middle, ln2_gain[layer_idx], ln2_bias[layer_idx]
        )
        normed_two_low = normed_two.astype(jnp.bfloat16)
        up_full, upb_full, down_full = (
            lax.all_gather(w_up[layer_idx], ("dp", "tensor"), axis=1, tiled=True),
            lax.all_gather(b_up[layer_idx], ("dp", "tensor"), axis=0, tiled=True),
            lax.all_gather(w_down[layer_idx], ("dp", "tensor"), axis=0, tiled=True),
        )
        hidden_pre = jnp.dot(
            normed_two_low, up_full, preferred_element_type=jnp.float32
        ) + upb_full.astype(jnp.float32)
        hidden_act, gelu_back = jax.vjp(jax.nn.gelu, hidden_pre)
        hidden_low = hidden_act.astype(jnp.bfloat16)
        current = (
            middle
            + jnp.dot(hidden_low, down_full, preferred_element_type=jnp.float32)
            + b_down[layer_idx]
        )
        kept_list.append(
            (
                norm_back,
                normed_full,
                mixer_back,
                keep_out,
                weight_out,
                norm_two_back,
                normed_two_low,
                None,
                None,
                hidden_low,
                gelu_back,
            )
        )
    grad_rows = cotangent
    per_layer = [None] * layer_count
    for layer_idx in reversed(range(layer_count)):
        (
            norm_back,
            normed_full,
            mixer_back,
            keep_out,
            weight_out,
            norm_two_back,
            normed_two_low,
            up_full,
            down_full,
            hidden_low,
            gelu_back,
        ) = kept_list[layer_idx]
        up_full, down_full = (
            lax.all_gather(w_up[layer_idx], ("dp", "tensor"), axis=1, tiled=True),
            lax.all_gather(w_down[layer_idx], ("dp", "tensor"), axis=0, tiled=True),
        )
        down_low = grad_rows.astype(jnp.bfloat16)
        grad_b_down = jnp.sum(down_low.astype(jnp.float32), axis=0)
        grad_w_down = jnp.einsum(
            "tf,td->fd", hidden_low, down_low, preferred_element_type=jnp.float32
        )
        grad_hidden = jnp.einsum(
            "td,fd->tf", down_low, down_full, preferred_element_type=jnp.float32
        )
        (grad_pre,) = gelu_back(grad_hidden)
        pre_low = grad_pre.astype(jnp.bfloat16)
        grad_w_up = jnp.einsum(
            "td,tf->df", normed_two_low, pre_low, preferred_element_type=jnp.float32
        )
        grad_b_up = jnp.sum(pre_low.astype(jnp.float32), axis=0)
        grad_normed_two = jnp.einsum(
            "tf,df->td", pre_low, up_full, preferred_element_type=jnp.float32
        )
        shard_w_up, shard_b_up, shard_w_down = (
            lax.psum_scatter(grad_w_up, ("dp", "tensor"), scatter_dimension=1, tiled=True),
            lax.psum_scatter(grad_b_up, ("dp", "tensor"), scatter_dimension=0, tiled=True),
            lax.psum_scatter(grad_w_down, ("dp", "tensor"), scatter_dimension=0, tiled=True),
        )
        grad_middle_ln, grad_ln2_gain, grad_ln2_bias = norm_two_back(grad_normed_two)
        grad_middle = grad_rows + grad_middle_ln
        out_low = grad_middle.astype(jnp.bfloat16)
        grad_b_out = jnp.sum(out_low.astype(jnp.float32), axis=0)
        grad_rows_mixed = jnp.einsum(
            "td,cd->tc", out_low, weight_out, preferred_element_type=jnp.float32
        )
        grad_mixed = lax.all_to_all(
            grad_rows_mixed.astype(jnp.bfloat16), "tensor", split_axis=1, concat_axis=0, tiled=True
        ).astype(grad_rows_mixed.dtype)
        grad_w_out = lax.psum_scatter(
            jnp.einsum("tc,td->cd", keep_out, out_low, preferred_element_type=jnp.float32).astype(
                jnp.bfloat16
            ),
            "tensor",
            scatter_dimension=0,
            tiled=True,
        ).astype(jnp.float32)
        grads_mixer = mixer_back(grad_mixed)
        proj_low = grads_mixer[0].astype(jnp.bfloat16)
        grad_w_in = jnp.einsum(
            "td,tkc->dkc", normed_full, proj_low, preferred_element_type=jnp.float32
        )
        grad_b_in = jnp.sum(proj_low.astype(jnp.float32), axis=0)
        weight_in = w_in[layer_idx]
        grad_normed = lax.psum_scatter(
            jnp.einsum(
                "tkc,dkc->td", proj_low, weight_in, preferred_element_type=jnp.float32
            ).astype(jnp.bfloat16),
            "tensor",
            scatter_dimension=0,
            tiled=True,
        ).astype(jnp.float32)
        grad_in_ln, grad_ln1_gain, grad_ln1_bias = norm_back(grad_normed)
        grad_rows = grad_middle + grad_in_ln
        per_layer[layer_idx] = (
            grad_ln1_gain,
            grad_ln1_bias,
            grad_w_in,
            grad_b_in,
            grads_mixer[1],
            grads_mixer[2],
            grads_mixer[3],
            grads_mixer[4],
            grads_mixer[5],
            grads_mixer[6],
            grads_mixer[7],
            grads_mixer[8],
            grads_mixer[9],
            grads_mixer[10],
            grad_w_out,
            grad_b_out,
            grad_ln2_gain,
            grad_ln2_bias,
            shard_w_up,
            shard_b_up,
            shard_w_down,
            grad_b_down,
        )
    stacks = [
        jnp.stack([per_layer[layer_pos][slot_pos] for layer_pos in range(layer_count)])
        for slot_pos in range(22)
    ]
    shared_done = lax.psum(
        (
            stacks[0],
            stacks[1],
            stacks[6],
            stacks[7],
            stacks[8],
            stacks[9],
            stacks[10],
            stacks[15],
            stacks[16],
            stacks[17],
            stacks[21],
        ),
        ("dp", "tensor"),
    )
    weight_done = (
        lax.psum_scatter(
            stacks[2].astype(jnp.bfloat16), "dp", scatter_dimension=1, tiled=True
        ).astype(jnp.float32),
        lax.psum_scatter(
            stacks[14].astype(jnp.bfloat16), "dp", scatter_dimension=2, tiled=True
        ).astype(jnp.float32),
    )
    group_done = (
        lax.psum(stacks[3].astype(jnp.bfloat16), "dp").astype(jnp.float32),
        lax.psum(stacks[4].astype(jnp.bfloat16), "dp").astype(jnp.float32),
        lax.psum(stacks[5].astype(jnp.bfloat16), "dp").astype(jnp.float32),
        lax.psum(stacks[11].astype(jnp.bfloat16), "dp").astype(jnp.float32),
        lax.psum(stacks[12].astype(jnp.bfloat16), "dp").astype(jnp.float32),
        lax.psum(stacks[13].astype(jnp.bfloat16), "dp").astype(jnp.float32),
    )
    return (
        current,
        grad_rows,
        shared_done[0],
        shared_done[1],
        weight_done[0],
        group_done[0],
        group_done[1],
        group_done[2],
        shared_done[2],
        shared_done[3],
        shared_done[4],
        shared_done[5],
        shared_done[6],
        group_done[3],
        group_done[4],
        group_done[5],
        weight_done[1],
        shared_done[7],
        shared_done[8],
        shared_done[9],
        stacks[18],
        stacks[19],
        stacks[20],
        shared_done[10],
    )


BF16 = jnp.bfloat16
F32 = jnp.float32
MESH = pl.DeviceIdType.MESH
SHARE = 4
GELU_C = math.sqrt(2.0 / math.pi)
GELU_A = 0.044715
VMEM_LIMIT = 63 * 1024 * 1024
ROW_DECAY, ROW_SKIP, ROW_ENDS, ROW_W3 = 15, 16, 17, 24


def dot_nn(a, b, precision=None):
    return lax.dot_general(
        a, b, (((1,), (0,)), ((), ())), precision=precision, preferred_element_type=F32
    )


def dot_nt(a, b, precision=None):
    return lax.dot_general(
        a, b, (((1,), (1,)), ((), ())), precision=precision, preferred_element_type=F32
    )


def dot_tn(a, b, precision=None):
    return lax.dot_general(
        a, b, (((0,), (0,)), ((), ())), precision=precision, preferred_element_type=F32
    )


class Sizes:
    def __init__(self, mesh_dp, mesh_tp, rows, width, chan, shard, slots, layers, emb, filt):
        self.ndp, self.n = mesh_dp, mesh_tp
        self.R, self.D, self.C = rows, width, chan
        self.T = rows * mesh_tp
        self.FFs = shard
        self.FR = 2 * shard + 16
        self.Y = mesh_dp // SHARE
        self.FB = mesh_tp * shard
        self.SL, self.L = slots, layers
        self.EMB, self.FILT = emb, filt
        self.EP = -(-emb // 8) * 8
        self.DB = width // mesh_dp
        self.DP = 4 * chan // mesh_dp
        self.PK = mesh_dp // 4
        self.TL = rows // 2
        self.FROWS = self.EP + filt + 8
        self.LF = layers * filt
        self.CROWS = ROW_W3 + filt

    def places(self):
        at_wo = self.L * self.FR
        at_rows = at_wo + self.L * self.DB
        at_side = at_rows + 8 * self.L
        at_out = at_side + -(-max(self.FROWS, self.CROWS) // 8) * 8
        return at_wo, at_rows, at_side, at_out

    def fits(self):
        return (
            self.n == SHARE
            and self.ndp == 2 * SHARE
            and self.FFs % 16 == 0
            and self.DP % 16 == 0
            and self.FB <= self.D
            and self.SL <= 8
            and self.TL == 64
            and self.LF + (2 * self.L - 1) * self.C <= self.D
            and 4 * self.C <= self.D
            and self.n == 4
            and vmem_bytes(scratch_shapes(self)[0]) < VMEM_LIMIT - 6 * 1024 * 1024
        )


INPUTS = (
    "x", "cot", "lens", "ln1g", "ln1b", "w_in", "b_in", "cw", "cb", "emb", "fw1", "fb1", "fw2",
    "fb2", "freq", "fw3", "decay", "skip", "w_out", "b_out", "ln2g", "ln2b", "w_up", "b_up",
    "w_down", "b_down", "dft", "dftt", "tdft", "tdftt",
)
OUTPUTS = ("pack",)


def scratch_shapes(z):
    R, D, C, T, n, L, Y = z.R, z.D, z.C, z.T, z.n, z.L, z.Y
    steps_dp = z.ndp.bit_length() - 1
    steps = steps_dp + n.bit_length() - 1
    per = 8 * (n - 1) + 8 * (z.ndp - 1) + 56 + n * Y + n * (Y - 1) + (n - 1) + 3 * (n - 1)
    sems = L * (per + 3 * steps + 2) + 8
    shapes = dict(
        xb=((R, D), BF16),
        xv=((R, D), BF16),
        cv=((R, D), BF16),
        ov=((R, D), BF16),
        gv=((R, D), BF16),
        xs=((max(L - 1, 1), R, D), F32),
        mids=((L, R, D), F32),
        gx=((R, D), F32),
        nF=((L, n, R, D), BF16),
        p=((L, 3, T + 8, C), F32),
        inn=((L, T, C), F32),
        innb=((T, C), BF16),
        g0s=((T, C), F32),
        fz=((2, T, z.LF), F32),
        fc=((2, T, z.LF), F32),
        fa=((2, T, z.LF), BF16),
        fw1p=((z.EP, z.LF), F32),
        fw2p=((z.LF, z.LF), F32),
        fw3p=((L, z.LF, C), BF16),
        frow=((8, z.LF), F32),
        taps=((L, T, C), BF16),
        hs=((L, 2, T, C), BF16),
        xf=((L, 2, T, C), BF16),
        yb=((2, T, C), BF16),
        qb=((2, T, C), BF16),
        longs=((L, T, C), F32),
        mx=((L, T, C), BF16),
        pin=((L, ROW_W3, C), F32),
        pv=((L, ROW_W3, C), F32),
        p3=((L, z.FILT, C), BF16),
        v3=((L, z.FILT, C), BF16),
        wz=((L, n, z.DP, D), BF16),
        wfull=((L, z.ndp, z.DP, D), BF16),
        n2S=((L, SHARE, R, D), BF16),
        rowb=((16, D), F32),
        ffw=((L, Y, n, z.FR, D), BF16),
        bup=((L, Y, 8, z.FB), F32),
        hp=((L, Y, SHARE, R, z.FB), BF16),
        spf=((2, SHARE, R // 2, D), F32),
        sp=((2, 3, R // 2, D), BF16),
        sr=((2, 3, R // 2, D), BF16),
        gdS=((L, SHARE, R, D), BF16),
        hb=((Y, SHARE, R, z.FB), BF16),
        gpb=((Y, SHARE, R, z.FB), BF16),
        ffry=((L, Y - 1, n, z.FR, D), BF16),
        ffrz=((L, n - 1, 2, z.FR, D), BF16),
        goF=((n, R, D), BF16),
        gg=((3, T + 8, C), F32),
        gpj=((3, T, C), BF16),
        gl=((T, C), F32),
        gtp=((T, C), F32),
        gtt=((z.TL, C), F32),
        hs64=((L, 2, z.TL, C), F32),
        xt=((L, 2, (z.SL - 1) * z.TL, C), BF16),
        tst=(((z.SL - 1) * z.TL, C), BF16),
        wg=((2, z.ndp, z.DB, 2 * C), BF16),
        wr=((L, 2, Y - 1, SHARE, z.DB, 2 * C), BF16),
        wr1=((L, 2, SHARE, z.DB, 2 * C), BF16),
        wr2=((L, 2, n - 1, z.DB, 2 * C), BF16),
        sa=((L, 8, D), F32),
        sf=((L, z.FROWS, z.LF), F32),
        sc=((L, z.CROWS, C), F32),
        sc0=((L, z.CROWS, C), F32),
        rA=((L, steps_dp, 8, D), F32),
        rF=((L, steps_dp, z.FROWS, z.LF), F32),
        rP=((z.ndp - 1, 8, D), F32),
        rZ=((n - 1, 8, D), F32),
        rAz=((steps - steps_dp, L, 8, D), F32),
        rFz=((steps - steps_dp, z.FROWS, z.LF), F32),
        rC=((L, steps_dp, z.CROWS, C), F32),
    )
    return shapes, sems, steps_dp, steps


def vmem_bytes(shapes):
    total = 0
    for dims, kind in shapes.values():
        size = 2 if kind == BF16 else 4
        sub = 32 // size
        lanes = -(-dims[-1] // 128) * 128
        rows = -(-dims[-2] // sub) * sub
        total += math.prod(dims[:-2]) * rows * lanes * size
    return total


def fused_kernel(z, names, *refs):
    R, D, C, T, n, L, Y, ndp = z.R, z.D, z.C, z.T, z.n, z.L, z.Y, z.ndp
    FFs, FB, FILT, EP, DB, TL, LF = z.FFs, z.FB, z.FILT, z.EP, z.DB, z.TL, z.LF
    s = types.SimpleNamespace(**dict(zip(names, refs)))
    dp = lax.axis_index("dp")
    ti = lax.axis_index("tensor")
    y = dp // SHARE
    a = dp % SHARE
    sib = (dp + 1 - 2 * (dp % 2), ti)
    xnb = (dp + 2 - 4 * ((dp // 2) % 2), ti)
    partner = (SHARE * y + ti, a)
    moved = a != ti
    member = [a, a + 1 - 2 * (a % 2), a + 2 - 4 * (a // 2)]
    member.append(member[1] + 2 - 4 * (member[1] // 2))
    HR = R // 2
    FR = z.FR
    used = [0]
    open_sends = []

    def make(src, dst, dev):
        idx = used[0]
        used[0] += 1
        return pltpu.make_async_remote_copy(
            src_ref=src, dst_ref=dst, send_sem=s.ssem.at[idx], recv_sem=s.rsem.at[idx],
            device_id=dev, device_id_type=MESH,
        )

    def push(src, dst, dev, valid=True):
        copy = make(src, dst, dev)
        if valid is True:
            copy.start()
        else:
            pl.when(valid)(copy.start)
        open_sends.append((copy, valid))
        return copy

    def sent(*copies):
        for item in [p for p in open_sends if any(p[0] is c for c in copies)]:
            if item[1] is True:
                item[0].wait_send()
            else:
                pl.when(item[1])(item[0].wait_send)
        open_sends[:] = [p for p in open_sends if not any(p[0] is c for c in copies)]

    def swap(src, dst):
        copy = make(src, dst, partner)
        pl.when(moved)(copy.start)

        @pl.when(a == ti)
        def _():
            dst[...] = src[...]

        open_sends.append((copy, moved))
        return copy

    def swapped(copy):
        pl.when(moved)(copy.wait_recv)

    def flush():
        sent(*[p[0] for p in open_sends])

    def done(copy):
        copy.wait_recv()

    def piece_copy(l, act):
        k = dp // z.PK
        rows = pl.ds(pl.multiple_of((dp % z.PK) * z.DP, z.DP), z.DP)
        dst = s.wz.at[l, ti]

        @pl.when(k < 3)
        def _():
            getattr(pltpu.make_async_copy(s.w_in.at[l, k, rows], dst, s.lsem.at[l]), act)()

        @pl.when(k >= 3)
        def _():
            getattr(pltpu.make_async_copy(s.w_out.at[l, rows], dst, s.lsem.at[l]), act)()

    for l in range(L):
        piece_copy(l, "start")

    barrier = pltpu.get_barrier_semaphore()
    for d in range(1, ndp):
        pl.semaphore_signal(barrier, inc=1, device_id=((dp + d) % ndp, ti), device_id_type=MESH)
    for d in range(1, n):
        pl.semaphore_signal(barrier, inc=1, device_id=(dp, (ti + d) % n), device_id_type=MESH)

    @pl.when(moved)
    def _():
        pl.semaphore_signal(barrier, inc=1, device_id=partner, device_id_type=MESH)

    s.xb[...] = s.x[...].astype(BF16)

    @pl.when(moved)
    def _():
        pl.semaphore_wait(barrier, ndp - 1 + n)

    @pl.when(a == ti)
    def _():
        pl.semaphore_wait(barrier, ndp - 1 + n - 1)

    def ln_parts(v):
        mu = jnp.mean(v, axis=-1, keepdims=True)
        c = v - mu
        r = lax.rsqrt(jnp.mean(c * c, axis=-1, keepdims=True) + NORM_EPS)
        return c * r, r

    def ln_back(v, gy, gain):
        xhat, r = ln_parts(v)
        gz = gy * gain
        gv = r * (
            gz - jnp.mean(gz, axis=-1, keepdims=True)
            - xhat * jnp.mean(gz * xhat, axis=-1, keepdims=True)
        )
        return gv, jnp.sum(gy * xhat, axis=0, keepdims=True), jnp.sum(gy, axis=0, keepdims=True)

    def chip_rows(i):
        return pl.ds(pl.multiple_of(i * 2 * R, 2 * R), 2 * R)

    def chip_block(ref, i):
        return ref[pl.ds(2 * i, 2)].reshape(2 * R, D)

    def layer_input(l, h):
        return s.xv[half(h), :].astype(F32) if l == 0 else s.xs[l - 1, half(h), :]

    def half(h):
        return pl.ds(h * HR, HR)

    def gather_s(buf, h):
        mine = buf.at[member[0], half(h)]
        to_x = push(mine, mine, xnb)
        to_sib = push(mine, mine, sib)
        yield
        done(to_x)
        other = buf.at[member[2], half(h)]
        onward = push(other, other, sib)
        done(to_sib)
        yield
        done(onward)
        sent(to_x, to_sib, onward)

    def scatter_s(h, block, hook=None):
        s.spf[h] = block().reshape(SHARE, HR, D)
        for chip in range(2):
            s.sp[h, chip] = s.spf[h, 2 * chip + 1 - a % 2].astype(BF16)
        c1 = push(s.sp.at[h, 0:2], s.sr.at[h, 0:2], sib)
        yield
        done(c1)
        far = s.spf[h, member[2]] + s.sr[h, 1 - a // 2].astype(F32)
        s.sp[h, 2] = far.astype(BF16)
        cx = push(s.sp.at[h, 2], s.sr.at[h, 2], xnb)
        if hook:
            hook()
        yield
        near = s.spf[h, a] + s.sr[h, a // 2].astype(F32)
        done(cx)
        sent(c1, cx)
        return near + s.sr[h, 2].astype(F32)

    def weave(*gens):
        gens = list(gens)
        while gens:
            for g in list(gens):
                try:
                    next(g)
                except StopIteration:
                    gens.remove(g)

    def y_peer(e):
        return (((y + e) % Y) * SHARE + a, ti)

    def w_gather(l):
        piece_copy(l, "wait")
        HP = z.DP // 2
        cuts = [pl.ds(h * HP, HP) for h in range(2)]
        order = (2, 1, 3)
        along_z, to_member, along_y = [], [], []
        for cut in cuts:
            own = s.wz.at[l, ti, cut]
            along_z.append([push(own, own, (dp, (ti + d) % n)) for d in range(1, n)])
        yield
        for h, cut in enumerate(cuts):
            for c in along_z[h]:
                done(c)
            to_member.append([])
            for d in order:
                m = (a + d) % SHARE
                to_member[h].append(
                    push(s.wz.at[l, m, cut], s.wfull.at[l, dp, cut], (y * SHARE + m, ti))
                )
            s.wfull[l, dp, cut] = s.wz[l, a, cut]
            mine = s.wfull.at[l, dp, cut]
            along_y += [push(mine, mine, y_peer(e)) for e in range(1, Y)]
            yield
        for h, cut in enumerate(cuts):
            for c, d in zip(to_member[h], order):
                done(c)
                piece = s.wfull.at[l, y * SHARE + (a + SHARE - d) % SHARE, cut]
                along_y += [push(piece, piece, y_peer(e)) for e in range(1, Y)]
            yield
        for c in along_y:
            done(c)
        yield

    def w_mat(l, k):
        return s.wfull[l, z.PK * k : z.PK * (k + 1)].reshape(C, D)

    def ff_gather(l):
        s.ffw[l, y, ti, 0:FFs, :] = s.w_up[l]
        s.ffw[l, y, ti, FFs : 2 * FFs, :] = s.w_down[l]
        s.rowb[...] = jnp.zeros((16, D), F32)
        s.rowb[0:1, 0:FFs] = s.b_up[...].astype(F32)[l : l + 1, :]
        s.ffw[l, y, ti, 2 * FFs : 2 * FFs + 16, :] = s.rowb[...].astype(BF16)
        along_y = []
        hops = []
        hop = None
        for h in range(n):
            low = (ti + n - h) % n
            high = (ti + h) % n
            has_low = ti >= h
            has_high = ti + h < n
            if h:
                pl.when(has_low)(hop[0].wait_recv)
                pl.when(has_high)(hop[1].wait_recv)
            lo, hi = s.ffw.at[l, y, low], s.ffw.at[l, y, high]
            if h < n - 1:
                hop = (
                    push(lo, lo, (dp, (ti + 1) % n), jnp.logical_and(has_low, ti < n - 1)),
                    push(hi, hi, (dp, (ti + n - 1) % n), jnp.logical_and(has_high, ti > 0)),
                )
                hops += hop
            for e in range(1, Y):
                if h == 1:
                    own = s.ffw.at[l, y, ti]
                    along_y.append((push(own, own, y_peer(e)), True))
                if h:
                    along_y.append((push(lo, lo, y_peer(e), has_low), has_low))
                    along_y.append((push(hi, hi, y_peer(e), has_high), has_high))
            yield
        for c, valid in along_y:
            if valid is True:
                done(c)
            else:
                pl.when(valid)(c.wait_recv)
        sent(*hops, *[c for c, _ in along_y])
        ff_ready(l)
        yield

    def ff_ready(l):
        for b in range(Y):
            row = jnp.zeros((16, D), F32)
            for j in range(n):
                part = s.ffw[l, b, j, 2 * FFs : 2 * FFs + 16, :].astype(F32)
                row = row + (pltpu.roll(part, FFs * j, 1) if j else part)
            s.bup[l, b] = row[:8, :FB]

    def ff_up(l, b):
        return s.ffw[l, b, :, 0:FFs, :].reshape(FB, D)

    def ff_down(l, b):
        return s.ffw[l, b, :, FFs : 2 * FFs, :].reshape(FB, D)

    CH = 64
    ENDS = range(z.SL - 1)

    def end_row(k):
        return s.pv[0, ROW_ENDS + k : ROW_ENDS + k + 1, :]

    def chunk_masks(r0, rows):
        t = (lax.broadcasted_iota(jnp.int32, (rows, C), 0) + r0).astype(F32)
        m1 = jnp.ones((rows, C), F32)
        for k in ENDS:
            m1 = jnp.where(t == end_row(k), 0.0, m1)
        m2 = m1
        for k in ENDS:
            m2 = jnp.where(t == end_row(k) + 1.0, 0.0, m2)
        return m1, m2

    def conv_row(l, step, k):
        return s.pv[l, 3 + step * 3 + k : 4 + step * 3 + k, :]

    def shifted(l, k, r0, masks):
        blk = s.p[l, k, pl.ds(r0, CH + 8), :]
        if masks is None:
            return blk[8:], blk[7:-1], blk[6:-2]
        return blk[8:], blk[7:-1] * masks[0], blk[6:-2] * masks[1]

    LAST = T // CH - 1

    def each_chunk(step):
        @pl.loop(0, LAST)
        def _(i):
            step(pl.multiple_of(i * CH, CH), None)

        step(LAST * CH, chunk_masks(LAST * CH, CH))

    def gate(l, k, parts):
        return (
            s.pv[l, 12 + k : 13 + k, :]
            + conv_row(l, 0, k) * parts[0]
            + conv_row(l, 1, k) * parts[1]
            + conv_row(l, 2, k) * parts[2]
        )

    def lag_rows():
        return lax.broadcasted_iota(jnp.int32, (T, C), 0).astype(F32)

    def decay_row(l):
        return s.pv[l, ROW_DECAY : ROW_DECAY + 1, :]

    def skip_row(l):
        return s.pv[l, ROW_SKIP : ROW_SKIP + 1, :]

    def filter_net():
        s.fw1p[...] = jnp.zeros((EP, LF), F32)
        s.fw2p[...] = jnp.zeros((LF, LF), F32)
        for l in range(L):
            at = slice(l * FILT, (l + 1) * FILT)
            row = slice(l, l + 1)
            for r in range(z.EMB):
                s.fw1p[r : r + 1, at] = s.fw1[r, row, :]
            s.fw2p[at, at] = s.fw2[l]
            s.frow[0:1, at] = s.fb1[row, :]
            s.frow[1:2, at] = s.fb2[row, :]
            s.frow[2:4, at] = s.freq[l]
        z1 = dot_nn(s.emb[...], s.fw1p[...], PRECISE) + s.frow[0:1, :]
        u1 = s.frow[2:3, :] * z1
        a1 = jnp.sin(u1)
        s.fz[0] = z1
        s.fa[0] = a1.astype(BF16)
        s.fc[0] = jnp.cos(u1)
        z2 = dot_nn(a1, s.fw2p[...], PRECISE) + s.frow[1:2, :]
        u2 = s.frow[3:4, :] * z2
        s.fz[1] = z2
        s.fa[1] = jnp.sin(u2).astype(BF16)
        s.fc[1] = jnp.cos(u2)

    def filter_taps_of(l):
        s.fw3p[l] = jnp.zeros((LF, C), BF16)
        s.fw3p[l, l * FILT : (l + 1) * FILT, :] = s.v3[l]
        tp = dot_nn(s.fa[1], s.fw3p[l]) * jnp.exp(-lag_rows() * decay_row(l))
        s.innb[...] = tp.astype(BF16)
        s.taps[l] = s.innb[...]
        s.hs64[l, 0] = dot_nn(s.tdft[0, 0:TL, 0:TL], s.innb[0:TL, :])
        s.hs64[l, 1] = dot_nn(s.tdft[1, 0:TL, 0:TL], s.innb[0:TL, :])

        @pl.loop(0, n // 2)
        def _(i):
            rows = chip_rows(i)
            s.hs[l, 0, rows, :] = dot_nn(s.dft[0, rows, :], s.innb[...]).astype(BF16)
            s.hs[l, 1, rows, :] = dot_nn(s.dft[1, rows, :], s.innb[...]).astype(BF16)

    def tail_masks():
        t = lax.broadcasted_iota(jnp.int32, (TL, C), 0).astype(F32) + float(T - TL)
        masks = []
        for k in ENDS:
            live = t >= end_row(k)
            if k + 1 < z.SL - 1:
                live = jnp.logical_and(live, t < end_row(k + 1))
            masks.append(live.astype(F32))
        return masks, t < end_row(0)

    def tail_spectrum(rows, masks):
        for k, mask in enumerate(masks):
            s.tst[k * TL : (k + 1) * TL, :] = (rows * mask).astype(BF16)
        return dot_nn(s.tdft[0], s.tst[...]), dot_nn(s.tdft[1], s.tst[...])

    def tail_back(re, im):
        res = dot_nn(s.tdftt[0], re.astype(BF16)) + dot_nn(s.tdftt[1], im.astype(BF16))
        res = res * (1.0 / TL)
        return [res[k * TL : (k + 1) * TL] for k in ENDS]

    def tail_filter(l, part):
        one = s.hs64[l, part]
        return jnp.concatenate([one] * len(ENDS), axis=0)

    def project(l, h):
        rows = s.nF[l, :, half(h), :].reshape(SHARE * HR, D)
        for k in range(3):
            if h == 0:
                s.p[l, k, 0:8, :] = jnp.zeros((8, C), F32)
            res = dot_nt(rows, w_mat(l, k)) + s.pv[l, k : k + 1, :]
            for m in range(SHARE):
                lo = 8 + m * R + h * HR
                s.p[l, k, lo : lo + HR, :] = res[m * HR : (m + 1) * HR]

    def mixer_forward(l, tick):
        def step(r0, masks):
            g0 = gate(l, 0, shifted(l, 0, r0, masks))
            g1 = gate(l, 1, shifted(l, 1, r0, masks))
            g2 = gate(l, 2, shifted(l, 2, r0, masks))
            inner = g2 * g1
            s.g0s[pl.ds(r0, CH), :] = g0
            s.inn[l, pl.ds(r0, CH), :] = inner
            s.innb[pl.ds(r0, CH), :] = inner.astype(BF16)

        each_chunk(step)

        @pl.loop(0, n // 2)
        def _(i):
            rows = chip_rows(i)
            xr = dot_nn(s.dft[0, rows, :], s.innb[...])
            xi = dot_nn(s.dft[1, rows, :], s.innb[...])
            hr = s.hs[l, 0, rows, :].astype(F32)
            hi = s.hs[l, 1, rows, :].astype(F32)
            s.xf[l, 0, rows, :] = xr.astype(BF16)
            s.xf[l, 1, rows, :] = xi.astype(BF16)
            s.yb[0, rows, :] = (xr * hr - xi * hi).astype(BF16)
            s.yb[1, rows, :] = (xr * hi + xi * hr).astype(BF16)

        masks, first = tail_masks()
        xr, xi = tail_spectrum(s.inn[l, T - TL : T, :], masks)
        s.xt[l, 0] = xr.astype(BF16)
        s.xt[l, 1] = xi.astype(BF16)
        hr, hi = tail_filter(l, 0), tail_filter(l, 1)
        parts = tail_back(xr * hr - xi * hi, xr * hi + xi * hr)
        tail = parts[0] * masks[0]
        for part, mask in zip(parts[1:], masks[1:]):
            tail = tail + part * mask
        s.gtt[...] = tail

        @pl.loop(0, n // 2)
        def _(i):
            rows = chip_rows(i)
            s.longs[l, rows, :] = (
                dot_nn(s.dftt[0, rows, :], s.yb[0]) + dot_nn(s.dftt[1, rows, :], s.yb[1])
            ) * (1.0 / T)
        s.longs[l, T - TL : T, :] = jnp.where(first, s.longs[l, T - TL : T, :], s.gtt[...])

        @pl.loop(0, n // 2)
        def _(i):
            rows = chip_rows(i)
            lg = s.longs[l, rows, :] + skip_row(l) * s.inn[l, rows, :]
            s.longs[l, rows, :] = lg
            s.mx[l, rows, :] = (lg * s.g0s[rows, :]).astype(BF16)
        tick()

    def gelu_tanh(v):
        return jnp.tanh(GELU_C * (v + GELU_A * v * v * v))

    def ff_block(l, h):
        v = s.n2S[l, :, half(h), :].reshape(SHARE * HR, D)
        acc = jnp.zeros((SHARE * HR, D), F32)
        for b in range(Y):
            pre = dot_nt(v, ff_up(l, b)) + s.bup[l, b, 0:1, :]
            s.hp[l, b, :, half(h), :] = pre.astype(BF16).reshape(SHARE, HR, FB)
            act = 0.5 * pre * (1.0 + gelu_tanh(pre))
            acc = acc + dot_nn(act.astype(BF16), ff_down(l, b))
        return acc

    def ff_back_block(l, h):
        g = s.gdS[l, :, half(h), :].reshape(SHARE * HR, D)
        acc = jnp.zeros((SHARE * HR, D), F32)
        for b in range(Y):
            gh = dot_nt(g, ff_down(l, b))
            v = s.hp[l, b, :, half(h), :].reshape(SHARE * HR, FB).astype(F32)
            th = gelu_tanh(v)
            act = (0.5 * v * (1.0 + th)).astype(BF16)
            s.hb[b, :, half(h), :] = act.reshape(SHARE, HR, FB)
            slope = 0.5 * (1.0 + th) + 0.5 * v * (1.0 - th * th) * (
                GELU_C * (1.0 + 3.0 * GELU_A * v * v)
            )
            gp = (gh * slope).astype(BF16)
            s.gpb[b, :, half(h), :] = gp.reshape(SHARE, HR, FB)
            acc = acc + dot_nn(gp, ff_up(l, b))
        return acc

    def ff_scatter(l):
        act = s.n2S[l].reshape(SHARE * R, D)
        gds = s.gdS[l].reshape(SHARE * R, D)

        def fill(b):
            g = s.gpb[b].reshape(SHARE * R, FB)
            h = s.hb[b].reshape(SHARE * R, FB)
            s.ffw[l, b, :, 0:FFs, :] = dot_tn(g, act).astype(BF16).reshape(n, FFs, D)
            s.ffw[l, b, :, FFs : 2 * FFs, :] = dot_tn(h, gds).astype(BF16).reshape(n, FFs, D)
            sums = jnp.sum(g.astype(F32), axis=0, keepdims=True)
            row = jnp.concatenate([sums, jnp.zeros((1, D - FB), F32)], axis=1) if D > FB else sums
            row = jnp.broadcast_to(row, (16, D))
            for j in range(n):
                part = pltpu.roll(row, (D - FFs * j) % D, 1) if j else row
                s.ffw[l, b, j, 2 * FFs : 2 * FFs + 16, :] = part.astype(BF16)

        order = [3 * (1 - ti // 2), (2 + 3 * ti) % 5, 1 + ti % 2, ti]
        along_y = []
        for e in range(1, Y):
            b = (y + e) % Y
            fill(b)
            for j in order:
                along_y.append(push(s.ffw.at[l, b, j], s.ffry.at[l, e - 1, j], y_peer(e)))
        fill(y)
        yield
        hop = None
        hops = []
        for pos, j in enumerate(order):
            acc = s.ffw[l, y, j].astype(F32)
            for e in range(1, Y):
                done(along_y[(e - 1) * n + pos])
                acc = acc + s.ffry[l, e - 1, j].astype(F32)
            if pos < n - 1:
                s.ffry[l, 0, j] = acc.astype(BF16)
            else:
                s.pack[l * FR : (l + 1) * FR, :] = acc
                sent(*along_y)
            if pos < n - 1:
                d = n - 1 - pos
                new = []
                for side, (valid, inner, to) in enumerate(
                    ((ti + d < n, ti >= 1, ti + 1), (ti >= d, ti < n - 1, ti + n - 1))
                ):
                    j = (ti + d) % n if side == 0 else (ti + n - d) % n
                    if pos:
                        more = jnp.logical_and(valid, inner)
                        pl.when(more)(hop[side].wait_recv)

                        @pl.when(more)
                        def _():
                            s.ffry[l, 0, j] = (
                                s.ffry[l, 0, j].astype(F32) + s.ffrz[l, pos - 1, side].astype(F32)
                            ).astype(BF16)

                    new.append(
                        push(
                            s.ffry.at[l, 0, j], s.ffrz.at[l, pos, side], (dp, to % n), valid
                        )
                    )
                hop = new
                hops += new
            yield
        for side, inner in ((0, ti >= 1), (1, ti < n - 1)):
            pl.when(inner)(hop[side].wait_recv)

            @pl.when(inner)
            def _():
                s.pack[l * FR : (l + 1) * FR, :] = (
                    s.pack[l * FR : (l + 1) * FR, :] + s.ffrz[l, n - 2, side].astype(F32)
                )

        sent(*hops)
        yield

    def mixer_backward(l, ticks):
        def first_step(r0, masks):
            rows = pl.ds(r0, CH)
            g0 = gate(l, 0, shifted(l, 0, r0, masks))
            gm = s.gtp[rows, :]
            glong = gm * g0
            s.gg[0, rows, :] = gm * s.longs[l, rows, :]
            s.gl[rows, :] = glong
            if masks is not None:
                t = (lax.broadcasted_iota(jnp.int32, (CH, C), 0) + r0).astype(F32)
                glong = jnp.where(t < end_row(0), glong, 0.0)
            s.innb[rows, :] = glong.astype(BF16)

        each_chunk(first_step)

        @pl.loop(0, n // 2)
        def _(i):
            rows = chip_rows(i)
            gr = dot_nn(s.dft[0, rows, :], s.innb[...])
            gi = dot_nn(s.dft[1, rows, :], s.innb[...])
            hr = s.hs[l, 0, rows, :].astype(F32)
            hi = s.hs[l, 1, rows, :].astype(F32)
            s.yb[0, rows, :] = (gr * hr + gi * hi).astype(BF16)
            s.yb[1, rows, :] = (gi * hr - gr * hi).astype(BF16)
            xr = s.xf[l, 0, rows, :].astype(F32)
            xi = s.xf[l, 1, rows, :].astype(F32)
            s.qb[0, rows, :] = (gr * xr + gi * xi).astype(BF16)
            s.qb[1, rows, :] = (gi * xr - gr * xi).astype(BF16)

        ticks[0]()
        masks, first = tail_masks()
        gr, gi = tail_spectrum(s.gl[T - TL : T, :], masks)
        hr, hi = tail_filter(l, 0), tail_filter(l, 1)
        parts = tail_back(gr * hr + gi * hi, gi * hr - gr * hi)
        tail = parts[0] * masks[0]
        for part, mask in zip(parts[1:], masks[1:]):
            tail = tail + part * mask
        xr, xi = s.xt[l, 0].astype(F32), s.xt[l, 1].astype(F32)
        parts = tail_back(gr * xr + gi * xi, gi * xr - gr * xi)
        s.gtt[...] = sum(parts[1:], parts[0])

        @pl.loop(0, n // 2)
        def _(i):
            rows = chip_rows(i)
            s.g0s[rows, :] = (
                dot_nn(s.dftt[0, rows, :], s.yb[0]) + dot_nn(s.dftt[1, rows, :], s.yb[1])
            ) * (1.0 / T)
            s.gtp[rows, :] = (
                dot_nn(s.dftt[0, rows, :], s.qb[0]) + dot_nn(s.dftt[1, rows, :], s.qb[1])
            ) * (1.0 / T)

        s.g0s[T - TL : T, :] = jnp.where(first, s.g0s[T - TL : T, :], tail)
        s.gtp[0:TL, :] = s.gtp[0:TL, :] + s.gtt[...]

        ticks[1]()

        def fold(v):
            return jnp.sum(v.reshape(CH // 8, 8, C), axis=0)

        for k in range(3):
            s.gg[k, T : T + 8, :] = jnp.zeros((8, C), F32)

        def gate_step(r0, masks, sums):
            rows = pl.ds(r0, CH)
            parts = [shifted(l, k, r0, masks) for k in range(3)]
            gl = s.gl[rows, :]
            ginner = s.g0s[rows, :] + skip_row(l) * gl
            gk = [s.gg[0, rows, :], ginner * gate(l, 2, parts[2]), ginner * gate(l, 1, parts[1])]
            s.gg[1, rows, :] = gk[1]
            s.gg[2, rows, :] = gk[2]
            new = []
            for step in range(3):
                for k in range(3):
                    new.append(sums[step * 3 + k] + fold(gk[k] * parts[k][step]))
            for k in range(3):
                new.append(sums[9 + k] + fold(gk[k]))
            new.append(sums[12] + fold(gl * s.inn[l, rows, :]))
            return tuple(new)

        sums = lax.fori_loop(
            0,
            LAST,
            lambda i, sums: gate_step(pl.multiple_of(i * CH, CH), None, sums),
            tuple(jnp.zeros((8, C), F32) for _ in range(13)),
        )
        sums = gate_step(LAST * CH, chunk_masks(LAST * CH, CH), sums)
        for pos in range(12):
            s.sc0[l, 3 + pos : 4 + pos, :] = jnp.sum(sums[pos], axis=0, keepdims=True)
        s.sc0[l, ROW_SKIP : ROW_SKIP + 1, :] = jnp.sum(sums[12], axis=0, keepdims=True)

        ticks[2]()

        def proj_step(r0, masks, sums):
            new = []
            for k in range(3):
                blk = s.gg[k, pl.ds(r0, CH + 8), :]
                b1 = blk if masks is None else blk * masks[0]
                b2 = blk if masks is None else blk * masks[1]
                gp = (
                    conv_row(l, 0, k) * blk[0:CH]
                    + conv_row(l, 1, k) * b1[1 : CH + 1]
                    + conv_row(l, 2, k) * b2[2 : CH + 2]
                ).astype(BF16)
                s.gpj[k, pl.ds(r0, CH), :] = gp
                new.append(sums[k] + fold(gp.astype(F32)))
            return tuple(new)

        sums = lax.fori_loop(
            0,
            LAST - 1,
            lambda i, sums: proj_step(pl.multiple_of(i * CH, CH), None, sums),
            tuple(jnp.zeros((8, C), F32) for _ in range(3)),
        )
        for i in (LAST - 1, LAST):
            sums = proj_step(i * CH, chunk_masks(i * CH, CH + 8), sums)
        for k in range(3):
            s.sc0[l, k : k + 1, :] = jnp.sum(sums[k], axis=0, keepdims=True)

    def filter_backward(l):
        lag = lag_rows()
        gt = s.gtp[...]
        s.sc0[l, ROW_DECAY : ROW_DECAY + 1, :] = -jnp.sum(
            lag * gt * s.taps[l].astype(F32), axis=0, keepdims=True
        )
        gtr = (gt * jnp.exp(-lag * decay_row(l))).astype(BF16)
        gw3 = dot_tn(s.fa[1], gtr)
        s.sc0[l, ROW_W3 : ROW_W3 + FILT, :] = gw3[l * FILT : (l + 1) * FILT]
        gu2 = dot_nt(gtr, s.fw3p[l]) * s.fc[1]
        gz2 = gu2 * s.frow[3:4, :]
        gz2b = gz2.astype(BF16)
        s.sf[l, EP : EP + FILT, :] = dot_tn(s.fa[0], gz2b)[l * FILT : (l + 1) * FILT]
        gu1 = dot_nt(gz2b, s.fw2p[...].astype(BF16)) * s.fc[0]
        gz1 = gu1 * s.frow[2:3, :]
        s.sf[l, 0:EP, :] = dot_tn(s.emb[...].astype(BF16), gz1.astype(BF16))
        row = EP + FILT
        s.sf[l, row : row + 1, :] = jnp.sum(gz1, axis=0, keepdims=True)
        s.sf[l, row + 1 : row + 2, :] = jnp.sum(gz2, axis=0, keepdims=True)
        s.sf[l, row + 2 : row + 3, :] = jnp.sum(gu1 * s.fz[0], axis=0, keepdims=True)
        s.sf[l, row + 3 : row + 4, :] = jnp.sum(gu2 * s.fz[1], axis=0, keepdims=True)

    def w_scatter(l):
        rows_all = s.nF[l].reshape(T, D)
        go_all = s.goF[...].reshape(T, D)
        order = (2, 3, 1, 0)
        along_y, to_member, along_z = [], [], []

        def fill(k):
            at = slice((k % 2) * C, (k % 2 + 1) * C)
            for h in range(0, D, 256):
                if k < 3:
                    g = dot_tn(rows_all[:, h : h + 256], s.gpj[k])
                else:
                    g = dot_tn(go_all[:, h : h + 256], s.mx[l])
                gb = g.astype(BF16)
                lo = h
                while lo < h + 256:
                    b = lo // DB
                    off = lo % DB
                    cnt = min(DB - off, h + 256 - lo)
                    s.wg[k // 2, b, off : off + cnt, at] = gb[lo - h : lo - h + cnt]
                    lo += cnt

        for half in range(2):
            fill(2 * half)
            fill(2 * half + 1)
            along_y.append([])
            for e in range(1, Y):
                for d in order:
                    m = (a + d) % SHARE
                    j = ((y + e) % Y) * SHARE + m
                    along_y[half].append(
                        push(s.wg.at[half, j], s.wr.at[l, half, e - 1, m], y_peer(e))
                    )
        yield

        def members(half):
            to_member.append([])
            for pos, d in enumerate(order):
                m = (a + d) % SHARE
                acc = s.wg[half, y * SHARE + m].astype(F32)
                for e in range(1, Y):
                    done(along_y[half][(e - 1) * SHARE + pos])
                    acc = acc + s.wr[l, half, e - 1, m].astype(F32)
                if d:
                    s.wr[l, half, 0, m] = acc.astype(BF16)
                    to_member[half].append(
                        push(s.wr.at[l, half, 0, m], s.wr1.at[l, half, a], (y * SHARE + m, ti))
                    )
                else:
                    s.wr1[l, half, a] = acc.astype(BF16)

        def levels(half):
            for c in to_member[half]:
                done(c)
            along_z.append([])
            for d in range(1, n):
                j = (ti + d) % n
                along_z[half].append(
                    push(s.wr1.at[l, half, j], s.wr2.at[l, half, d - 1], (dp, j))
                )

        members(0)
        yield
        members(1)
        sent(*along_y[0], *along_y[1])
        levels(0)
        yield
        levels(1)
        yield
        for half in range(2):
            acc = s.wr1[l, half, ti].astype(F32)
            for d in range(1, n):
                done(along_z[half][d - 1])
                acc = acc + s.wr2[l, half, d - 1].astype(F32)
            lo = at_wo + l * DB
            s.pack[lo : lo + DB, half * 2 * C : (half + 1) * 2 * C] = acc
            sent(*to_member[half], *along_z[half])
        yield

    def small_plane(l, names):
        pick = dict(a=(s.sa, s.rA), f=(s.sf, s.rF), c=(s.sc, s.rC))
        pairs = [pick[x] for x in names]
        for step in range(ndp.bit_length() - 1):
            bit = 1 << step
            peer = (dp + bit - 2 * bit * ((dp // bit) % 2), ti)
            copies = [push(v.at[l], r.at[l, step], peer) for v, r in pairs]
            yield
            for c in copies:
                done(c)
            sent(*copies)
            for v, r in pairs:
                v[l] = v[l] + r[l, step]
        yield

    def rows_last():
        copies = [
            push(s.sa.at[0], s.rP.at[d - 1], ((dp + d) % ndp, ti)) for d in range(1, ndp)
        ]
        yield
        acc = s.sa[0]
        for d in range(1, ndp):
            done(copies[d - 1])
            acc = acc + s.rP[d - 1]
        sent(*copies)
        s.sa[0] = acc
        copies = [push(s.sa.at[0], s.rZ.at[d - 1], (dp, (ti + d) % n)) for d in range(1, n)]
        yield
        for d in range(1, n):
            done(copies[d - 1])
            acc = acc + s.rZ[d - 1]
        sent(*copies)
        s.sa[0] = acc
        yield

    def small_levels():
        total = s.sf[0]
        for l in range(1, L):
            total = total + s.sf[l]
        s.sf[0] = total
        for step in range(n.bit_length() - 1):
            bit = 1 << step
            peer = (dp, ti + bit - 2 * bit * ((ti // bit) % 2))
            copies = [push(s.sf.at[0], s.rFz.at[step], peer)]
            for l in range(1, L):
                copies.append(push(s.sa.at[l], s.rAz.at[step, l], peer))
            yield
            for c in copies:
                done(c)
            sent(*copies)
            for l in range(1, L):
                s.sa[l] = s.sa[l] + s.rAz[step, l]
            s.sf[0] = s.sf[0] + s.rFz[step]
        yield

    at_wo, at_rows, at_side, at_out = z.places()
    wgen = {0: w_gather(0)}
    next(wgen[0])
    for l in range(L):
        s.pin[l] = jnp.zeros((ROW_W3, C), F32)
        for k in range(3):
            s.pin[l, k : k + 1, :] = s.b_in[k, l : l + 1, :]
            s.pin[l, 12 + k : 13 + k, :] = s.cb[k, l : l + 1, :]
        for k in range(9):
            s.pin[l, 3 + k : 4 + k, :] = s.cw[k, l : l + 1, :]
        s.pin[l, ROW_DECAY : ROW_DECAY + 1, :] = s.decay[l : l + 1, :]
        s.pin[l, ROW_SKIP : ROW_SKIP + 1, :] = s.skip[l : l + 1, :]
        s.p3[l] = s.fw3[l].astype(BF16)
    total = s.lens[0, 0]
    for k in ENDS:
        if k:
            total = total + s.lens[0, k]
        s.pin[0, ROW_ENDS + k : ROW_ENDS + k + 1, :] = jnp.full((1, C), total, jnp.int32).astype(F32)
    pc = swap(s.pin, s.pv)
    xc = [swap(s.xb.at[half(h)], s.xv.at[half(h)]) for h in range(2)]
    p3c = {0: swap(s.p3.at[0], s.v3.at[0])}
    filter_net()
    fgen = {l: ff_gather(l) for l in range(L)}
    wgen[1] = w_gather(1)

    def run(*gens):
        def go():
            for g in gens:
                next(g)

        return go

    def seq(*acts):
        def go():
            for act in acts:
                act()

        return go

    def norm_one(l, h, x):
        xhat, _ = ln_parts(x)
        s.nF[l, a, half(h), :] = (xhat * s.ln1g[l : l + 1, :] + s.ln1b[l : l + 1, :]).astype(BF16)

    def first_rows(h):
        swapped(xc[h])
        norm_one(0, h, layer_input(0, h))
        yield from gather_s(s.nF.at[0], h)

    rows = [first_rows(0), first_rows(1)]
    run(wgen[0], wgen[0])()
    run(rows[0], rows[1], wgen[0], rows[0], rows[1], wgen[0], fgen[0])()
    p3c[1] = swap(s.p3.at[1], s.v3.at[1])
    weave(*rows)
    swapped(pc)
    swapped(p3c[0])
    filter_taps_of(0)
    run(wgen[0])()
    project(0, 0)
    project(0, 1)
    run(fgen[0])()

    def taps_one():
        swapped(p3c[1])
        filter_taps_of(1)

    def forward_rows(l, h, hooks):
        def call(pos):
            if (h, pos) in hooks:
                hooks[(h, pos)]()

        mixed = lambda: s.mx[l].reshape(SHARE, R, C)[:, h * HR : (h + 1) * HR].reshape(
            SHARE * HR, C
        )
        res = yield from scatter_s(h, lambda: dot_nn(mixed(), w_mat(l, 3)), lambda: call(0))
        mid = layer_input(l, h) + s.b_out[l : l + 1, :] + res
        s.mids[l, half(h), :] = mid
        xhat, _ = ln_parts(mid)
        s.n2S[l, a, half(h), :] = (xhat * s.ln2g[l : l + 1, :] + s.ln2b[l : l + 1, :]).astype(BF16)
        yield from gather_s(s.n2S.at[l], h)
        call(1)
        res = yield from scatter_s(h, lambda: ff_block(l, h), lambda: call(2))
        cur = s.mids[l, half(h), :] + s.b_down[l : l + 1, :] + res
        if l + 1 < L:
            s.xs[l, half(h), :] = cur
            norm_one(l + 1, h, cur)
            yield from gather_s(s.nF.at[l + 1], h)
            call(3)
            project(l + 1, h)
        else:
            s.ov[half(h), :] = cur.astype(BF16)

    mixer_forward(0, run(fgen[0]))
    hooks = {
        (1, 0): seq(run(fgen[0], wgen[1]), taps_one),
        (0, 1): run(fgen[0]),
        (1, 1): run(fgen[1], wgen[1], wgen[1]),
        (1, 2): run(wgen[1], wgen[1], fgen[1]),
        (0, 3): run(wgen[1]),
    }
    weave(forward_rows(0, 0, hooks), forward_rows(0, 1, hooks))
    sent(*xc)
    s.xb[...] = s.cot[...].astype(BF16)
    mixer_forward(1, run(fgen[1]))
    cots = []
    hooks = {
        (1, 0): seq(run(fgen[1]), lambda: cots.append(swap(s.xb, s.cv))),
        (0, 1): run(fgen[1]),
    }
    weave(forward_rows(1, 0, hooks), forward_rows(1, 1, hooks))
    swapped(cots[0])
    outs = swap(s.ov, s.gv)
    s.gx[...] = s.cv[...].astype(F32)

    def add_row(l, pos, row):
        s.sa[l, pos : pos + 1, :] = s.sa[l, pos : pos + 1, :] + row

    def back_block(l, h):
        def rows(k):
            return s.gpj[k].reshape(SHARE, R, C)[:, h * HR : (h + 1) * HR].reshape(SHARE * HR, C)

        acc = dot_nn(rows(0), w_mat(l, 0))
        acc = acc + dot_nn(rows(1), w_mat(l, 1))
        return acc + dot_nn(rows(2), w_mat(l, 2))

    def backward_rows(l, h, hooks):
        def call(pos):
            if (h, pos) in hooks:
                hooks[(h, pos)]()

        if l + 1 < L:
            yield from last_rows(l + 1, h, hooks)
        if l < 0:
            return
        gd = s.gx[half(h), :].astype(BF16)
        s.gdS[l, a, half(h), :] = gd
        add_row(l, 5, jnp.sum(gd.astype(F32), axis=0, keepdims=True))
        yield from gather_s(s.gdS.at[l], h)
        call(1)
        gn = yield from scatter_s(h, lambda: ff_back_block(l, h), lambda: call(2))
        gv, gain_row, bias_row = ln_back(s.mids[l, half(h), :], gn, s.ln2g[l : l + 1, :])
        add_row(l, 2, gain_row)
        add_row(l, 3, bias_row)
        gm = s.gx[half(h), :] + gv
        s.gx[half(h), :] = gm
        go = gm.astype(BF16)
        add_row(l, 4, jnp.sum(go.astype(F32), axis=0, keepdims=True))
        s.goF[a, half(h), :] = go
        yield from gather_s(s.goF, h)
        call(3)
        rows = s.goF[:, half(h), :].reshape(SHARE * HR, D)
        res = dot_nt(rows, w_mat(l, 3))
        for m in range(SHARE):
            lo = m * R + h * HR
            s.gtp[lo : lo + HR, :] = res[m * HR : (m + 1) * HR]

    def last_rows(l, h, hooks):
        def hook():
            if (h, 0) in hooks:
                hooks[(h, 0)]()

        gn = yield from scatter_s(h, lambda: back_block(l, h), hook)
        gv, gain_row, bias_row = ln_back(layer_input(l, h), gn, s.ln1g[l : l + 1, :])
        add_row(l, 0, gain_row)
        add_row(l, 1, bias_row)
        s.gx[half(h), :] = s.gx[half(h), :] + gv

    for l in range(L):
        s.sa[l] = jnp.zeros((8, D), F32)
        s.sf[l] = jnp.zeros((z.FROWS, LF), F32)
        s.sc0[l] = jnp.zeros((z.CROWS, C), F32)

    ffs = [ff_scatter(l) for l in range(L)]
    wsc = [w_scatter(l) for l in range(L)]
    small1 = small_plane(1, "afc")
    side0 = small_plane(0, "f")
    corner0 = small_plane(0, "c")
    rows0 = rows_last()
    levels = small_levels()
    none = lambda: None

    def filters(l):
        def go():
            filter_backward(l)

        return go

    hooks = {(1, 2): run(ffs[1])}
    weave(backward_rows(1, 0, hooks), backward_rows(1, 1, hooks))
    mixer_backward(1, [none, run(ffs[1]), none])
    corner = {}

    def corner_swap(l):
        def go():
            corner[l] = swap(s.sc0.at[l], s.sc.at[l])

        return go

    hooks = {
        (1, 0): seq(run(wsc[1], ffs[1]), filters(1), corner_swap(1)),
        (1, 1): run(ffs[1]),
        (1, 2): run(ffs[0], wsc[1]),
        (0, 3): run(ffs[1], wsc[1]),
        (1, 3): seq(lambda: swapped(corner[1]), run(small1, ffs[0])),
    }
    weave(backward_rows(0, 0, hooks), backward_rows(0, 1, hooks))
    mixer_backward(
        0,
        [
            run(small1, wsc[1]),
            seq(run(small1, ffs[1], ffs[0]), filters(0), run(side0)),
            run(side0),
        ],
    )
    corner_swap(0)()
    run(side0, wsc[0])()
    hooks = {
        (0, 0): run(ffs[0]),
        (1, 0): seq(run(small1, side0, levels), lambda: swapped(corner[0]), run(corner0)),
    }
    weave(last_rows(0, 0, hooks), last_rows(0, 1, hooks))
    sent(outs)
    s.ov[...] = s.gx[...].astype(BF16)
    run(rows0)()
    gins = swap(s.ov, s.cv)
    run(corner0, levels, wsc[0], corner0, rows0, wsc[0], ffs[0], levels, corner0, wsc[0])()
    swapped(outs)
    s.pack[at_out : at_out + R, :] = s.gv[...].astype(F32)
    run(wsc[1], ffs[0], rows0)()
    swapped(gins)
    s.pack[at_out + R : at_out + 2 * R, :] = s.cv[...].astype(F32)
    run(wsc[0])()
    for l in range(L):
        s.pack[at_rows + 8 * l : at_rows + 8 * (l + 1), :] = s.sa[l]
        lo = LF + 2 * C * l
        s.pack[at_side : at_side + z.CROWS, lo : lo + C] = s.sc[l]
    s.pack[at_side : at_side + z.FROWS, 0:LF] = s.sf[0]
    flush()


class View:
    def __init__(self, ref, row, rows, lane, lanes):
        self.ref, self.row, self.rows, self.lane, self.lanes = ref, row, rows, lane, lanes

    def __getitem__(self, at):
        rows, lanes = at
        top, bottom, _ = rows.indices(self.rows)
        left, right, _ = lanes.indices(self.lanes)
        return self.ref[
            self.row + top : self.row + bottom, self.lane + left : self.lane + right
        ]


def finish_kernel(z, *refs):
    o = types.SimpleNamespace(**dict(zip(FINAL, refs[1 : 1 + len(FINAL)])))
    held, sem = refs[-2:]
    copy = pltpu.make_async_copy(refs[0], held, sem)
    copy.start()
    copy.wait()
    at_wo, at_rows, at_side, at_out = z.places()
    C, R = z.C, z.R
    o.out[...] = held[at_out : at_out + R, :]
    o.gin[...] = held[at_out + R : at_out + 2 * R, :]
    for l in range(z.L):
        at = z.EP + z.FILT
        lo = z.LF + 2 * C * l
        sa = View(held, at_rows + 8 * l, 8, 0, z.D)
        sc = View(held, at_side, z.CROWS, lo, C)
        sf = View(held, at_side, z.FROWS, l * z.FILT, z.FILT)
        wo = View(held, at_wo + l * z.DB, z.DB, 0, 4 * C)
        ffo = View(held, l * z.FR, z.FR, 0, z.D)
        row = slice(l, l + 1)
        for pos, ref in enumerate((o.ln1g, o.ln1b, o.ln2g, o.ln2b, o.b_out, o.b_down)):
            ref[row, :] = sa[pos : pos + 1, :]
        for k in range(3):
            o.w_in[l, k] = wo[:, k * C : (k + 1) * C]
            o.b_in[k, row, :] = sc[k : k + 1, :]
            o.cb[k, row, :] = sc[12 + k : 13 + k, :]
        for k in range(9):
            o.cw[k, row, :] = sc[3 + k : 4 + k, :]
        o.w_out[l] = wo[:, 3 * C : 4 * C].T
        for r in range(z.EMB):
            o.fw1[r, row, :] = sf[r : r + 1, :]
        o.fw2[l] = sf[z.EP : at, :]
        o.fb1[row, :] = sf[at : at + 1, :]
        o.fb2[row, :] = sf[at + 1 : at + 2, :]
        o.freq[l] = sf[at + 2 : at + 4, :]
        o.fw3[l] = sc[ROW_W3 : z.CROWS, :]
        o.decay[row, :] = sc[ROW_DECAY : ROW_DECAY + 1, :]
        o.skip[row, :] = sc[ROW_SKIP : ROW_SKIP + 1, :]
        o.w_up[l] = ffo[0 : z.FFs, :]
        o.w_down[l] = ffo[z.FFs : 2 * z.FFs, :]
        o.b_up[row, :] = ffo[2 * z.FFs : 2 * z.FFs + 1, 0 : z.FFs]


FINAL = (
    "out", "gin", "ln1g", "ln1b", "w_in", "b_in", "cw", "cb", "fw1", "fb1", "fw2", "fb2", "freq", "fw3",
    "decay", "skip", "w_out", "b_out", "ln2g", "ln2b", "w_up", "b_up", "w_down", "b_down",
)


def fused_local(z, *args):
    (inputs, cotangent, lengths, ln1_gain, ln1_bias, w_in, b_in, conv_weight, conv_bias, filt_w1,
     filt_b1, filt_w2, filt_b2, filt_freq, filt_w3, decay_rate, skip_gain, w_out, b_out, ln2_gain,
     ln2_bias, w_up, b_up, w_down, b_down) = args
    L, D, C, T, FFs, FILT = z.L, z.D, z.C, z.T, z.FFs, z.FILT
    lag = np.arange(T) / T
    bands = np.arange(1, z.EMB // 2 + 1)
    phases = 2.0 * math.pi * lag[:, None] * bands[None, :]
    emb = np.concatenate([lag[:, None], np.cos(phases), np.sin(phases)], axis=1)
    emb = np.pad(emb, ((0, 0), (0, z.EP - z.EMB))).astype(np.float32)
    def tables(length, copies):
        turn = (np.arange(length) * 2 + 1)[:, None] * np.arange(length)[None, :] % (4 * length)
        turn = turn * (math.pi / (2 * length))
        pair = [np.kron(np.eye(copies), f(turn)) for f in (np.cos, np.sin)]
        there = np.stack(pair).astype(jnp.bfloat16)
        back = np.stack([m.T for m in pair]).astype(jnp.bfloat16)
        return jnp.asarray(there), jnp.asarray(back)

    values = (
        inputs, cotangent, lengths, ln1_gain, ln1_bias, jnp.transpose(w_in, (0, 2, 3, 1)),
        jnp.swapaxes(b_in, 0, 1), jnp.transpose(conv_weight, (1, 2, 0, 3)).reshape(9, L, C),
        jnp.swapaxes(conv_bias, 0, 1), jnp.asarray(emb), jnp.swapaxes(filt_w1, 0, 1), filt_b1, filt_w2, filt_b2,
        filt_freq, filt_w3, decay_rate, skip_gain, w_out, b_out, ln2_gain, ln2_bias,
        jnp.swapaxes(w_up, 1, 2), b_up, w_down, b_down, *tables(T, 1), *tables(z.TL, z.SL - 1),
    )
    shapes, sems, _, _ = scratch_shapes(z)
    names = INPUTS + OUTPUTS + tuple(shapes) + ("ssem", "rsem", "lsem")
    f32 = lambda *dims: jax.ShapeDtypeStruct(dims, F32)
    outs = (f32(z.places()[3] + 2 * z.R, D),)
    vmem = pl.BlockSpec(memory_space=pltpu.VMEM)
    place = {"lens": pltpu.SMEM, "w_in": pl.ANY, "w_out": pl.ANY}
    specs = [pl.BlockSpec(memory_space=place.get(name, pltpu.VMEM)) for name in INPUTS]
    (packed,) = pl.pallas_call(
        functools.partial(fused_kernel, z, names),
        out_shape=outs,
        in_specs=specs,
        out_specs=[vmem] * len(outs),
        scratch_shapes=[pltpu.VMEM(*spec) for spec in shapes.values()]
        + [
            pltpu.SemaphoreType.DMA((sems,)),
            pltpu.SemaphoreType.DMA((sems,)),
            pltpu.SemaphoreType.DMA((L,)),
        ],
        compiler_params=pltpu.CompilerParams(
            collective_id=0, has_side_effects=True, vmem_limit_bytes=VMEM_LIMIT
        ),
        name="hyena_layers",
    )(*values)
    final = dict(
        out=f32(z.R, D), gin=f32(z.R, D),
        ln1g=f32(L, D), ln1b=f32(L, D), w_in=f32(L, 3, z.DB, C), b_in=f32(3, L, C),
        cw=f32(9, L, C), cb=f32(3, L, C), fw1=f32(z.EMB, L, FILT), fb1=f32(L, FILT),
        fw2=f32(L, FILT, FILT), fb2=f32(L, FILT), freq=f32(L, 2, FILT), fw3=f32(L, FILT, C),
        decay=f32(L, C), skip=f32(L, C), w_out=f32(L, C, z.DB), b_out=f32(L, D),
        ln2g=f32(L, D), ln2b=f32(L, D), w_up=f32(L, FFs, D), b_up=f32(L, FFs),
        w_down=f32(L, FFs, D), b_down=f32(L, D),
    )
    res = pl.pallas_call(
        functools.partial(finish_kernel, z),
        out_shape=tuple(final[name] for name in FINAL),
        in_specs=[pl.BlockSpec(memory_space=pl.ANY)],
        out_specs=[vmem] * len(FINAL),
        scratch_shapes=[pltpu.VMEM(packed.shape, F32), pltpu.SemaphoreType.DMA],
        compiler_params=pltpu.CompilerParams(vmem_limit_bytes=40 * 1024 * 1024),
        name="hyena_unpack",
    )(packed)
    g = types.SimpleNamespace(**dict(zip(FINAL, res)))
    return (
        g.out, g.gin, g.ln1g, g.ln1b, jnp.swapaxes(g.w_in, 1, 2), jnp.swapaxes(g.b_in, 0, 1),
        jnp.transpose(g.cw.reshape(3, 3, L, C), (2, 0, 1, 3)), jnp.swapaxes(g.cb, 0, 1),
        jnp.swapaxes(g.fw1, 0, 1), g.fb1, g.fw2, g.fb2, g.freq, g.fw3, g.decay, g.skip, g.w_out,
        g.b_out, g.ln2g, g.ln2b, jnp.swapaxes(g.w_up, 1, 2), g.b_up, g.w_down, g.b_down,
    )


def local_any(mesh, *args):
    z = Sizes(
        mesh.shape["dp"], mesh.shape["tensor"], args[0].shape[0], args[0].shape[1],
        args[5].shape[3], args[21].shape[2], args[2].shape[1], args[5].shape[0],
        args[9].shape[1], args[9].shape[2],
    )
    return fused_local(z, *args) if z.fits() else local(*args)


def solution(mesh):
    in_specs = (
        P(("dp", "tensor"), None),
        P(("dp", "tensor"), None),
        P("dp", None),
        P(),
        P(),
        P(None, None, None, "tensor"),
        P(None, None, "tensor"),
        P(None, None, None, "tensor"),
        P(None, None, "tensor"),
        P(),
        P(),
        P(),
        P(),
        P(),
        P(None, None, "tensor"),
        P(None, "tensor"),
        P(None, "tensor"),
        P(None, "tensor", None),
        P(),
        P(),
        P(),
        P(None, None, ("dp", "tensor")),
        P(None, ("dp", "tensor")),
        P(None, ("dp", "tensor"), None),
        P(),
    )
    out_specs = (
        P(("dp", "tensor"), None),
        P(("dp", "tensor"), None),
        P(),
        P(),
        P(None, "dp", None, "tensor"),
        P(None, None, "tensor"),
        P(None, None, None, "tensor"),
        P(None, None, "tensor"),
        P(),
        P(),
        P(),
        P(),
        P(),
        P(None, None, "tensor"),
        P(None, "tensor"),
        P(None, "tensor"),
        P(None, "tensor", "dp"),
        P(),
        P(),
        P(),
        P(None, None, ("dp", "tensor")),
        P(None, ("dp", "tensor")),
        P(None, ("dp", "tensor"), None),
        P(),
    )
    return jax.shard_map(functools.partial(local_any, mesh), mesh=mesh, in_specs=in_specs, out_specs=out_specs, check_vma=False)
```

```python
import functools
import math
import types

import jax
import jax.numpy as jnp
import numpy as np
from jax import lax
from jax.experimental import pallas as pl
from jax.experimental.pallas import tpu as pltpu
from jax.sharding import PartitionSpec as P

NORM_EPS = 1e-05
PRECISE = lax.Precision.HIGHEST


def layer_norm(values, norm_gain, norm_shift):
    center = values - jnp.mean(values, axis=-1, keepdims=True)
    spread = jnp.mean(center * center, axis=-1, keepdims=True)
    return center * lax.rsqrt(spread + NORM_EPS) * norm_gain + norm_shift


def filter_taps(w_first, b_first, w_second, b_second, freq_pair, w_third, decay_row, length):
    lag_pos = jnp.arange(length).astype(jnp.float32)
    fraction = lag_pos / length
    band_ids = jnp.arange(1, w_first.shape[0] // 2 + 1).astype(jnp.float32)
    phases = 2.0 * math.pi * fraction[:, None] * band_ids[None, :]
    embedding = jnp.concatenate([fraction[:, None], jnp.cos(phases), jnp.sin(phases)], axis=1)
    layer_one = jnp.sin(freq_pair[0] * (jnp.dot(embedding, w_first, precision=PRECISE) + b_first))
    layer_two = jnp.sin(freq_pair[1] * (jnp.dot(layer_one, w_second, precision=PRECISE) + b_second))
    return jnp.dot(layer_two, w_third, precision=PRECISE) * jnp.exp(
        -lag_pos[:, None] * decay_row[None, :]
    )


def segment_ids(lens_row, length):
    places = jnp.arange(length)
    ends = jnp.cumsum(lens_row)
    return jnp.sum((places[:, None] >= ends[None, :-1]).astype(jnp.int32), axis=1)


def short_conv(projected, weight_short, bias_short, seg_ids):
    summed = bias_short[None] + weight_short[0][None] * projected
    for offset in (1, 2):
        shifted = jnp.concatenate(
            [jnp.zeros((offset,) + projected.shape[1:], jnp.float32), projected[:-offset]], axis=0
        )
        earlier = jnp.concatenate([jnp.full((offset,), -1, jnp.int32), seg_ids[:-offset]], axis=0)
        within = (earlier == seg_ids).astype(jnp.float32)
        summed = summed + weight_short[offset][None] * shifted * within[:, None, None]
    return summed


def trig_table(count_rows, count_cols, modulus):
    product = jnp.arange(count_rows)[:, None] * jnp.arange(count_cols)[None, :] % modulus
    phases = product.astype(jnp.float32) * (2.0 * math.pi / modulus)
    return (jnp.cos(phases), jnp.sin(phases))


def forward_dft(signal, tables):
    cos_a, sin_a, cos_t, sin_t, cos_b, sin_b = tables
    shaped = signal.reshape(cos_a.shape[0], cos_b.shape[0], signal.shape[1])
    real_one = jnp.einsum("abc,ak->kbc", shaped, cos_a, precision=PRECISE)
    imag_one = -jnp.einsum("abc,ak->kbc", shaped, sin_a, precision=PRECISE)
    turn_re = cos_t[:, :, None]
    turn_im = sin_t[:, :, None]
    real_two = real_one * turn_re + imag_one * turn_im
    imag_two = imag_one * turn_re - real_one * turn_im
    real_out = jnp.einsum("kbc,bj->kjc", real_two, cos_b, precision=PRECISE) + jnp.einsum(
        "kbc,bj->kjc", imag_two, sin_b, precision=PRECISE
    )
    imag_out = jnp.einsum("kbc,bj->kjc", imag_two, cos_b, precision=PRECISE) - jnp.einsum(
        "kbc,bj->kjc", real_two, sin_b, precision=PRECISE
    )
    return (real_out, imag_out)


def inverse_dft(real_in, imag_in, tables):
    cos_a, sin_a, cos_t, sin_t, cos_b, sin_b = tables
    real_one = jnp.einsum("kjc,bj->kbc", real_in, cos_b, precision=PRECISE) - jnp.einsum(
        "kjc,bj->kbc", imag_in, sin_b, precision=PRECISE
    )
    imag_one = jnp.einsum("kjc,bj->kbc", imag_in, cos_b, precision=PRECISE) + jnp.einsum(
        "kjc,bj->kbc", real_in, sin_b, precision=PRECISE
    )
    turn_re = cos_t[:, :, None]
    turn_im = sin_t[:, :, None]
    real_two = real_one * turn_re - imag_one * turn_im
    imag_two = imag_one * turn_re + real_one * turn_im
    shaped = jnp.einsum("kbc,ak->abc", real_two, cos_a, precision=PRECISE) - jnp.einsum(
        "kbc,ak->abc", imag_two, sin_a, precision=PRECISE
    )
    total_len = 2 * shaped.shape[0] * shaped.shape[1]
    return shaped.reshape(shaped.shape[0] * shaped.shape[1], shaped.shape[2]) / total_len


def local(
    inputs,
    cotangent,
    lengths,
    ln1_gain,
    ln1_bias,
    w_in,
    b_in,
    conv_weight,
    conv_bias,
    filt_w1,
    filt_b1,
    filt_w2,
    filt_b2,
    filt_freq,
    filt_w3,
    decay_rate,
    skip_gain,
    w_out,
    b_out,
    ln2_gain,
    ln2_bias,
    w_up,
    b_up,
    w_down,
    b_down,
):
    rows_dev = inputs.shape[0]
    tensor_size = lax.axis_size("tensor")
    group_len = rows_dev * tensor_size
    layer_count = w_in.shape[0]
    seg_ids = segment_ids(lengths[0], group_len)
    masks_seq = tuple(
        ((seg_ids == seq_pos).astype(jnp.float32) for seq_pos in range(lengths.shape[1]))
    )
    full_len = 2 * group_len
    fold_a = math.gcd(full_len, 128)
    fold_b = full_len // fold_a
    cos_a, sin_a = trig_table(fold_a // 2, fold_a, fold_a)
    cos_t, sin_t = trig_table(fold_a, fold_b, full_len)
    cos_b, sin_b = trig_table(fold_b, fold_b, fold_b)
    tables = (cos_a, sin_a, cos_t, sin_t, cos_b, sin_b)

    def mixer_local(
        projected,
        weight_short,
        bias_short,
        fw_one,
        fb_one,
        fw_two,
        fb_two,
        freq_pair,
        fw_three,
        decay_row,
        skip_row,
    ):
        gated = short_conv(projected, weight_short, bias_short, seg_ids)
        taps_long = filter_taps(
            fw_one, fb_one, fw_two, fb_two, freq_pair, fw_three, decay_row, group_len
        )
        filt_re, filt_im = forward_dft(taps_long, tables)
        mixed_in = gated[:, 2] * gated[:, 1]
        result = skip_row * mixed_in
        for mask_one in masks_seq:
            sig_re, sig_im = forward_dft(mixed_in * mask_one[:, None], tables)
            result = result + mask_one[:, None] * inverse_dft(
                sig_re * filt_re - sig_im * filt_im, sig_re * filt_im + sig_im * filt_re, tables
            )
        return result * gated[:, 0]

    kept_list = []
    current = inputs
    for layer_idx in range(layer_count):
        normed, norm_back = jax.vjp(layer_norm, current, ln1_gain[layer_idx], ln1_bias[layer_idx])
        normed_full = lax.all_gather(normed.astype(jnp.bfloat16), "tensor", axis=0, tiled=True)
        projected = (
            jnp.einsum(
                "td,dkc->tkc", normed_full, w_in[layer_idx], preferred_element_type=jnp.float32
            )
            + b_in[layer_idx]
        )
        mixer_val, mixer_back = jax.vjp(
            mixer_local,
            projected,
            conv_weight[layer_idx],
            conv_bias[layer_idx],
            filt_w1[layer_idx],
            filt_b1[layer_idx],
            filt_w2[layer_idx],
            filt_b2[layer_idx],
            filt_freq[layer_idx],
            filt_w3[layer_idx],
            decay_rate[layer_idx],
            skip_gain[layer_idx],
        )
        mixer_low = mixer_val.astype(jnp.bfloat16)
        weight_out = w_out[layer_idx]
        keep_out = lax.all_to_all(mixer_low, "tensor", split_axis=0, concat_axis=1, tiled=True)
        weight_out = lax.all_gather(weight_out, "tensor", axis=0, tiled=True)
        branch_out = jnp.dot(keep_out, weight_out, preferred_element_type=jnp.float32)
        middle = current + branch_out + b_out[layer_idx]
        normed_two, norm_two_back = jax.vjp(
            layer_norm, middle, ln2_gain[layer_idx], ln2_bias[layer_idx]
        )
        normed_two_low = normed_two.astype(jnp.bfloat16)
        up_full, upb_full, down_full = (
            lax.all_gather(w_up[layer_idx], ("dp", "tensor"), axis=1, tiled=True),
            lax.all_gather(b_up[layer_idx], ("dp", "tensor"), axis=0, tiled=True),
            lax.all_gather(w_down[layer_idx], ("dp", "tensor"), axis=0, tiled=True),
        )
        hidden_pre = jnp.dot(
            normed_two_low, up_full, preferred_element_type=jnp.float32
        ) + upb_full.astype(jnp.float32)
        hidden_act, gelu_back = jax.vjp(jax.nn.gelu, hidden_pre)
        hidden_low = hidden_act.astype(jnp.bfloat16)
        current = (
            middle
            + jnp.dot(hidden_low, down_full, preferred_element_type=jnp.float32)
            + b_down[layer_idx]
        )
        kept_list.append(
            (
                norm_back,
                normed_full,
                mixer_back,
                keep_out,
                weight_out,
                norm_two_back,
                normed_two_low,
                None,
                None,
                hidden_low,
                gelu_back,
            )
        )
    grad_rows = cotangent
    per_layer = [None] * layer_count
    for layer_idx in reversed(range(layer_count)):
        (
            norm_back,
            normed_full,
            mixer_back,
            keep_out,
            weight_out,
            norm_two_back,
            normed_two_low,
            up_full,
            down_full,
            hidden_low,
            gelu_back,
        ) = kept_list[layer_idx]
        up_full, down_full = (
            lax.all_gather(w_up[layer_idx], ("dp", "tensor"), axis=1, tiled=True),
            lax.all_gather(w_down[layer_idx], ("dp", "tensor"), axis=0, tiled=True),
        )
        down_low = grad_rows.astype(jnp.bfloat16)
        grad_b_down = jnp.sum(down_low.astype(jnp.float32), axis=0)
        grad_w_down = jnp.einsum(
            "tf,td->fd", hidden_low, down_low, preferred_element_type=jnp.float32
        )
        grad_hidden = jnp.einsum(
            "td,fd->tf", down_low, down_full, preferred_element_type=jnp.float32
        )
        (grad_pre,) = gelu_back(grad_hidden)
        pre_low = grad_pre.astype(jnp.bfloat16)
        grad_w_up = jnp.einsum(
            "td,tf->df", normed_two_low, pre_low, preferred_element_type=jnp.float32
        )
        grad_b_up = jnp.sum(pre_low.astype(jnp.float32), axis=0)
        grad_normed_two = jnp.einsum(
            "tf,df->td", pre_low, up_full, preferred_element_type=jnp.float32
        )
        shard_w_up, shard_b_up, shard_w_down = (
            lax.psum_scatter(grad_w_up, ("dp", "tensor"), scatter_dimension=1, tiled=True),
            lax.psum_scatter(grad_b_up, ("dp", "tensor"), scatter_dimension=0, tiled=True),
            lax.psum_scatter(grad_w_down, ("dp", "tensor"), scatter_dimension=0, tiled=True),
        )
        grad_middle_ln, grad_ln2_gain, grad_ln2_bias = norm_two_back(grad_normed_two)
        grad_middle = grad_rows + grad_middle_ln
        out_low = grad_middle.astype(jnp.bfloat16)
        grad_b_out = jnp.sum(out_low.astype(jnp.float32), axis=0)
        grad_rows_mixed = jnp.einsum(
            "td,cd->tc", out_low, weight_out, preferred_element_type=jnp.float32
        )
        grad_mixed = lax.all_to_all(
            grad_rows_mixed.astype(jnp.bfloat16), "tensor", split_axis=1, concat_axis=0, tiled=True
        ).astype(grad_rows_mixed.dtype)
        grad_w_out = lax.psum_scatter(
            jnp.einsum("tc,td->cd", keep_out, out_low, preferred_element_type=jnp.float32).astype(
                jnp.bfloat16
            ),
            "tensor",
            scatter_dimension=0,
            tiled=True,
        ).astype(jnp.float32)
        grads_mixer = mixer_back(grad_mixed)
        proj_low = grads_mixer[0].astype(jnp.bfloat16)
        grad_w_in = jnp.einsum(
            "td,tkc->dkc", normed_full, proj_low, preferred_element_type=jnp.float32
        )
        grad_b_in = jnp.sum(proj_low.astype(jnp.float32), axis=0)
        weight_in = w_in[layer_idx]
        grad_normed = lax.psum_scatter(
            jnp.einsum(
                "tkc,dkc->td", proj_low, weight_in, preferred_element_type=jnp.float32
            ).astype(jnp.bfloat16),
            "tensor",
            scatter_dimension=0,
            tiled=True,
        ).astype(jnp.float32)
        grad_in_ln, grad_ln1_gain, grad_ln1_bias = norm_back(grad_normed)
        grad_rows = grad_middle + grad_in_ln
        per_layer[layer_idx] = (
            grad_ln1_gain,
            grad_ln1_bias,
            grad_w_in,
            grad_b_in,
            grads_mixer[1],
            grads_mixer[2],
            grads_mixer[3],
            grads_mixer[4],
            grads_mixer[5],
            grads_mixer[6],
            grads_mixer[7],
            grads_mixer[8],
            grads_mixer[9],
            grads_mixer[10],
            grad_w_out,
            grad_b_out,
            grad_ln2_gain,
            grad_ln2_bias,
            shard_w_up,
            shard_b_up,
            shard_w_down,
            grad_b_down,
        )
    stacks = [
        jnp.stack([per_layer[layer_pos][slot_pos] for layer_pos in range(layer_count)])
        for slot_pos in range(22)
    ]
    shared_done = lax.psum(
        (
            stacks[0],
            stacks[1],
            stacks[6],
            stacks[7],
            stacks[8],
            stacks[9],
            stacks[10],
            stacks[15],
            stacks[16],
            stacks[17],
            stacks[21],
        ),
        ("dp", "tensor"),
    )
    weight_done = (
        lax.psum_scatter(
            stacks[2].astype(jnp.bfloat16), "dp", scatter_dimension=1, tiled=True
        ).astype(jnp.float32),
        lax.psum_scatter(
            stacks[14].astype(jnp.bfloat16), "dp", scatter_dimension=2, tiled=True
        ).astype(jnp.float32),
    )
    group_done = (
        lax.psum(stacks[3].astype(jnp.bfloat16), "dp").astype(jnp.float32),
        lax.psum(stacks[4].astype(jnp.bfloat16), "dp").astype(jnp.float32),
        lax.psum(stacks[5].astype(jnp.bfloat16), "dp").astype(jnp.float32),
        lax.psum(stacks[11].astype(jnp.bfloat16), "dp").astype(jnp.float32),
        lax.psum(stacks[12].astype(jnp.bfloat16), "dp").astype(jnp.float32),
        lax.psum(stacks[13].astype(jnp.bfloat16), "dp").astype(jnp.float32),
    )
    return (
        current,
        grad_rows,
        shared_done[0],
        shared_done[1],
        weight_done[0],
        group_done[0],
        group_done[1],
        group_done[2],
        shared_done[2],
        shared_done[3],
        shared_done[4],
        shared_done[5],
        shared_done[6],
        group_done[3],
        group_done[4],
        group_done[5],
        weight_done[1],
        shared_done[7],
        shared_done[8],
        shared_done[9],
        stacks[18],
        stacks[19],
        stacks[20],
        shared_done[10],
    )


BF16 = jnp.bfloat16
F32 = jnp.float32
MESH = pl.DeviceIdType.MESH
SHARE = 4
GELU_C = math.sqrt(2.0 / math.pi)
GELU_A = 0.044715
VMEM_LIMIT = 63 * 1024 * 1024
ROW_DECAY, ROW_SKIP, ROW_ENDS, ROW_W3 = 15, 16, 17, 24


def dot_nn(a, b, precision=None):
    return lax.dot_general(
        a, b, (((1,), (0,)), ((), ())), precision=precision, preferred_element_type=F32
    )


def dot_nt(a, b, precision=None):
    return lax.dot_general(
        a, b, (((1,), (1,)), ((), ())), precision=precision, preferred_element_type=F32
    )


def dot_tn(a, b, precision=None):
    return lax.dot_general(
        a, b, (((0,), (0,)), ((), ())), precision=precision, preferred_element_type=F32
    )


class Sizes:
    def __init__(self, mesh_dp, mesh_tp, rows, width, chan, shard, slots, layers, emb, filt):
        self.ndp, self.n = mesh_dp, mesh_tp
        self.R, self.D, self.C = rows, width, chan
        self.T = rows * mesh_tp
        self.FFs = shard
        self.FR = 2 * shard + 16
        self.Y = mesh_dp // SHARE
        self.FB = mesh_tp * shard
        self.SL, self.L = slots, layers
        self.EMB, self.FILT = emb, filt
        self.EP = -(-emb // 8) * 8
        self.DB = width // mesh_dp
        self.DP = 4 * chan // mesh_dp
        self.PK = mesh_dp // 4
        self.TL = rows // 2
        self.FROWS = self.EP + filt + 8
        self.LF = layers * filt
        self.CROWS = ROW_W3 + filt

    def places(self):
        at_wo = self.L * self.FR
        at_rows = at_wo + self.L * self.DB
        at_side = at_rows + 8 * self.L
        at_out = at_side + -(-max(self.FROWS, self.CROWS) // 8) * 8
        return at_wo, at_rows, at_side, at_out

    def fits(self):
        return (
            self.n == SHARE
            and self.ndp == 2 * SHARE
            and self.FFs % 16 == 0
            and self.DP % 32 == 0
            and self.FB <= self.D
            and self.SL <= 8
            and self.TL == 64
            and self.LF + (2 * self.L - 1) * self.C <= self.D
            and 4 * self.C <= self.D
            and self.n == 4
            and vmem_bytes(scratch_shapes(self)[0]) < VMEM_LIMIT - 6 * 1024 * 1024
        )


INPUTS = (
    "x", "cot", "lens", "ln1g", "ln1b", "w_in", "b_in", "cw", "cb", "emb", "fw1", "fb1", "fw2",
    "fb2", "freq", "fw3", "decay", "skip", "w_out", "b_out", "ln2g", "ln2b", "w_up", "b_up",
    "w_down", "b_down", "dft", "dftt", "tdft", "tdftt",
)
OUTPUTS = ("pack",)


def scratch_shapes(z):
    R, D, C, T, n, L, Y = z.R, z.D, z.C, z.T, z.n, z.L, z.Y
    steps_dp = z.ndp.bit_length() - 1
    steps = steps_dp + n.bit_length() - 1
    per = 24 + 8 * (n - 1) + 8 * (z.ndp - 1) + 56 + n * Y + n * (Y - 1) + (n - 1) + 3 * (n - 1)
    sems = L * (per + 3 * steps + 2) + 8
    shapes = dict(
        xb=((R, D), BF16),
        xv=((R, D), BF16),
        cv=((R, D), BF16),
        ov=((R, D), BF16),
        gv=((R, D), BF16),
        xs=((max(L - 1, 1), R, D), F32),
        mids=((L, R, D), F32),
        gx=((R, D), F32),
        nF=((L, n, R, D), BF16),
        p=((L, 3, T + 8, C), F32),
        inn=((L, T, C), F32),
        innb=((T, C), BF16),
        g0s=((T, C), F32),
        fz=((2, T, z.LF), F32),
        fc=((2, T, z.LF), F32),
        fa=((2, T, z.LF), BF16),
        fw1p=((z.EP, z.LF), F32),
        fw2p=((z.LF, z.LF), F32),
        fw3p=((L, z.LF, C), BF16),
        frow=((8, z.LF), F32),
        taps=((L, T, C), BF16),
        hs=((L, 2, T, C), BF16),
        xf=((L, 2, T, C), BF16),
        yb=((2, T, C), BF16),
        qb=((2, T, C), BF16),
        longs=((L, T, C), F32),
        mx=((L, T, C), BF16),
        pin=((L, ROW_W3, C), F32),
        pv=((L, ROW_W3, C), F32),
        p3=((L, z.FILT, C), BF16),
        v3=((L, z.FILT, C), BF16),
        wz=((L, n, z.DP, D), BF16),
        wfull=((L, z.ndp, z.DP, D), BF16),
        n2S=((L, SHARE, R, D), BF16),
        rowb=((16, D), F32),
        ffw=((L, Y, n, z.FR, D), BF16),
        bup=((L, Y, 8, z.FB), F32),
        hp=((L, Y, SHARE, R, z.FB), BF16),
        spf=((2, SHARE, R // 2, D), F32),
        sp=((2, 3, R // 2, D), BF16),
        sr=((2, 3, R // 2, D), BF16),
        gdS=((L, SHARE, R, D), BF16),
        hb=((Y, SHARE, R, z.FB), BF16),
        gpb=((Y, SHARE, R, z.FB), BF16),
        ffry=((L, Y - 1, n, z.FR, D), BF16),
        ffrz=((L, n - 1, 2, z.FR, D), BF16),
        goF=((n, R, D), BF16),
        gg=((3, T + 8, C), F32),
        gpj=((3, T, C), BF16),
        gl=((T, C), F32),
        gtp=((T, C), F32),
        gtt=((z.TL, C), F32),
        hs64=((L, 2, z.TL, C), F32),
        xt=((L, 2, (z.SL - 1) * z.TL, C), BF16),
        tst=(((z.SL - 1) * z.TL, C), BF16),
        wg=((2, z.ndp, z.DB, 2 * C), BF16),
        wr=((L, 2, Y - 1, SHARE, z.DB, 2 * C), BF16),
        wr1=((L, 2, SHARE, z.DB, 2 * C), BF16),
        wr2=((L, 2, n - 1, z.DB, 2 * C), BF16),
        sa=((L, 8, D), F32),
        sf=((L, z.FROWS, z.LF), F32),
        sc=((L, z.CROWS, C), F32),
        sc0=((L, z.CROWS, C), F32),
        rA=((L, steps_dp, 8, D), F32),
        rF=((L, steps_dp, z.FROWS, z.LF), F32),
        rP=((z.ndp - 1, 8, D), F32),
        rZ=((n - 1, 8, D), F32),
        rAz=((steps - steps_dp, L, 8, D), F32),
        rFz=((steps - steps_dp, z.FROWS, z.LF), F32),
        rC=((L, steps_dp, z.CROWS, C), F32),
    )
    return shapes, sems, steps_dp, steps


def vmem_bytes(shapes):
    total = 0
    for dims, kind in shapes.values():
        size = 2 if kind == BF16 else 4
        sub = 32 // size
        lanes = -(-dims[-1] // 128) * 128
        rows = -(-dims[-2] // sub) * sub
        total += math.prod(dims[:-2]) * rows * lanes * size
    return total


def fused_kernel(z, names, *refs):
    R, D, C, T, n, L, Y, ndp = z.R, z.D, z.C, z.T, z.n, z.L, z.Y, z.ndp
    FFs, FB, FILT, EP, DB, TL, LF = z.FFs, z.FB, z.FILT, z.EP, z.DB, z.TL, z.LF
    s = types.SimpleNamespace(**dict(zip(names, refs)))
    dp = lax.axis_index("dp")
    ti = lax.axis_index("tensor")
    y = dp // SHARE
    a = dp % SHARE
    sib = (dp + 1 - 2 * (dp % 2), ti)
    xnb = (dp + 2 - 4 * ((dp // 2) % 2), ti)
    partner = (SHARE * y + ti, a)
    moved = a != ti
    member = [a, a + 1 - 2 * (a % 2), a + 2 - 4 * (a // 2)]
    member.append(member[1] + 2 - 4 * (member[1] // 2))
    HR = R // 2
    FR = z.FR
    used = [0]
    open_sends = []

    def make(src, dst, dev):
        idx = used[0]
        used[0] += 1
        return pltpu.make_async_remote_copy(
            src_ref=src, dst_ref=dst, send_sem=s.ssem.at[idx], recv_sem=s.rsem.at[idx],
            device_id=dev, device_id_type=MESH,
        )

    def push(src, dst, dev, valid=True):
        copy = make(src, dst, dev)
        if valid is True:
            copy.start()
        else:
            pl.when(valid)(copy.start)
        open_sends.append((copy, valid))
        return copy

    def sent(*copies):
        for item in [p for p in open_sends if any(p[0] is c for c in copies)]:
            if item[1] is True:
                item[0].wait_send()
            else:
                pl.when(item[1])(item[0].wait_send)
        open_sends[:] = [p for p in open_sends if not any(p[0] is c for c in copies)]

    def swap(src, dst):
        copy = make(src, dst, partner)
        pl.when(moved)(copy.start)

        @pl.when(a == ti)
        def _():
            dst[...] = src[...]

        open_sends.append((copy, moved))
        return copy

    def swapped(copy):
        pl.when(moved)(copy.wait_recv)

    def flush():
        sent(*[p[0] for p in open_sends])

    def done(copy):
        copy.wait_recv()

    def piece_of(yy, m):
        last = m // (SHARE - 1)
        return (1 - last) * ((SHARE - 1) * yy + m) + last * ((SHARE - 1) * Y + yy)

    def piece_copy(l, act):
        piece = piece_of(y, a)
        k = piece // z.PK
        rows = pl.ds(pl.multiple_of((piece % z.PK) * z.DP, z.DP), z.DP)
        dst = s.wz.at[l, ti]

        @pl.when(k < 3)
        def _():
            getattr(pltpu.make_async_copy(s.w_in.at[l, k, rows], dst, s.lsem.at[l]), act)()

        @pl.when(k >= 3)
        def _():
            getattr(pltpu.make_async_copy(s.w_out.at[l, rows], dst, s.lsem.at[l]), act)()

    for l in range(L):
        piece_copy(l, "start")

    barrier = pltpu.get_barrier_semaphore()
    for d in range(1, ndp):
        pl.semaphore_signal(barrier, inc=1, device_id=((dp + d) % ndp, ti), device_id_type=MESH)
    for d in range(1, n):
        pl.semaphore_signal(barrier, inc=1, device_id=(dp, (ti + d) % n), device_id_type=MESH)

    @pl.when(moved)
    def _():
        pl.semaphore_signal(barrier, inc=1, device_id=partner, device_id_type=MESH)

    s.xb[...] = s.x[...].astype(BF16)

    @pl.when(moved)
    def _():
        pl.semaphore_wait(barrier, ndp - 1 + n)

    @pl.when(a == ti)
    def _():
        pl.semaphore_wait(barrier, ndp - 1 + n - 1)

    def ln_parts(v):
        mu = jnp.mean(v, axis=-1, keepdims=True)
        c = v - mu
        r = lax.rsqrt(jnp.mean(c * c, axis=-1, keepdims=True) + NORM_EPS)
        return c * r, r

    def ln_back(v, gy, gain):
        xhat, r = ln_parts(v)
        gz = gy * gain
        gv = r * (
            gz - jnp.mean(gz, axis=-1, keepdims=True)
            - xhat * jnp.mean(gz * xhat, axis=-1, keepdims=True)
        )
        return gv, jnp.sum(gy * xhat, axis=0, keepdims=True), jnp.sum(gy, axis=0, keepdims=True)

    def chip_rows(i):
        return pl.ds(pl.multiple_of(i * 2 * R, 2 * R), 2 * R)

    def chip_block(ref, i):
        return ref[pl.ds(2 * i, 2)].reshape(2 * R, D)

    def layer_input(l, h):
        return s.xv[half(h), :].astype(F32) if l == 0 else s.xs[l - 1, half(h), :]

    def half(h):
        return pl.ds(h * HR, HR)

    def gather_s(buf, h):
        mine = buf.at[member[0], half(h)]
        to_x = push(mine, mine, xnb)
        to_sib = push(mine, mine, sib)
        yield
        done(to_x)
        other = buf.at[member[2], half(h)]
        onward = push(other, other, sib)
        done(to_sib)
        yield
        done(onward)
        sent(to_x, to_sib, onward)

    def scatter_s(h, block, hook=None):
        s.spf[h] = block().reshape(SHARE, HR, D)
        for chip in range(2):
            s.sp[h, chip] = s.spf[h, 2 * chip + 1 - a % 2].astype(BF16)
        c1 = push(s.sp.at[h, 0:2], s.sr.at[h, 0:2], sib)
        yield
        done(c1)
        far = s.spf[h, member[2]] + s.sr[h, 1 - a // 2].astype(F32)
        s.sp[h, 2] = far.astype(BF16)
        cx = push(s.sp.at[h, 2], s.sr.at[h, 2], xnb)
        if hook:
            hook()
        yield
        near = s.spf[h, a] + s.sr[h, a // 2].astype(F32)
        done(cx)
        sent(c1, cx)
        return near + s.sr[h, 2].astype(F32)

    def weave(*gens):
        gens = list(gens)
        while gens:
            for g in list(gens):
                try:
                    next(g)
                except StopIteration:
                    gens.remove(g)

    def y_peer(e):
        return (((y + e) % Y) * SHARE + a, ti)

    def w_gather(l):
        piece_copy(l, "wait")
        HP = z.DP // 2
        cuts = [pl.ds(h * HP, HP) for h in range(2)]
        order = (2, 1, 3)
        along_z, to_member, early, late = [], [], [], []

        def forward(m, cut, valid):
            piece = s.wfull.at[l, piece_of(y, m), cut]
            return [(push(piece, piece, y_peer(e), valid), valid) for e in range(1, Y)]

        for cut in cuts:
            own = s.wz.at[l, ti, cut]
            along_z.append([push(own, own, (dp, (ti + d) % n)) for d in range(1, n)])
        yield
        for h, cut in enumerate(cuts):
            for c in along_z[h]:
                done(c)
            to_member.append([])
            for d in order:
                m = (a + d) % SHARE
                to_member[h].append(
                    push(s.wz.at[l, m, cut], s.wfull.at[l, piece_of(y, a), cut], (y * SHARE + m, ti))
                )
            s.wfull[l, piece_of(y, a), cut] = s.wz[l, a, cut]
            early += forward(a, cut, a < SHARE - 1)
            yield
        others = [(a + SHARE - d) % SHARE for d in order]
        for h, cut in enumerate(cuts):
            for c, m in zip(to_member[h], others):
                done(c)
                early += forward(m, cut, m < SHARE - 1)
            if h == 1:
                for half_cut in cuts:
                    for m in [a] + others:
                        late += forward(m, half_cut, m == SHARE - 1)
            yield
        for c, valid in early:
            pl.when(valid)(c.wait_recv)
        yield
        for c, valid in late:
            pl.when(valid)(c.wait_recv)
        yield

    def w_mat(l, k):
        return s.wfull[l, z.PK * k : z.PK * (k + 1)].reshape(C, D)

    def ff_gather(l):
        s.ffw[l, y, ti, 0:FFs, :] = s.w_up[l]
        s.ffw[l, y, ti, FFs : 2 * FFs, :] = s.w_down[l]
        s.rowb[...] = jnp.zeros((16, D), F32)
        s.rowb[0:1, 0:FFs] = s.b_up[...].astype(F32)[l : l + 1, :]
        s.ffw[l, y, ti, 2 * FFs : 2 * FFs + 16, :] = s.rowb[...].astype(BF16)
        along_y = []
        hops = []
        hop = None
        for h in range(n):
            low = (ti + n - h) % n
            high = (ti + h) % n
            has_low = ti >= h
            has_high = ti + h < n
            if h:
                pl.when(has_low)(hop[0].wait_recv)
                pl.when(has_high)(hop[1].wait_recv)
            lo, hi = s.ffw.at[l, y, low], s.ffw.at[l, y, high]
            if h < n - 1:
                hop = (
                    push(lo, lo, (dp, (ti + 1) % n), jnp.logical_and(has_low, ti < n - 1)),
                    push(hi, hi, (dp, (ti + n - 1) % n), jnp.logical_and(has_high, ti > 0)),
                )
                hops += hop
            for e in range(1, Y):
                if h == 1:
                    own = s.ffw.at[l, y, ti]
                    along_y.append((push(own, own, y_peer(e)), True))
                if h:
                    along_y.append((push(lo, lo, y_peer(e), has_low), has_low))
                    along_y.append((push(hi, hi, y_peer(e), has_high), has_high))
            yield
        for c, valid in along_y:
            if valid is True:
                done(c)
            else:
                pl.when(valid)(c.wait_recv)
        sent(*hops, *[c for c, _ in along_y])
        ff_ready(l)
        yield

    def ff_ready(l):
        for b in range(Y):
            row = jnp.zeros((16, D), F32)
            for j in range(n):
                part = s.ffw[l, b, j, 2 * FFs : 2 * FFs + 16, :].astype(F32)
                row = row + (pltpu.roll(part, FFs * j, 1) if j else part)
            s.bup[l, b] = row[:8, :FB]

    def ff_up(l, b):
        return s.ffw[l, b, :, 0:FFs, :].reshape(FB, D)

    def ff_down(l, b):
        return s.ffw[l, b, :, FFs : 2 * FFs, :].reshape(FB, D)

    CH = 64
    ENDS = range(z.SL - 1)

    def end_row(k):
        return s.pv[0, ROW_ENDS + k : ROW_ENDS + k + 1, :]

    def chunk_masks(r0, rows):
        t = (lax.broadcasted_iota(jnp.int32, (rows, C), 0) + r0).astype(F32)
        m1 = jnp.ones((rows, C), F32)
        for k in ENDS:
            m1 = jnp.where(t == end_row(k), 0.0, m1)
        m2 = m1
        for k in ENDS:
            m2 = jnp.where(t == end_row(k) + 1.0, 0.0, m2)
        return m1, m2

    def conv_row(l, step, k):
        return s.pv[l, 3 + step * 3 + k : 4 + step * 3 + k, :]

    def shifted(l, k, r0, masks):
        blk = s.p[l, k, pl.ds(r0, CH + 8), :]
        if masks is None:
            return blk[8:], blk[7:-1], blk[6:-2]
        return blk[8:], blk[7:-1] * masks[0], blk[6:-2] * masks[1]

    LAST = T // CH - 1

    def each_chunk(step):
        @pl.loop(0, LAST)
        def _(i):
            step(pl.multiple_of(i * CH, CH), None)

        step(LAST * CH, chunk_masks(LAST * CH, CH))

    def gate(l, k, parts):
        return (
            s.pv[l, 12 + k : 13 + k, :]
            + conv_row(l, 0, k) * parts[0]
            + conv_row(l, 1, k) * parts[1]
            + conv_row(l, 2, k) * parts[2]
        )

    def lag_rows():
        return lax.broadcasted_iota(jnp.int32, (T, C), 0).astype(F32)

    def decay_row(l):
        return s.pv[l, ROW_DECAY : ROW_DECAY + 1, :]

    def skip_row(l):
        return s.pv[l, ROW_SKIP : ROW_SKIP + 1, :]

    def filter_net():
        s.fw1p[...] = jnp.zeros((EP, LF), F32)
        s.fw2p[...] = jnp.zeros((LF, LF), F32)
        for l in range(L):
            at = slice(l * FILT, (l + 1) * FILT)
            row = slice(l, l + 1)
            for r in range(z.EMB):
                s.fw1p[r : r + 1, at] = s.fw1[r, row, :]
            s.fw2p[at, at] = s.fw2[l]
            s.frow[0:1, at] = s.fb1[row, :]
            s.frow[1:2, at] = s.fb2[row, :]
            s.frow[2:4, at] = s.freq[l]
        z1 = dot_nn(s.emb[...], s.fw1p[...], PRECISE) + s.frow[0:1, :]
        u1 = s.frow[2:3, :] * z1
        a1 = jnp.sin(u1)
        s.fz[0] = z1
        s.fa[0] = a1.astype(BF16)
        s.fc[0] = jnp.cos(u1)
        z2 = dot_nn(a1, s.fw2p[...], PRECISE) + s.frow[1:2, :]
        u2 = s.frow[3:4, :] * z2
        s.fz[1] = z2
        s.fa[1] = jnp.sin(u2).astype(BF16)
        s.fc[1] = jnp.cos(u2)

    def filter_taps_of(l):
        s.fw3p[l] = jnp.zeros((LF, C), BF16)
        s.fw3p[l, l * FILT : (l + 1) * FILT, :] = s.v3[l]
        tp = dot_nn(s.fa[1], s.fw3p[l]) * jnp.exp(-lag_rows() * decay_row(l))
        s.innb[...] = tp.astype(BF16)
        s.taps[l] = s.innb[...]
        s.hs64[l, 0] = dot_nn(s.tdft[0, 0:TL, 0:TL], s.innb[0:TL, :])
        s.hs64[l, 1] = dot_nn(s.tdft[1, 0:TL, 0:TL], s.innb[0:TL, :])

        @pl.loop(0, n // 2)
        def _(i):
            rows = chip_rows(i)
            s.hs[l, 0, rows, :] = dot_nn(s.dft[0, rows, :], s.innb[...]).astype(BF16)
            s.hs[l, 1, rows, :] = dot_nn(s.dft[1, rows, :], s.innb[...]).astype(BF16)

    def tail_masks():
        t = lax.broadcasted_iota(jnp.int32, (TL, C), 0).astype(F32) + float(T - TL)
        masks = []
        for k in ENDS:
            live = t >= end_row(k)
            if k + 1 < z.SL - 1:
                live = jnp.logical_and(live, t < end_row(k + 1))
            masks.append(live.astype(F32))
        return masks, t < end_row(0)

    def tail_spectrum(rows, masks):
        for k, mask in enumerate(masks):
            s.tst[k * TL : (k + 1) * TL, :] = (rows * mask).astype(BF16)
        return dot_nn(s.tdft[0], s.tst[...]), dot_nn(s.tdft[1], s.tst[...])

    def tail_back(re, im):
        res = dot_nn(s.tdftt[0], re.astype(BF16)) + dot_nn(s.tdftt[1], im.astype(BF16))
        res = res * (1.0 / TL)
        return [res[k * TL : (k + 1) * TL] for k in ENDS]

    def tail_filter(l, part):
        one = s.hs64[l, part]
        return jnp.concatenate([one] * len(ENDS), axis=0)

    def project(l, h):
        rows = s.nF[l, :, half(h), :].reshape(SHARE * HR, D)
        for k in range(3):
            if h == 0:
                s.p[l, k, 0:8, :] = jnp.zeros((8, C), F32)
            res = dot_nt(rows, w_mat(l, k)) + s.pv[l, k : k + 1, :]
            for m in range(SHARE):
                lo = 8 + m * R + h * HR
                s.p[l, k, lo : lo + HR, :] = res[m * HR : (m + 1) * HR]

    def mixer_forward(l, tick):
        def step(r0, masks):
            g0 = gate(l, 0, shifted(l, 0, r0, masks))
            g1 = gate(l, 1, shifted(l, 1, r0, masks))
            g2 = gate(l, 2, shifted(l, 2, r0, masks))
            inner = g2 * g1
            s.g0s[pl.ds(r0, CH), :] = g0
            s.inn[l, pl.ds(r0, CH), :] = inner
            s.innb[pl.ds(r0, CH), :] = inner.astype(BF16)

        each_chunk(step)

        @pl.loop(0, n // 2)
        def _(i):
            rows = chip_rows(i)
            xr = dot_nn(s.dft[0, rows, :], s.innb[...])
            xi = dot_nn(s.dft[1, rows, :], s.innb[...])
            hr = s.hs[l, 0, rows, :].astype(F32)
            hi = s.hs[l, 1, rows, :].astype(F32)
            s.xf[l, 0, rows, :] = xr.astype(BF16)
            s.xf[l, 1, rows, :] = xi.astype(BF16)
            s.yb[0, rows, :] = (xr * hr - xi * hi).astype(BF16)
            s.yb[1, rows, :] = (xr * hi + xi * hr).astype(BF16)

        masks, first = tail_masks()
        xr, xi = tail_spectrum(s.inn[l, T - TL : T, :], masks)
        s.xt[l, 0] = xr.astype(BF16)
        s.xt[l, 1] = xi.astype(BF16)
        hr, hi = tail_filter(l, 0), tail_filter(l, 1)
        parts = tail_back(xr * hr - xi * hi, xr * hi + xi * hr)
        tail = parts[0] * masks[0]
        for part, mask in zip(parts[1:], masks[1:]):
            tail = tail + part * mask
        s.gtt[...] = tail

        @pl.loop(0, n // 2)
        def _(i):
            rows = chip_rows(i)
            s.longs[l, rows, :] = (
                dot_nn(s.dftt[0, rows, :], s.yb[0]) + dot_nn(s.dftt[1, rows, :], s.yb[1])
            ) * (1.0 / T)
        s.longs[l, T - TL : T, :] = jnp.where(first, s.longs[l, T - TL : T, :], s.gtt[...])

        @pl.loop(0, n // 2)
        def _(i):
            rows = chip_rows(i)
            lg = s.longs[l, rows, :] + skip_row(l) * s.inn[l, rows, :]
            s.longs[l, rows, :] = lg
            s.mx[l, rows, :] = (lg * s.g0s[rows, :]).astype(BF16)
        tick()

    def gelu_tanh(v):
        return jnp.tanh(GELU_C * (v + GELU_A * v * v * v))

    def ff_block(l, h):
        v = s.n2S[l, :, half(h), :].reshape(SHARE * HR, D)
        acc = jnp.zeros((SHARE * HR, D), F32)
        for b in range(Y):
            pre = dot_nt(v, ff_up(l, b)) + s.bup[l, b, 0:1, :]
            s.hp[l, b, :, half(h), :] = pre.astype(BF16).reshape(SHARE, HR, FB)
            act = 0.5 * pre * (1.0 + gelu_tanh(pre))
            acc = acc + dot_nn(act.astype(BF16), ff_down(l, b))
        return acc

    def ff_back_block(l, h):
        g = s.gdS[l, :, half(h), :].reshape(SHARE * HR, D)
        acc = jnp.zeros((SHARE * HR, D), F32)
        for b in range(Y):
            gh = dot_nt(g, ff_down(l, b))
            v = s.hp[l, b, :, half(h), :].reshape(SHARE * HR, FB).astype(F32)
            th = gelu_tanh(v)
            act = (0.5 * v * (1.0 + th)).astype(BF16)
            s.hb[b, :, half(h), :] = act.reshape(SHARE, HR, FB)
            slope = 0.5 * (1.0 + th) + 0.5 * v * (1.0 - th * th) * (
                GELU_C * (1.0 + 3.0 * GELU_A * v * v)
            )
            gp = (gh * slope).astype(BF16)
            s.gpb[b, :, half(h), :] = gp.reshape(SHARE, HR, FB)
            acc = acc + dot_nn(gp, ff_up(l, b))
        return acc

    def ff_scatter(l):
        act = s.n2S[l].reshape(SHARE * R, D)
        gds = s.gdS[l].reshape(SHARE * R, D)

        def fill(b):
            g = s.gpb[b].reshape(SHARE * R, FB)
            h = s.hb[b].reshape(SHARE * R, FB)
            s.ffw[l, b, :, 0:FFs, :] = dot_tn(g, act).astype(BF16).reshape(n, FFs, D)
            s.ffw[l, b, :, FFs : 2 * FFs, :] = dot_tn(h, gds).astype(BF16).reshape(n, FFs, D)
            sums = jnp.sum(g.astype(F32), axis=0, keepdims=True)
            row = jnp.concatenate([sums, jnp.zeros((1, D - FB), F32)], axis=1) if D > FB else sums
            row = jnp.broadcast_to(row, (16, D))
            for j in range(n):
                part = pltpu.roll(row, (D - FFs * j) % D, 1) if j else row
                s.ffw[l, b, j, 2 * FFs : 2 * FFs + 16, :] = part.astype(BF16)

        order = [3 * (1 - ti // 2), (2 + 3 * ti) % 5, 1 + ti % 2, ti]
        along_y = []
        for e in range(1, Y):
            b = (y + e) % Y
            fill(b)
            for j in order:
                along_y.append(push(s.ffw.at[l, b, j], s.ffry.at[l, e - 1, j], y_peer(e)))
        fill(y)
        yield
        hop = None
        hops = []
        for pos, j in enumerate(order):
            acc = s.ffw[l, y, j].astype(F32)
            for e in range(1, Y):
                done(along_y[(e - 1) * n + pos])
                acc = acc + s.ffry[l, e - 1, j].astype(F32)
            if pos < n - 1:
                s.ffry[l, 0, j] = acc.astype(BF16)
            else:
                s.pack[l * FR : (l + 1) * FR, :] = acc
                sent(*along_y)
            if pos < n - 1:
                d = n - 1 - pos
                new = []
                for side, (valid, inner, to) in enumerate(
                    ((ti + d < n, ti >= 1, ti + 1), (ti >= d, ti < n - 1, ti + n - 1))
                ):
                    j = (ti + d) % n if side == 0 else (ti + n - d) % n
                    if pos:
                        more = jnp.logical_and(valid, inner)
                        pl.when(more)(hop[side].wait_recv)

                        @pl.when(more)
                        def _():
                            s.ffry[l, 0, j] = (
                                s.ffry[l, 0, j].astype(F32) + s.ffrz[l, pos - 1, side].astype(F32)
                            ).astype(BF16)

                    new.append(
                        push(
                            s.ffry.at[l, 0, j], s.ffrz.at[l, pos, side], (dp, to % n), valid
                        )
                    )
                hop = new
                hops += new
            yield
        for side, inner in ((0, ti >= 1), (1, ti < n - 1)):
            pl.when(inner)(hop[side].wait_recv)

            @pl.when(inner)
            def _():
                s.pack[l * FR : (l + 1) * FR, :] = (
                    s.pack[l * FR : (l + 1) * FR, :] + s.ffrz[l, n - 2, side].astype(F32)
                )

        sent(*hops)
        yield

    def mixer_backward(l, ticks):
        def first_step(r0, masks):
            rows = pl.ds(r0, CH)
            g0 = gate(l, 0, shifted(l, 0, r0, masks))
            gm = s.gtp[rows, :]
            glong = gm * g0
            s.gg[0, rows, :] = gm * s.longs[l, rows, :]
            s.gl[rows, :] = glong
            if masks is not None:
                t = (lax.broadcasted_iota(jnp.int32, (CH, C), 0) + r0).astype(F32)
                glong = jnp.where(t < end_row(0), glong, 0.0)
            s.innb[rows, :] = glong.astype(BF16)

        each_chunk(first_step)

        @pl.loop(0, n // 2)
        def _(i):
            rows = chip_rows(i)
            gr = dot_nn(s.dft[0, rows, :], s.innb[...])
            gi = dot_nn(s.dft[1, rows, :], s.innb[...])
            hr = s.hs[l, 0, rows, :].astype(F32)
            hi = s.hs[l, 1, rows, :].astype(F32)
            s.yb[0, rows, :] = (gr * hr + gi * hi).astype(BF16)
            s.yb[1, rows, :] = (gi * hr - gr * hi).astype(BF16)
            xr = s.xf[l, 0, rows, :].astype(F32)
            xi = s.xf[l, 1, rows, :].astype(F32)
            s.qb[0, rows, :] = (gr * xr + gi * xi).astype(BF16)
            s.qb[1, rows, :] = (gi * xr - gr * xi).astype(BF16)

        ticks[0]()
        masks, first = tail_masks()
        gr, gi = tail_spectrum(s.gl[T - TL : T, :], masks)
        hr, hi = tail_filter(l, 0), tail_filter(l, 1)
        parts = tail_back(gr * hr + gi * hi, gi * hr - gr * hi)
        tail = parts[0] * masks[0]
        for part, mask in zip(parts[1:], masks[1:]):
            tail = tail + part * mask
        xr, xi = s.xt[l, 0].astype(F32), s.xt[l, 1].astype(F32)
        parts = tail_back(gr * xr + gi * xi, gi * xr - gr * xi)
        s.gtt[...] = sum(parts[1:], parts[0])

        @pl.loop(0, n // 2)
        def _(i):
            rows = chip_rows(i)
            s.g0s[rows, :] = (
                dot_nn(s.dftt[0, rows, :], s.yb[0]) + dot_nn(s.dftt[1, rows, :], s.yb[1])
            ) * (1.0 / T)
            s.gtp[rows, :] = (
                dot_nn(s.dftt[0, rows, :], s.qb[0]) + dot_nn(s.dftt[1, rows, :], s.qb[1])
            ) * (1.0 / T)

        s.g0s[T - TL : T, :] = jnp.where(first, s.g0s[T - TL : T, :], tail)
        s.gtp[0:TL, :] = s.gtp[0:TL, :] + s.gtt[...]

        ticks[1]()

        def fold(v):
            return jnp.sum(v.reshape(CH // 8, 8, C), axis=0)

        for k in range(3):
            s.gg[k, T : T + 8, :] = jnp.zeros((8, C), F32)

        def gate_step(r0, masks, sums):
            rows = pl.ds(r0, CH)
            parts = [shifted(l, k, r0, masks) for k in range(3)]
            gl = s.gl[rows, :]
            ginner = s.g0s[rows, :] + skip_row(l) * gl
            gk = [s.gg[0, rows, :], ginner * gate(l, 2, parts[2]), ginner * gate(l, 1, parts[1])]
            s.gg[1, rows, :] = gk[1]
            s.gg[2, rows, :] = gk[2]
            new = []
            for step in range(3):
                for k in range(3):
                    new.append(sums[step * 3 + k] + fold(gk[k] * parts[k][step]))
            for k in range(3):
                new.append(sums[9 + k] + fold(gk[k]))
            new.append(sums[12] + fold(gl * s.inn[l, rows, :]))
            return tuple(new)

        sums = lax.fori_loop(
            0,
            LAST,
            lambda i, sums: gate_step(pl.multiple_of(i * CH, CH), None, sums),
            tuple(jnp.zeros((8, C), F32) for _ in range(13)),
        )
        sums = gate_step(LAST * CH, chunk_masks(LAST * CH, CH), sums)
        for pos in range(12):
            s.sc0[l, 3 + pos : 4 + pos, :] = jnp.sum(sums[pos], axis=0, keepdims=True)
        s.sc0[l, ROW_SKIP : ROW_SKIP + 1, :] = jnp.sum(sums[12], axis=0, keepdims=True)

        ticks[2]()

        def proj_step(r0, masks, sums):
            new = []
            for k in range(3):
                blk = s.gg[k, pl.ds(r0, CH + 8), :]
                b1 = blk if masks is None else blk * masks[0]
                b2 = blk if masks is None else blk * masks[1]
                gp = (
                    conv_row(l, 0, k) * blk[0:CH]
                    + conv_row(l, 1, k) * b1[1 : CH + 1]
                    + conv_row(l, 2, k) * b2[2 : CH + 2]
                ).astype(BF16)
                s.gpj[k, pl.ds(r0, CH), :] = gp
                new.append(sums[k] + fold(gp.astype(F32)))
            return tuple(new)

        sums = lax.fori_loop(
            0,
            LAST - 1,
            lambda i, sums: proj_step(pl.multiple_of(i * CH, CH), None, sums),
            tuple(jnp.zeros((8, C), F32) for _ in range(3)),
        )
        for i in (LAST - 1, LAST):
            sums = proj_step(i * CH, chunk_masks(i * CH, CH + 8), sums)
        for k in range(3):
            s.sc0[l, k : k + 1, :] = jnp.sum(sums[k], axis=0, keepdims=True)

    def filter_backward(l):
        lag = lag_rows()
        gt = s.gtp[...]
        s.sc0[l, ROW_DECAY : ROW_DECAY + 1, :] = -jnp.sum(
            lag * gt * s.taps[l].astype(F32), axis=0, keepdims=True
        )
        gtr = (gt * jnp.exp(-lag * decay_row(l))).astype(BF16)
        gw3 = dot_tn(s.fa[1], gtr)
        s.sc0[l, ROW_W3 : ROW_W3 + FILT, :] = gw3[l * FILT : (l + 1) * FILT]
        gu2 = dot_nt(gtr, s.fw3p[l]) * s.fc[1]
        gz2 = gu2 * s.frow[3:4, :]
        gz2b = gz2.astype(BF16)
        s.sf[l, EP : EP + FILT, :] = dot_tn(s.fa[0], gz2b)[l * FILT : (l + 1) * FILT]
        gu1 = dot_nt(gz2b, s.fw2p[...].astype(BF16)) * s.fc[0]
        gz1 = gu1 * s.frow[2:3, :]
        s.sf[l, 0:EP, :] = dot_tn(s.emb[...].astype(BF16), gz1.astype(BF16))
        row = EP + FILT
        s.sf[l, row : row + 1, :] = jnp.sum(gz1, axis=0, keepdims=True)
        s.sf[l, row + 1 : row + 2, :] = jnp.sum(gz2, axis=0, keepdims=True)
        s.sf[l, row + 2 : row + 3, :] = jnp.sum(gu1 * s.fz[0], axis=0, keepdims=True)
        s.sf[l, row + 3 : row + 4, :] = jnp.sum(gu2 * s.fz[1], axis=0, keepdims=True)

    def w_scatter(l):
        rows_all = s.nF[l].reshape(T, D)
        go_all = s.goF[...].reshape(T, D)
        order = (2, 3, 1, 0)
        along_y, to_member, along_z = [], [], []

        def fill(k):
            at = slice((k % 2) * C, (k % 2 + 1) * C)
            for h in range(0, D, 256):
                if k < 3:
                    g = dot_tn(rows_all[:, h : h + 256], s.gpj[k])
                else:
                    g = dot_tn(go_all[:, h : h + 256], s.mx[l])
                gb = g.astype(BF16)
                lo = h
                while lo < h + 256:
                    b = lo // DB
                    off = lo % DB
                    cnt = min(DB - off, h + 256 - lo)
                    s.wg[k // 2, b, off : off + cnt, at] = gb[lo - h : lo - h + cnt]
                    lo += cnt

        for half in range(2):
            fill(2 * half)
            fill(2 * half + 1)
            along_y.append([])
            for e in range(1, Y):
                for d in order:
                    m = (a + d) % SHARE
                    j = ((y + e) % Y) * SHARE + m
                    along_y[half].append(
                        push(s.wg.at[half, j], s.wr.at[l, half, e - 1, m], y_peer(e))
                    )
        yield

        def members(half):
            to_member.append([])
            for pos, d in enumerate(order):
                m = (a + d) % SHARE
                acc = s.wg[half, y * SHARE + m].astype(F32)
                for e in range(1, Y):
                    done(along_y[half][(e - 1) * SHARE + pos])
                    acc = acc + s.wr[l, half, e - 1, m].astype(F32)
                if d:
                    s.wr[l, half, 0, m] = acc.astype(BF16)
                    to_member[half].append(
                        push(s.wr.at[l, half, 0, m], s.wr1.at[l, half, a], (y * SHARE + m, ti))
                    )
                else:
                    s.wr1[l, half, a] = acc.astype(BF16)

        def levels(half):
            for c in to_member[half]:
                done(c)
            along_z.append([])
            for d in range(1, n):
                j = (ti + d) % n
                along_z[half].append(
                    push(s.wr1.at[l, half, j], s.wr2.at[l, half, d - 1], (dp, j))
                )

        members(0)
        yield
        members(1)
        sent(*along_y[0], *along_y[1])
        levels(0)
        yield
        levels(1)
        yield
        for half in range(2):
            acc = s.wr1[l, half, ti].astype(F32)
            for d in range(1, n):
                done(along_z[half][d - 1])
                acc = acc + s.wr2[l, half, d - 1].astype(F32)
            lo = at_wo + l * DB
            s.pack[lo : lo + DB, half * 2 * C : (half + 1) * 2 * C] = acc
            sent(*to_member[half], *along_z[half])
        yield

    def small_plane(l, names):
        pick = dict(a=(s.sa, s.rA), f=(s.sf, s.rF), c=(s.sc, s.rC))
        pairs = [pick[x] for x in names]
        for step in range(ndp.bit_length() - 1):
            bit = 1 << step
            peer = (dp + bit - 2 * bit * ((dp // bit) % 2), ti)
            copies = [push(v.at[l], r.at[l, step], peer) for v, r in pairs]
            yield
            for c in copies:
                done(c)
            sent(*copies)
            for v, r in pairs:
                v[l] = v[l] + r[l, step]
        yield

    def rows_last():
        copies = [
            push(s.sa.at[0], s.rP.at[d - 1], ((dp + d) % ndp, ti)) for d in range(1, ndp)
        ]
        yield
        acc = s.sa[0]
        for d in range(1, ndp):
            done(copies[d - 1])
            acc = acc + s.rP[d - 1]
        sent(*copies)
        s.sa[0] = acc
        copies = [push(s.sa.at[0], s.rZ.at[d - 1], (dp, (ti + d) % n)) for d in range(1, n)]
        yield
        for d in range(1, n):
            done(copies[d - 1])
            acc = acc + s.rZ[d - 1]
        sent(*copies)
        s.sa[0] = acc
        yield

    def small_levels():
        total = s.sf[0]
        for l in range(1, L):
            total = total + s.sf[l]
        s.sf[0] = total
        for step in range(n.bit_length() - 1):
            bit = 1 << step
            peer = (dp, ti + bit - 2 * bit * ((ti // bit) % 2))
            copies = [push(s.sf.at[0], s.rFz.at[step], peer)]
            for l in range(1, L):
                copies.append(push(s.sa.at[l], s.rAz.at[step, l], peer))
            yield
            for c in copies:
                done(c)
            sent(*copies)
            for l in range(1, L):
                s.sa[l] = s.sa[l] + s.rAz[step, l]
            s.sf[0] = s.sf[0] + s.rFz[step]
        yield

    at_wo, at_rows, at_side, at_out = z.places()
    wgen = {0: w_gather(0)}
    next(wgen[0])
    for l in range(L):
        s.pin[l] = jnp.zeros((ROW_W3, C), F32)
        for k in range(3):
            s.pin[l, k : k + 1, :] = s.b_in[k, l : l + 1, :]
            s.pin[l, 12 + k : 13 + k, :] = s.cb[k, l : l + 1, :]
        for k in range(9):
            s.pin[l, 3 + k : 4 + k, :] = s.cw[k, l : l + 1, :]
        s.pin[l, ROW_DECAY : ROW_DECAY + 1, :] = s.decay[l : l + 1, :]
        s.pin[l, ROW_SKIP : ROW_SKIP + 1, :] = s.skip[l : l + 1, :]
        s.p3[l] = s.fw3[l].astype(BF16)
    total = s.lens[0, 0]
    for k in ENDS:
        if k:
            total = total + s.lens[0, k]
        s.pin[0, ROW_ENDS + k : ROW_ENDS + k + 1, :] = jnp.full((1, C), total, jnp.int32).astype(F32)
    pc = swap(s.pin, s.pv)
    xc = [swap(s.xb.at[half(h)], s.xv.at[half(h)]) for h in range(2)]
    p3c = {0: swap(s.p3.at[0], s.v3.at[0])}
    filter_net()
    fgen = {l: ff_gather(l) for l in range(L)}
    wgen[1] = w_gather(1)

    def run(*gens):
        def go():
            for g in gens:
                next(g)

        return go

    def seq(*acts):
        def go():
            for act in acts:
                act()

        return go

    def norm_one(l, h, x):
        xhat, _ = ln_parts(x)
        s.nF[l, a, half(h), :] = (xhat * s.ln1g[l : l + 1, :] + s.ln1b[l : l + 1, :]).astype(BF16)

    def first_rows(h):
        swapped(xc[h])
        norm_one(0, h, layer_input(0, h))
        yield from gather_s(s.nF.at[0], h)

    rows = [first_rows(0), first_rows(1)]
    run(wgen[0], wgen[0])()
    run(rows[0], rows[1], wgen[0], rows[0], rows[1], wgen[0], fgen[0])()
    p3c[1] = swap(s.p3.at[1], s.v3.at[1])
    weave(*rows)
    swapped(pc)
    swapped(p3c[0])
    filter_taps_of(0)
    run(wgen[0])()
    project(0, 0)
    project(0, 1)
    run(fgen[0])()

    def taps_one():
        swapped(p3c[1])
        filter_taps_of(1)

    def forward_rows(l, h, hooks):
        def call(pos):
            if (h, pos) in hooks:
                hooks[(h, pos)]()

        mixed = lambda: s.mx[l].reshape(SHARE, R, C)[:, h * HR : (h + 1) * HR].reshape(
            SHARE * HR, C
        )
        res = yield from scatter_s(h, lambda: dot_nn(mixed(), w_mat(l, 3)), lambda: call(0))
        mid = layer_input(l, h) + s.b_out[l : l + 1, :] + res
        s.mids[l, half(h), :] = mid
        xhat, _ = ln_parts(mid)
        s.n2S[l, a, half(h), :] = (xhat * s.ln2g[l : l + 1, :] + s.ln2b[l : l + 1, :]).astype(BF16)
        yield from gather_s(s.n2S.at[l], h)
        call(1)
        res = yield from scatter_s(h, lambda: ff_block(l, h), lambda: call(2))
        cur = s.mids[l, half(h), :] + s.b_down[l : l + 1, :] + res
        if l + 1 < L:
            s.xs[l, half(h), :] = cur
            norm_one(l + 1, h, cur)
            yield from gather_s(s.nF.at[l + 1], h)
            call(3)
            project(l + 1, h)
        else:
            s.ov[half(h), :] = cur.astype(BF16)

    mixer_forward(0, run(fgen[0]))
    run(wgen[0])()
    hooks = {
        (1, 0): seq(run(fgen[0], wgen[1]), taps_one),
        (0, 1): run(fgen[0]),
        (1, 1): run(fgen[1], wgen[1], wgen[1]),
        (1, 2): run(wgen[1], wgen[1], fgen[1]),
        (0, 3): run(wgen[1]),
    }
    weave(forward_rows(0, 0, hooks), forward_rows(0, 1, hooks))
    sent(*xc)
    s.xb[...] = s.cot[...].astype(BF16)
    mixer_forward(1, run(fgen[1]))
    run(wgen[1])()
    cots = []
    hooks = {
        (1, 0): seq(run(fgen[1]), lambda: cots.append(swap(s.xb, s.cv))),
        (0, 1): run(fgen[1]),
    }
    weave(forward_rows(1, 0, hooks), forward_rows(1, 1, hooks))
    swapped(cots[0])
    outs = swap(s.ov, s.gv)
    s.gx[...] = s.cv[...].astype(F32)

    def add_row(l, pos, row):
        s.sa[l, pos : pos + 1, :] = s.sa[l, pos : pos + 1, :] + row

    def back_block(l, h):
        def rows(k):
            return s.gpj[k].reshape(SHARE, R, C)[:, h * HR : (h + 1) * HR].reshape(SHARE * HR, C)

        acc = dot_nn(rows(0), w_mat(l, 0))
        acc = acc + dot_nn(rows(1), w_mat(l, 1))
        return acc + dot_nn(rows(2), w_mat(l, 2))

    def backward_rows(l, h, hooks):
        def call(pos):
            if (h, pos) in hooks:
                hooks[(h, pos)]()

        if l + 1 < L:
            yield from last_rows(l + 1, h, hooks)
        if l < 0:
            return
        gd = s.gx[half(h), :].astype(BF16)
        s.gdS[l, a, half(h), :] = gd
        add_row(l, 5, jnp.sum(gd.astype(F32), axis=0, keepdims=True))
        yield from gather_s(s.gdS.at[l], h)
        call(1)
        gn = yield from scatter_s(h, lambda: ff_back_block(l, h), lambda: call(2))
        gv, gain_row, bias_row = ln_back(s.mids[l, half(h), :], gn, s.ln2g[l : l + 1, :])
        add_row(l, 2, gain_row)
        add_row(l, 3, bias_row)
        gm = s.gx[half(h), :] + gv
        s.gx[half(h), :] = gm
        go = gm.astype(BF16)
        add_row(l, 4, jnp.sum(go.astype(F32), axis=0, keepdims=True))
        s.goF[a, half(h), :] = go
        yield from gather_s(s.goF, h)
        call(3)
        rows = s.goF[:, half(h), :].reshape(SHARE * HR, D)
        res = dot_nt(rows, w_mat(l, 3))
        for m in range(SHARE):
            lo = m * R + h * HR
            s.gtp[lo : lo + HR, :] = res[m * HR : (m + 1) * HR]

    def last_rows(l, h, hooks):
        def hook():
            if (h, 0) in hooks:
                hooks[(h, 0)]()

        gn = yield from scatter_s(h, lambda: back_block(l, h), hook)
        gv, gain_row, bias_row = ln_back(layer_input(l, h), gn, s.ln1g[l : l + 1, :])
        add_row(l, 0, gain_row)
        add_row(l, 1, bias_row)
        grad = s.gx[half(h), :] + gv
        s.gx[half(h), :] = grad
        if l == 0:
            s.ov[half(h), :] = grad.astype(BF16)
            gins.append(swap(s.ov.at[half(h)], s.cv.at[half(h)]))

    gins = []
    for l in range(L):
        s.sa[l] = jnp.zeros((8, D), F32)
        s.sf[l] = jnp.zeros((z.FROWS, LF), F32)
        s.sc0[l] = jnp.zeros((z.CROWS, C), F32)

    ffs = [ff_scatter(l) for l in range(L)]
    wsc = [w_scatter(l) for l in range(L)]
    small1 = small_plane(1, "afc")
    side0 = small_plane(0, "f")
    corner0 = small_plane(0, "c")
    rows0 = rows_last()
    levels = small_levels()
    none = lambda: None

    def filters(l):
        def go():
            filter_backward(l)

        return go

    hooks = {(1, 2): run(ffs[1])}
    weave(backward_rows(1, 0, hooks), backward_rows(1, 1, hooks))
    mixer_backward(1, [none, run(ffs[1]), none])
    corner = {}

    def corner_swap(l):
        def go():
            corner[l] = swap(s.sc0.at[l], s.sc.at[l])

        return go

    hooks = {
        (1, 0): seq(run(wsc[1], ffs[1]), filters(1), corner_swap(1)),
        (1, 1): run(ffs[1]),
        (1, 2): run(ffs[0], wsc[1]),
        (0, 3): run(ffs[1], wsc[1]),
        (1, 3): seq(lambda: swapped(corner[1]), run(small1, ffs[0])),
    }
    weave(backward_rows(0, 0, hooks), backward_rows(0, 1, hooks))
    mixer_backward(
        0,
        [
            run(small1, wsc[1]),
            seq(run(small1, ffs[1], ffs[0]), filters(0), run(side0)),
            run(side0),
        ],
    )
    corner_swap(0)()
    run(side0, wsc[0])()
    hooks = {
        (0, 0): run(ffs[0]),
        (1, 0): seq(run(small1, side0, levels), lambda: swapped(corner[0]), run(corner0)),
    }
    sent(outs)
    weave(last_rows(0, 0, hooks), last_rows(0, 1, hooks))
    run(rows0)()
    run(corner0, levels, wsc[0], corner0, rows0, wsc[0], ffs[0], levels, corner0, wsc[0])()
    swapped(outs)
    s.pack[at_out : at_out + R, :] = s.gv[...].astype(F32)
    run(wsc[1], ffs[0], rows0)()
    for c in gins:
        swapped(c)
    s.pack[at_out + R : at_out + 2 * R, :] = s.cv[...].astype(F32)
    run(wsc[0])()
    for l in range(L):
        s.pack[at_rows + 8 * l : at_rows + 8 * (l + 1), :] = s.sa[l]
        lo = LF + 2 * C * l
        s.pack[at_side : at_side + z.CROWS, lo : lo + C] = s.sc[l]
    s.pack[at_side : at_side + z.FROWS, 0:LF] = s.sf[0]
    flush()


class View:
    def __init__(self, ref, row, rows, lane, lanes):
        self.ref, self.row, self.rows, self.lane, self.lanes = ref, row, rows, lane, lanes

    def __getitem__(self, at):
        rows, lanes = at
        top, bottom, _ = rows.indices(self.rows)
        left, right, _ = lanes.indices(self.lanes)
        return self.ref[
            self.row + top : self.row + bottom, self.lane + left : self.lane + right
        ]


def finish_kernel(z, *refs):
    o = types.SimpleNamespace(**dict(zip(FINAL, refs[1 : 1 + len(FINAL)])))
    held = refs[0]
    at_wo, at_rows, at_side, at_out = z.places()
    C, R = z.C, z.R
    o.out[...] = held[at_out : at_out + R, :]
    o.gin[...] = held[at_out + R : at_out + 2 * R, :]
    for l in range(z.L):
        at = z.EP + z.FILT
        lo = z.LF + 2 * C * l
        sa = View(held, at_rows + 8 * l, 8, 0, z.D)
        sc = View(held, at_side, z.CROWS, lo, C)
        sf = View(held, at_side, z.FROWS, l * z.FILT, z.FILT)
        wo = View(held, at_wo + l * z.DB, z.DB, 0, 4 * C)
        ffo = View(held, l * z.FR, z.FR, 0, z.D)
        row = slice(l, l + 1)
        for pos, ref in enumerate((o.ln1g, o.ln1b, o.ln2g, o.ln2b, o.b_out, o.b_down)):
            ref[row, :] = sa[pos : pos + 1, :]
        for k in range(3):
            o.w_in[l, k] = wo[:, k * C : (k + 1) * C]
            o.b_in[k, row, :] = sc[k : k + 1, :]
            o.cb[k, row, :] = sc[12 + k : 13 + k, :]
        for k in range(9):
            o.cw[k, row, :] = sc[3 + k : 4 + k, :]
        o.w_out[l] = wo[:, 3 * C : 4 * C].T
        for r in range(z.EMB):
            o.fw1[r, row, :] = sf[r : r + 1, :]
        o.fw2[l] = sf[z.EP : at, :]
        o.fb1[row, :] = sf[at : at + 1, :]
        o.fb2[row, :] = sf[at + 1 : at + 2, :]
        o.freq[l] = sf[at + 2 : at + 4, :]
        o.fw3[l] = sc[ROW_W3 : z.CROWS, :]
        o.decay[row, :] = sc[ROW_DECAY : ROW_DECAY + 1, :]
        o.skip[row, :] = sc[ROW_SKIP : ROW_SKIP + 1, :]
        o.w_up[l] = ffo[0 : z.FFs, :]
        o.w_down[l] = ffo[z.FFs : 2 * z.FFs, :]
        o.b_up[row, :] = ffo[2 * z.FFs : 2 * z.FFs + 1, 0 : z.FFs]


FINAL = (
    "out", "gin", "ln1g", "ln1b", "w_in", "b_in", "cw", "cb", "fw1", "fb1", "fw2", "fb2", "freq", "fw3",
    "decay", "skip", "w_out", "b_out", "ln2g", "ln2b", "w_up", "b_up", "w_down", "b_down",
)


def fused_local(z, *args):
    (inputs, cotangent, lengths, ln1_gain, ln1_bias, w_in, b_in, conv_weight, conv_bias, filt_w1,
     filt_b1, filt_w2, filt_b2, filt_freq, filt_w3, decay_rate, skip_gain, w_out, b_out, ln2_gain,
     ln2_bias, w_up, b_up, w_down, b_down) = args
    L, D, C, T, FFs, FILT = z.L, z.D, z.C, z.T, z.FFs, z.FILT
    lag = np.arange(T) / T
    bands = np.arange(1, z.EMB // 2 + 1)
    phases = 2.0 * math.pi * lag[:, None] * bands[None, :]
    emb = np.concatenate([lag[:, None], np.cos(phases), np.sin(phases)], axis=1)
    emb = np.pad(emb, ((0, 0), (0, z.EP - z.EMB))).astype(np.float32)
    def tables(length, copies):
        turn = (np.arange(length) * 2 + 1)[:, None] * np.arange(length)[None, :] % (4 * length)
        turn = turn * (math.pi / (2 * length))
        pair = [np.kron(np.eye(copies), f(turn)) for f in (np.cos, np.sin)]
        there = np.stack(pair).astype(jnp.bfloat16)
        back = np.stack([m.T for m in pair]).astype(jnp.bfloat16)
        return jnp.asarray(there), jnp.asarray(back)

    values = (
        inputs, cotangent, lengths, ln1_gain, ln1_bias, jnp.transpose(w_in, (0, 2, 3, 1)),
        jnp.swapaxes(b_in, 0, 1), jnp.transpose(conv_weight, (1, 2, 0, 3)).reshape(9, L, C),
        jnp.swapaxes(conv_bias, 0, 1), jnp.asarray(emb), jnp.swapaxes(filt_w1, 0, 1), filt_b1, filt_w2, filt_b2,
        filt_freq, filt_w3, decay_rate, skip_gain, w_out, b_out, ln2_gain, ln2_bias,
        jnp.swapaxes(w_up, 1, 2), b_up, w_down, b_down, *tables(T, 1), *tables(z.TL, z.SL - 1),
    )
    shapes, sems, _, _ = scratch_shapes(z)
    names = INPUTS + OUTPUTS + tuple(shapes) + ("ssem", "rsem", "lsem")
    f32 = lambda *dims: jax.ShapeDtypeStruct(dims, F32)
    outs = (f32(z.places()[3] + 2 * z.R, D),)
    vmem = pl.BlockSpec(memory_space=pltpu.VMEM)
    place = {"lens": pltpu.SMEM, "w_in": pl.ANY, "w_out": pl.ANY}
    specs = [pl.BlockSpec(memory_space=place.get(name, pltpu.VMEM)) for name in INPUTS]
    (packed,) = pl.pallas_call(
        functools.partial(fused_kernel, z, names),
        out_shape=outs,
        in_specs=specs,
        out_specs=[vmem] * len(outs),
        scratch_shapes=[pltpu.VMEM(*spec) for spec in shapes.values()]
        + [
            pltpu.SemaphoreType.DMA((sems,)),
            pltpu.SemaphoreType.DMA((sems,)),
            pltpu.SemaphoreType.DMA((L,)),
        ],
        compiler_params=pltpu.CompilerParams(
            collective_id=0, has_side_effects=True, vmem_limit_bytes=VMEM_LIMIT
        ),
        name="hyena_layers",
    )(*values)
    final = dict(
        out=f32(z.R, D), gin=f32(z.R, D),
        ln1g=f32(L, D), ln1b=f32(L, D), w_in=f32(L, 3, z.DB, C), b_in=f32(3, L, C),
        cw=f32(9, L, C), cb=f32(3, L, C), fw1=f32(z.EMB, L, FILT), fb1=f32(L, FILT),
        fw2=f32(L, FILT, FILT), fb2=f32(L, FILT), freq=f32(L, 2, FILT), fw3=f32(L, FILT, C),
        decay=f32(L, C), skip=f32(L, C), w_out=f32(L, C, z.DB), b_out=f32(L, D),
        ln2g=f32(L, D), ln2b=f32(L, D), w_up=f32(L, FFs, D), b_up=f32(L, FFs),
        w_down=f32(L, FFs, D), b_down=f32(L, D),
    )
    res = pl.pallas_call(
        functools.partial(finish_kernel, z),
        out_shape=tuple(final[name] for name in FINAL),
        in_specs=[vmem],
        out_specs=[vmem] * len(FINAL),
        compiler_params=pltpu.CompilerParams(vmem_limit_bytes=40 * 1024 * 1024),
        name="hyena_unpack",
    )(packed)
    g = types.SimpleNamespace(**dict(zip(FINAL, res)))
    return (
        g.out, g.gin, g.ln1g, g.ln1b, jnp.swapaxes(g.w_in, 1, 2), jnp.swapaxes(g.b_in, 0, 1),
        jnp.transpose(g.cw.reshape(3, 3, L, C), (2, 0, 1, 3)), jnp.swapaxes(g.cb, 0, 1),
        jnp.swapaxes(g.fw1, 0, 1), g.fb1, g.fw2, g.fb2, g.freq, g.fw3, g.decay, g.skip, g.w_out,
        g.b_out, g.ln2g, g.ln2b, jnp.swapaxes(g.w_up, 1, 2), g.b_up, g.w_down, g.b_down,
    )


def local_any(mesh, *args):
    z = Sizes(
        mesh.shape["dp"], mesh.shape["tensor"], args[0].shape[0], args[0].shape[1],
        args[5].shape[3], args[21].shape[2], args[2].shape[1], args[5].shape[0],
        args[9].shape[1], args[9].shape[2],
    )
    return fused_local(z, *args) if z.fits() else local(*args)


def solution(mesh):
    in_specs = (
        P(("dp", "tensor"), None),
        P(("dp", "tensor"), None),
        P("dp", None),
        P(),
        P(),
        P(None, None, None, "tensor"),
        P(None, None, "tensor"),
        P(None, None, None, "tensor"),
        P(None, None, "tensor"),
        P(),
        P(),
        P(),
        P(),
        P(),
        P(None, None, "tensor"),
        P(None, "tensor"),
        P(None, "tensor"),
        P(None, "tensor", None),
        P(),
        P(),
        P(),
        P(None, None, ("dp", "tensor")),
        P(None, ("dp", "tensor")),
        P(None, ("dp", "tensor"), None),
        P(),
    )
    out_specs = (
        P(("dp", "tensor"), None),
        P(("dp", "tensor"), None),
        P(),
        P(),
        P(None, "dp", None, "tensor"),
        P(None, None, "tensor"),
        P(None, None, None, "tensor"),
        P(None, None, "tensor"),
        P(),
        P(),
        P(),
        P(),
        P(),
        P(None, None, "tensor"),
        P(None, "tensor"),
        P(None, "tensor"),
        P(None, "tensor", "dp"),
        P(),
        P(),
        P(),
        P(None, None, ("dp", "tensor")),
        P(None, ("dp", "tensor")),
        P(None, ("dp", "tensor"), None),
        P(),
    )
    return jax.shard_map(functools.partial(local_any, mesh), mesh=mesh, in_specs=in_specs, out_specs=out_specs, check_vma=False)
```
